128 devices in a mesh: role: 2 (over core), dp: 64 (over y, x, z).
Axes of the slice: x: 4, y: 4, z: 4, core: 2. Of those that a mesh axis runs over, the one named last changes fastest.
Arguments:
- board_now: bfloat16 [4096, 10, 10, 128], P('dp'), may hold values from -6 to 6
- traj_boards: bfloat16 [64, 16, 10, 10, 128], P('dp'), may hold values from -6 to 6
- actions: int32 [64, 16], P('dp'), may hold values from 0 to 399
- lengths: int32 [64], P('dp'), may hold values from 1 to 16, 640 in all
- behaviour: float32 [64, 16], P('dp'), may hold values from -7 to -4.5
- regular: float32 [64, 16], P('dp'), may hold values from -7 to -4.5
- rewards: float32 [64, 16], P('dp'), may hold values from -4 to 4
- torso: float32 [2304, 128], replicated, may hold values from -0.1875 to 0.1875
- policy_head: bfloat16 [128, 4], replicated, may hold values from -0.5 to 0.5
- value_head: bfloat16 [128], replicated, may hold values from -2.390625 to 2.390625
- first_moment: float32 [2304, 128], P('dp'), may hold values from -6 to 6
- second_moment: float32 [2304, 128], P('dp'), may hold values from 0.5 to 2
Outputs:
- new_weights: float32 [2304, 128], P('dp')
- move_logp: float32 [4096, 400], P('dp')
The draws below stay inside these ranges and needn't reach their ends.
Inputs may be any that keep to these rules, and one draw needn't show every extreme that they name: `lengths`: live moves of a trajectory are its first slots; some trajectory has all 16.
All inputs are finite; a program needn't handle non-finite values. No bound on the sum of `lengths` on one device may be relied on, other than what follows from the above.
Results may differ from the reference program's by a relative error of at most 0.0027.
The reference program's roundings to bfloat16 on the way (of `kernels` and `hidden`) count: a program that leaves them out, or rounds other values in their place, can miss the bound.
Values sent between devices are 32-bit elements; how exact they have to be, the bound alone decides.
No kernel may reach another device: no remote copies, remote signals or barrier semaphores. Data moves between devices by JAX's collectives and lax.ppermute only.
A program may use at most 128 MiB of HBM per device.

```python
import math
import jax
import jax.numpy as jnp
import numpy as np
from jax import lax

CH = 128
SIDE = 10
DIRS = 4
LEN = 16
G_DEV = 64
TRAJ = 64
GAMES = 4096
NW = 2304


def plant(result, rng, least, top_value):
    dims = result.shape
    spot = [jax.random.randint(jax.random.fold_in(rng, axis), (), 0, dims[axis]) for axis in range(len(dims))]
    result = result.at[tuple(spot)].set(least)
    longest = dims.index(max(dims))
    spot[longest] = (spot[longest] + 1) % dims[longest]
    return result.at[tuple(spot)].set(top_value)


def block_scale(rng, shape, cuts, low, high):
    factor_of = 1.0
    for axis_at, blocks in cuts:
        heights = jax.random.uniform(jax.random.fold_in(jax.random.fold_in(rng, 6), axis_at), (blocks,), jnp.float32, low / len(cuts), high / len(cuts))
        factor_of = factor_of * jnp.repeat(jnp.exp(heights), shape[axis_at] // blocks).reshape((-1,) + (1,) * (len(shape) - 1 - axis_at))
    return factor_of


def length_profile(amount, total, limit, lean):
    loads = [(1 << 20) // math.isqrt(rank ** lean) + 1 for rank in range(2, amount + 1)]
    rest, given = total - limit - (amount - 1), [1] * (amount - 1)
    while rest > 0:
        candidates = [i for i in range(amount - 1) if given[i] < limit]
        mass, remaining = sum([loads[i] for i in candidates]), rest
        for i in candidates:
            more = min(limit - given[i], max(1, remaining * loads[i] // mass), rest)
            given[i] = given[i] + more
            rest = rest - more
    return np.array([limit] + given)


def uneven(own_key, amount, total, reach, slope):
    if amount == 2:
        one = jax.random.randint(own_key, (), max(1, total - reach), min(reach, total - 1) + 1)
        return jnp.stack([one, total - one])
    tallies = jnp.asarray(length_profile(amount, total, reach, slope), jnp.int32)
    pairs = (amount - 1) // 2
    giver, taker = tallies[1:1 + 2 * pairs:2], tallies[2:2 + 2 * pairs:2]
    margin = jnp.minimum(giver - 1, reach - taker)
    shifted = jax.random.randint(jax.random.fold_in(own_key, 1), (pairs,), 0, 1 << 20) % (margin + 1)
    tallies = tallies.at[1:1 + 2 * pairs:2].set(giver - shifted).at[2:2 + 2 * pairs:2].set(taker + shifted)
    return tallies[jax.random.permutation(jax.random.fold_in(own_key, 2), amount)]


def gaussian(own_key, shape, scale, most, cuts=(), kind=jnp.bfloat16):
    factor_of = block_scale(own_key, shape, cuts, -0.22, 0.18) if cuts else 1.0
    result = jax.random.normal(own_key, shape, jnp.float32) * scale * factor_of
    return jnp.minimum(jnp.maximum(result, -most), most).astype(kind)


def setup_inputs(seed: int = 0) -> dict:
    streams_of = jax.random.split(jax.random.key(seed), 13)
    return {
        "board_now": gaussian(streams_of[0], (GAMES, SIDE, SIDE, CH), 1.0, 6.0, ((0, 64),)),
        "traj_boards": gaussian(streams_of[1], (TRAJ, LEN, SIDE, SIDE, CH), 1.0, 6.0, ((0, 64),)),
        "actions": plant(jax.random.randint(streams_of[2], (TRAJ, LEN), 0, DIRS * SIDE * SIDE), jax.random.fold_in(streams_of[2], 1), 0, (DIRS * SIDE * SIDE) - 1).astype(jnp.int32),
        "lengths": uneven(streams_of[3], TRAJ, TRAJ * LEN * 5 // 8, LEN, 1).astype(jnp.int32),
        "behaviour": jnp.clip(-7.0 + 2.5 * jax.random.uniform(streams_of[4], (TRAJ, LEN), jnp.float32) ** block_scale(streams_of[4], (TRAJ, LEN), ((0, 64),), -0.2, 0.2), -7.0, -4.5),
        "regular": jnp.clip(-7.0 + 2.5 * jax.random.uniform(streams_of[5], (TRAJ, LEN), jnp.float32) ** block_scale(streams_of[5], (TRAJ, LEN), ((0, 64),), -0.2, 0.2), -7.0, -4.5),
        "rewards": gaussian(streams_of[6], (TRAJ, LEN), 1.0, 4.0, ((0, 64),), jnp.float32),
        "torso": gaussian(streams_of[7], (NW, CH), (9 * CH) ** -0.5, 0.1875, (), jnp.float32),
        "policy_head": gaussian(streams_of[8], (CH, DIRS), CH ** -0.5, 0.5),
        "value_head": gaussian(streams_of[9], (CH,), 0.4, 2.390625),
        "first_moment": gaussian(streams_of[10], (NW, CH), 1.0, 6.0, ((0, 64),), jnp.float32),
        "second_moment": jnp.clip(jnp.exp(math.log(2.0) - 1.3862944 * jax.random.uniform(streams_of[11], (NW, CH), jnp.float32) ** block_scale(streams_of[11], (NW, CH), ((0, 64),), -0.2, 0.2)), 0.5, 2.0),
    }


ETA = 0.2
LEARN_RATE = 0.03
BETA_ONE = 0.9
BETA_TWO = 0.999
ADAM_EPS = 1e-08
NORM_EPS = 1e-12

def conv_sum(boards, kernel):
    extent = boards.shape[1]
    padded = jnp.pad(boards, ((0, 0), (1, 1), (1, 1), (0, 0)))
    summed = jnp.zeros(boards.shape, jnp.float32)
    for offset in range(9):
        row_start = offset // 3
        col_start = offset % 3
        window = padded[:, row_start:row_start + extent, col_start:col_start + extent, :]
        summed = summed + jnp.dot(window, kernel[offset], preferred_element_type=jnp.float32)
    return summed

def torso_forward(boards, kernels):
    layer_inputs = []
    pre_acts = []
    hidden = boards
    for layer_index in range(kernels.shape[0]):
        pre_act = conv_sum(hidden, kernels[layer_index])
        layer_inputs.append(hidden)
        pre_acts.append(pre_act)
        hidden = (hidden.astype(jnp.float32) + jax.nn.relu(pre_act)).astype(jnp.bfloat16)
    return (hidden, layer_inputs, pre_acts)

def policy_logits(hidden, policy_head):
    per_cell = jnp.dot(hidden, policy_head, preferred_element_type=jnp.float32)
    return jnp.transpose(per_cell, (0, 3, 1, 2)).reshape(hidden.shape[0], -1)

def heads_forward(hidden, policy_head, value_head, actions):
    logits = policy_logits(hidden, policy_head)
    log_total = jnp.log(lax.optimization_barrier(jnp.sum(jnp.exp(logits), axis=1)))
    action_ids = lax.broadcasted_iota(jnp.int32, logits.shape, 1)
    picked = lax.optimization_barrier(jnp.sum(jnp.where(action_ids == actions[:, None], logits, 0.0), axis=1))
    value_cells = jnp.dot(hidden, value_head, preferred_element_type=jnp.float32)
    value_estimates = jnp.tanh(lax.optimization_barrier(jnp.mean(value_cells, axis=(1, 2))))
    return (logits, log_total, picked - log_total, value_estimates)

def vee_trace_cotangents(policy_log_probs, value_estimates, behaviour, regular, rewards, trajectory_length):
    positions = jnp.arange(policy_log_probs.shape[0], dtype=jnp.int32)
    live_mask = (positions < trajectory_length).astype(jnp.float32)
    next_live = (positions + 1 < trajectory_length).astype(jnp.float32)
    clipped_ratio = jnp.minimum(1.0, jnp.exp(policy_log_probs - behaviour))
    shaped = rewards - ETA * (policy_log_probs - regular)
    next_values = jnp.concatenate([value_estimates[1:], jnp.zeros((1,), jnp.float32)]) * next_live
    deltas = live_mask * clipped_ratio * (shaped + next_values - value_estimates)

    def backward_step(running, inputs):
        delta_now, ratio_now, live_now = inputs
        correction = live_now * (delta_now + ratio_now * running)
        return (correction, correction)
    _, corrections = lax.scan(backward_step, jnp.zeros((), jnp.float32), (deltas, clipped_ratio, live_mask), reverse=True)
    targets = value_estimates + corrections
    next_targets = jnp.concatenate([targets[1:], jnp.zeros((1,), jnp.float32)]) * next_live
    policy_gradient_term = -live_mask * clipped_ratio * (shaped + next_targets - value_estimates)
    value_gradient_term = -live_mask * (targets - value_estimates)
    return (policy_gradient_term, value_gradient_term)

def heads_backward(board_shape, policy_gradient_term, value_gradient_term, logits, log_total, value_estimates, actions, policy_head, value_head):
    probabilities = jnp.exp(logits - log_total[:, None])
    action_ids = lax.broadcasted_iota(jnp.int32, logits.shape, 1)
    onehot = (action_ids == actions[:, None]).astype(jnp.float32)
    logit_grad = policy_gradient_term[:, None] * (onehot - probabilities)
    row_count = board_shape[0]
    extent = board_shape[1]
    cell_grad = jnp.transpose(logit_grad.reshape(row_count, -1, extent, extent), (0, 2, 3, 1))
    hidden_grad = jnp.dot(cell_grad, policy_head.astype(jnp.float32).T, precision=lax.Precision.HIGHEST)
    value_cell = value_gradient_term * (1.0 - value_estimates * value_estimates) / (extent * extent)
    return hidden_grad + value_cell[:, None, None, None] * value_head.astype(jnp.float32)

def layer_backward(layer_input, pre_act, out_grad, kernel, need_input):
    extent = layer_input.shape[1]
    channels = layer_input.shape[3]
    act_grad = (out_grad * (pre_act > 0)).astype(jnp.bfloat16)
    act_rows = act_grad.reshape(-1, channels)
    padded = jnp.pad(layer_input, ((0, 0), (1, 1), (1, 1), (0, 0)))
    kernel_grads = []
    input_grad = out_grad
    for offset in range(9):
        row_start = offset // 3
        col_start = offset % 3
        window = padded[:, row_start:row_start + extent, col_start:col_start + extent, :]
        kernel_grads.append(lax.dot_general(window.reshape(-1, channels), act_rows, (((0,), (0,)), ((), ())), preferred_element_type=jnp.float32))
        if need_input:
            back_term = jnp.dot(act_grad, kernel[offset].T, preferred_element_type=jnp.float32)
            back_padded = jnp.pad(back_term, ((0, 0), (row_start, 2 - row_start), (col_start, 2 - col_start), (0, 0)))
            input_grad = input_grad + back_padded[:, 1:1 + extent, 1:1 + extent, :]
    return (jnp.stack(kernel_grads), input_grad)

def torso_backward(layer_inputs, pre_acts, hidden_grad, kernels):
    kernel_grads = [None] * kernels.shape[0]
    out_grad = hidden_grad
    for layer_index in range(kernels.shape[0] - 1, -1, -1):
        kernel_grads[layer_index], out_grad = layer_backward(layer_inputs[layer_index], pre_acts[layer_index], out_grad, kernels[layer_index], layer_index > 0)
    return jnp.stack(kernel_grads)

def trajectory_gradient(kernels, policy_head, value_head, boards, actions, behaviour, regular, rewards, trajectory_length):
    hidden, layer_inputs, pre_acts = torso_forward(boards, kernels)
    logits, log_total, policy_log_probs, value_estimates = heads_forward(hidden, policy_head, value_head, actions)
    policy_gradient_term, value_gradient_term = vee_trace_cotangents(policy_log_probs, value_estimates, behaviour, regular, rewards, trajectory_length)
    hidden_grad = heads_backward(boards.shape, policy_gradient_term, value_gradient_term, logits, log_total, value_estimates, actions, policy_head, value_head)
    return torso_backward(layer_inputs, pre_acts, hidden_grad, kernels)

def reference(board_now, traj_boards, actions, lengths, behaviour, regular, rewards, torso, policy_head, value_head, first_moment, second_moment):
    channels = torso.shape[1]
    kernels = torso.astype(jnp.bfloat16).reshape(-1, 9, channels, channels)

    def gradient_accumulator(running, inputs):
        boards_one, actions_one, behaviour_one, regular_one, single_game_rewards, length_one = inputs
        term = trajectory_gradient(kernels, policy_head, value_head, boards_one, actions_one, behaviour_one, regular_one, single_game_rewards, length_one)
        return (running + term, None)
    initial = jnp.zeros(kernels.shape, jnp.float32)
    summed_grad, _ = lax.scan(gradient_accumulator, initial, (traj_boards, actions, behaviour, regular, rewards, lengths))
    gradient = summed_grad.reshape(torso.shape)
    square_sum = jnp.sum(gradient * gradient)
    factor = jnp.minimum(1.0, jnp.sqrt(float(gradient.size)) / jnp.sqrt(square_sum + NORM_EPS))
    clipped = gradient * factor
    moment_one = BETA_ONE * first_moment + (1.0 - BETA_ONE) * clipped
    moment_two = BETA_TWO * second_moment + (1.0 - BETA_TWO) * clipped * clipped
    new_weights = torso - LEARN_RATE * moment_one / (jnp.sqrt(moment_two) + ADAM_EPS)
    new_kernels = new_weights.astype(jnp.bfloat16).reshape(-1, 9, channels, channels)
    game_blocks = board_now.reshape((GAMES // G_DEV, G_DEV) + board_now.shape[1:])

    def act_block(boards_block):
        hidden, _, _ = torso_forward(boards_block, new_kernels)
        logits = policy_logits(hidden, policy_head)
        return logits - jnp.log(lax.optimization_barrier(jnp.sum(jnp.exp(logits), axis=1, keepdims=True)))
    move_logp = lax.map(act_block, game_blocks).reshape(GAMES, -1)
    return (new_weights, move_logp)
```

```python
import math

import jax
import jax.numpy as jnp
from jax import lax
from jax.sharding import PartitionSpec as P

ETA = 0.2
LEARN_RATE = 0.03
BETA_ONE = 0.9
BETA_TWO = 0.999
ADAM_EPS = 1e-08
NORM_EPS = 1e-12


SIDE_CHIPS = 4


def shift_pairs(axis, step):
    stride = {"y": 16, "x": 4, "z": 1}[axis]
    pairs = []
    for source in range(SIDE_CHIPS**3):
        at = source // stride % SIDE_CHIPS
        pairs.append((source, source + ((at + step) % SIDE_CHIPS - at) * stride))
    return pairs


def shifted(x, axis, step):
    return lax.ppermute(x, "dp", shift_pairs(axis, step))


def line_total(x, axis):
    return (x + shifted(x, axis, 2)) + (shifted(x, axis, 1) + shifted(x, axis, 3))


def line_scatter(x, axis, position):
    chunks = x.reshape((SIDE_CHIPS, -1) + x.shape[1:])

    def chunk(step):
        return lax.dynamic_index_in_dim(chunks, (position + step) % SIDE_CHIPS, 0, keepdims=False)

    return (chunk(0) + shifted(chunk(2), axis, 2)) + (
        shifted(chunk(1), axis, 1) + shifted(chunk(3), axis, 3)
    )


def line_gather(x, axis, position):
    whole = jnp.zeros((SIDE_CHIPS,) + x.shape, x.dtype)
    whole = lax.dynamic_update_index_in_dim(whole, x, position, 0)
    for step in range(1, SIDE_CHIPS):
        whole = lax.dynamic_update_index_in_dim(
            whole, shifted(x, axis, step), (position - step) % SIDE_CHIPS, 0
        )
    return whole.reshape((-1,) + x.shape[1:])


def role_swap(x):
    return lax.ppermute(x, "role", [(0, 1), (1, 0)])


def plane_moments(first_moment, second_moment, role_index):
    both = jnp.stack([first_moment, second_moment])
    planes = [[16 * y + k for k in range(16)] for y in range(SIDE_CHIPS)]
    plane = lax.all_gather(both, "dp", axis_index_groups=planes)
    half = lax.dynamic_slice_in_dim(plane, role_index * 8, 8, 0)
    pairs = []
    for role in range(2):
        for y in range(SIDE_CHIPS):
            for k in range(16):
                pairs.append((role * 64 + y * 16 + k, (y // 2) * 64 + (2 * (y % 2) + role) * 16 + k))
    half = lax.ppermute(half, ("role", "dp"), pairs)
    half = jnp.swapaxes(half, 0, 1).reshape(2, -1, half.shape[-1])
    return half[0], half[1]


def conv_sum(boards, kernel):
    extent = boards.shape[1]
    padded = jnp.pad(boards, ((0, 0), (1, 1), (1, 1), (0, 0)))
    summed = jnp.zeros(boards.shape, jnp.float32)
    for offset in range(9):
        row_start = offset // 3
        col_start = offset % 3
        window = padded[:, row_start : row_start + extent, col_start : col_start + extent, :]
        summed = summed + jnp.dot(window, kernel[offset], preferred_element_type=jnp.float32)
    return summed


def torso_forward(boards, kernels):
    layer_inputs = []
    pre_acts = []
    hidden = boards
    for layer_index in range(kernels.shape[0]):
        pre_act = conv_sum(hidden, kernels[layer_index])
        layer_inputs.append(hidden)
        pre_acts.append(pre_act)
        hidden = (hidden.astype(jnp.float32) + jax.nn.relu(pre_act)).astype(jnp.bfloat16)
    return (hidden, layer_inputs, pre_acts)


def policy_logits(hidden, policy_head):
    per_cell = jnp.dot(hidden, policy_head, preferred_element_type=jnp.float32)
    return jnp.transpose(per_cell, (0, 3, 1, 2)).reshape(hidden.shape[0], -1)


def heads_forward(hidden, policy_head, value_head, actions):
    logits = policy_logits(hidden, policy_head)
    log_total = jnp.log(jnp.sum(jnp.exp(logits), axis=1))
    action_ids = lax.broadcasted_iota(jnp.int32, logits.shape, 1)
    picked = jnp.sum(jnp.where(action_ids == actions[:, None], logits, 0.0), axis=1)
    value_cells = jnp.dot(hidden, value_head, preferred_element_type=jnp.float32)
    value_estimates = jnp.tanh(jnp.mean(value_cells, axis=(1, 2)))
    return (logits, log_total, picked - log_total, value_estimates)


def vee_trace_cotangents(
    policy_log_probs, value_estimates, behaviour, regular, rewards, trajectory_length
):
    positions = jnp.arange(policy_log_probs.shape[0], dtype=jnp.int32)
    live_mask = (positions < trajectory_length).astype(jnp.float32)
    next_live = (positions + 1 < trajectory_length).astype(jnp.float32)
    clipped_ratio = jnp.minimum(1.0, jnp.exp(policy_log_probs - behaviour))
    shaped = rewards - ETA * (policy_log_probs - regular)
    next_values = jnp.concatenate([value_estimates[1:], jnp.zeros((1,), jnp.float32)]) * next_live
    deltas = live_mask * clipped_ratio * (shaped + next_values - value_estimates)

    corrections = deltas
    decay = live_mask * clipped_ratio
    reach = 1
    while reach < positions.shape[0]:
        later = jnp.concatenate([corrections[reach:], jnp.zeros((reach,), jnp.float32)])
        corrections = corrections + decay * later
        decay = decay * jnp.concatenate([decay[reach:], jnp.zeros((reach,), jnp.float32)])
        reach *= 2
    targets = value_estimates + corrections
    next_targets = jnp.concatenate([targets[1:], jnp.zeros((1,), jnp.float32)]) * next_live
    policy_gradient_term = -live_mask * clipped_ratio * (shaped + next_targets - value_estimates)
    value_gradient_term = -live_mask * (targets - value_estimates)
    return (policy_gradient_term, value_gradient_term)


def heads_backward(
    board_shape,
    policy_gradient_term,
    value_gradient_term,
    logits,
    log_total,
    value_estimates,
    actions,
    policy_head,
    value_head,
):
    probabilities = jnp.exp(logits - log_total[:, None])
    action_ids = lax.broadcasted_iota(jnp.int32, logits.shape, 1)
    onehot = (action_ids == actions[:, None]).astype(jnp.float32)
    logit_grad = policy_gradient_term[:, None] * (onehot - probabilities)
    row_count = board_shape[0]
    extent = board_shape[1]
    cell_grad = jnp.transpose(logit_grad.reshape(row_count, -1, extent, extent), (0, 2, 3, 1))
    hidden_grad = jnp.dot(
        cell_grad, policy_head.astype(jnp.float32).T, precision=lax.Precision.HIGHEST
    )
    value_cell = value_gradient_term * (1.0 - value_estimates * value_estimates) / (extent * extent)
    return hidden_grad + value_cell[:, None, None, None] * value_head.astype(jnp.float32)


def layer_backward(layer_input, pre_act, out_grad, kernel, need_input):
    extent = layer_input.shape[1]
    channels = layer_input.shape[3]
    act_grad = (out_grad * (pre_act > 0)).astype(jnp.bfloat16)
    act_rows = act_grad.reshape(-1, channels)
    padded = jnp.pad(layer_input, ((0, 0), (1, 1), (1, 1), (0, 0)))
    kernel_grads = []
    input_grad = out_grad
    for offset in range(9):
        row_start = offset // 3
        col_start = offset % 3
        window = padded[:, row_start : row_start + extent, col_start : col_start + extent, :]
        kernel_grads.append(
            lax.dot_general(
                window.reshape(-1, channels),
                act_rows,
                (((0,), (0,)), ((), ())),
                preferred_element_type=jnp.float32,
            )
        )
        if need_input:
            back_term = jnp.dot(act_grad, kernel[offset].T, preferred_element_type=jnp.float32)
            back_padded = jnp.pad(
                back_term, ((0, 0), (row_start, 2 - row_start), (col_start, 2 - col_start), (0, 0))
            )
            input_grad = input_grad + back_padded[:, 1 : 1 + extent, 1 : 1 + extent, :]
    return (jnp.stack(kernel_grads), input_grad)


def torso_backward(layer_inputs, pre_acts, hidden_grad, kernels):
    kernel_grads = [None] * kernels.shape[0]
    out_grad = hidden_grad
    for layer_index in range(kernels.shape[0] - 1, -1, -1):
        kernel_grads[layer_index], out_grad = layer_backward(
            layer_inputs[layer_index],
            pre_acts[layer_index],
            out_grad,
            kernels[layer_index],
            layer_index > 0,
        )
    return jnp.stack(kernel_grads)


def learner_gradient(
    kernels,
    policy_head,
    value_head,
    boards,
    actions,
    behaviour,
    regular,
    rewards,
    trajectory_length,
):
    hidden, layer_inputs, pre_acts = torso_forward(boards, kernels)
    logits, log_total, policy_log_probs, value_estimates = heads_forward(
        hidden, policy_head, value_head, actions
    )
    policy_gradient_term, value_gradient_term = vee_trace_cotangents(
        policy_log_probs, value_estimates, behaviour, regular, rewards, trajectory_length
    )
    hidden_grad = heads_backward(
        boards.shape,
        policy_gradient_term,
        value_gradient_term,
        logits,
        log_total,
        value_estimates,
        actions,
        policy_head,
        value_head,
    )
    return torso_backward(layer_inputs, pre_acts, hidden_grad, kernels)


def body(
    board_now,
    traj_boards,
    actions,
    lengths,
    behaviour,
    regular,
    rewards,
    torso,
    policy_head,
    value_head,
    first_moment,
    second_moment,
):
    role_index = lax.axis_index("role")
    dp_index = lax.axis_index("dp")
    channels = torso.shape[1]
    kernels = torso.astype(jnp.bfloat16).reshape(-1, 9, channels, channels)

    y = dp_index // 16
    moment_one, moment_two = plane_moments(first_moment, second_moment, role_index)
    gradients = learner_gradient(
        kernels,
        policy_head,
        value_head,
        traj_boards[0],
        actions[0],
        behaviour[0],
        regular[0],
        rewards[0],
        lengths[0],
    )
    mine = lax.dynamic_index_in_dim(gradients, role_index, 0, keepdims=False)
    mine = mine.reshape(-1, channels)
    layer_rows = mine.shape[0]
    quarter = layer_rows // SIDE_CHIPS
    share = line_scatter(mine, "y", y)
    share = line_total(share, "x")
    share = line_total(share, "z")
    squares = jnp.sum(share * share, axis=0, keepdims=True)
    squares = squares + role_swap(squares)
    squares = line_total(squares, "y")
    square_sum = jnp.sum(squares)
    factor = jnp.minimum(1.0, jnp.sqrt(float(torso.size)) / jnp.sqrt(square_sum + NORM_EPS))
    clipped = share * factor
    moment_one = BETA_ONE * moment_one + (1.0 - BETA_ONE) * clipped
    moment_two = BETA_TWO * moment_two + (1.0 - BETA_TWO) * clipped * clipped
    old_share = lax.dynamic_slice_in_dim(torso, role_index * layer_rows + y * quarter, quarter, 0)
    weight_share = old_share - LEARN_RATE * moment_one / (jnp.sqrt(moment_two) + ADAM_EPS)
    layer_mine = line_gather(weight_share, "y", y)
    layer_other = role_swap(layer_mine)
    new_torso = jnp.concatenate(
        [
            jnp.where(role_index == 0, layer_mine, layer_other),
            jnp.where(role_index == 0, layer_other, layer_mine),
        ]
    )
    share_rows = first_moment.shape[0]
    new_share = lax.dynamic_slice_in_dim(new_torso, dp_index * share_rows, share_rows, 0)
    new_kernels = new_torso.astype(jnp.bfloat16).reshape(-1, 9, channels, channels)
    hidden, _, _ = torso_forward(board_now, new_kernels)
    logits = policy_logits(hidden, policy_head)
    move_logp = logits - jnp.log(jnp.sum(jnp.exp(logits), axis=1, keepdims=True))
    return (new_share, move_logp)


def solution(mesh):
    return jax.shard_map(
        body,
        mesh=mesh,
        in_specs=(
            P("dp", None, None, None),
            P("dp", None, None, None, None),
            P("dp", None),
            P("dp"),
            P("dp", None),
            P("dp", None),
            P("dp", None),
            P(),
            P(),
            P(),
            P("dp", None),
            P("dp", None),
        ),
        out_specs=(P("dp", None), P("dp", None)),
        check_vma=False,
    )
```

```python
import functools

import jax
import jax.numpy as jnp
from jax import lax
from jax.experimental import pallas as pl
from jax.experimental.pallas import tpu as pltpu
from jax.sharding import PartitionSpec as P

ETA = 0.2
LEARN_RATE = 0.03
BETA_ONE = 0.9
BETA_TWO = 0.999
ADAM_EPS = 1e-08
NORM_EPS = 1e-12
ROWS = 1152
LINE = 4
SHARE = ROWS // (LINE * LINE)


def by_cell(boards):
    return jnp.transpose(boards, (1, 2, 0, 3))


def inner_cells(ref):
    return ref.reshape((12, 12) + ref.shape[3:]).at[1:11, 1:11]


def clear_border(ref):
    zero_row = jnp.zeros(ref.shape[1:], ref.dtype)
    ref[0] = zero_row
    ref[11] = zero_row
    zero_col = jnp.zeros((12,) + ref.shape[3:], ref.dtype)
    ref[:, 0, 0] = zero_col
    ref[:, 5, 1] = zero_col


def pair_kernels(kernel_of, store):
    nothing = jnp.zeros((128, 128), jnp.bfloat16)
    for p in range(3):
        row = [kernel_of(p, q) for q in range(3)]
        for q in range(4):
            left = row[q] if q < 3 else nothing
            right = row[q - 1] if q > 0 else nothing
            store(4 * p + q, jnp.concatenate([left, right], axis=1))


def conv_pairs(source, pair_weights, first, count):
    windows = []
    for p in range(3):
        for q in range(4):
            window = source[pl.ds(first + p, count), q // 2 : q // 2 + 5, q % 2]
            windows.append(window.reshape(-1, 128))
    return jnp.dot(
        jnp.concatenate(windows, axis=1), pair_weights, preferred_element_type=jnp.float32
    )


def residual(source, first, count, parity):
    if parity == 0:
        window = source[pl.ds(first + 1, count), 0:5, 1]
    else:
        window = source[pl.ds(first + 1, count), 1:6, 0]
    return window


def put_cells(target, first, count, parity, value):
    if parity == 0:
        target[pl.ds(first + 1, count), 0:5, 1] = value
    else:
        target[pl.ds(first + 1, count), 1:6, 0] = value


def actor_kernel(
    count, unroll, role, mine, other, boards_in, heads8, out, boards, pairs, middle, last, heads, done
):
    games = boards.shape[3]
    fetch = pltpu.make_async_copy(boards_in, inner_cells(boards), done)
    fetch.start()
    spread = lax.broadcasted_iota(jnp.int32, (8, 1280), 1)
    row = lax.broadcasted_iota(jnp.int32, (8, 1280), 0)
    spread = ((spread % 128 == 10 * row + spread // 128) & (row < 4)).astype(jnp.float32)
    by_column = lax.dot_general(
        heads8[...], spread, (((0,), (0,)), ((), ())), preferred_element_type=jnp.float32
    )
    for j in range(10):
        heads[128 * j : 128 * j + 128, :] = by_column[:, 128 * j : 128 * j + 128].astype(jnp.bfloat16)
    for layer in range(2):
        def kernel_of(p, q, layer=layer):
            at = (3 * p + q) * 128
            block = jnp.where(role[0] == layer, mine[at : at + 128, :], other[at : at + 128, :])
            return block.astype(jnp.bfloat16)

        def store(block, value, layer=layer):
            pairs[layer, block * 128 : (block + 1) * 128, :] = value

        pair_kernels(kernel_of, store)
    clear_border(middle)
    clear_border(boards)
    fetch.wait()

    def run_layer(layer, source, emit):
        def step(at, carry):
            first = at * count
            pre = conv_pairs(source, pairs[layer], first, count)
            for parity in range(2):
                part = pre[:, parity * 128 : (parity + 1) * 128].reshape(count, 5, games, 128)
                before = residual(source, first, count, parity).astype(jnp.float32)
                emit(first, parity, (before + jnp.maximum(part, 0.0)).astype(jnp.bfloat16))
            return carry

        lax.fori_loop(0, 10 // count, step, 0, unroll=unroll)

    run_layer(0, boards, lambda first, parity, value: put_cells(middle, first, count, parity, value))

    def to_last(first, parity, value):
        last[pl.ds(first, count), :, parity] = value

    run_layer(1, middle, to_last)
    cells = [last[:, j // 2, j % 2].reshape(-1, 128) for j in range(10)]
    logits = jnp.dot(jnp.concatenate(cells, axis=1), heads[...], preferred_element_type=jnp.float32)
    logits = logits.reshape(10, games, 128)
    lanes = lax.broadcasted_iota(jnp.int32, (games, 128), 1)
    moves = []
    total = jnp.zeros((games, 1), jnp.float32)
    for d in range(4):
        gathered = jnp.zeros((games, 128), jnp.float32)
        for i in range(10):
            turned = pltpu.roll(logits[i], (10 * i - 10 * d) % 128, 1)
            gathered = jnp.where((lanes >= 10 * i) & (lanes < 10 * i + 10), turned, gathered)
        moves.append(gathered)
        total = total + jnp.sum(
            jnp.where(lanes < 100, jnp.exp(gathered), 0.0), axis=1, keepdims=True
        )
    log_total = jnp.log(total)
    for d in range(4):
        out[:, 100 * d : 100 * d + 100] = (moves[d] - log_total)[:, :100]


def act(role, mine, other, boards, heads8, count=2, unroll=1):
    games = boards.shape[2]
    vmem = pl.BlockSpec(memory_space=pltpu.VMEM)
    return pl.pallas_call(
        functools.partial(actor_kernel, count, unroll),
        out_shape=jax.ShapeDtypeStruct((games, 400), jnp.float32),
        in_specs=[
            pl.BlockSpec(memory_space=pltpu.SMEM), vmem, vmem, pl.BlockSpec(memory_space=pltpu.HBM), vmem
        ],
        out_specs=vmem,
        scratch_shapes=[
            pltpu.VMEM((12, 6, 2, games, 128), jnp.bfloat16),
            pltpu.VMEM((2, 1536, 256), jnp.bfloat16),
            pltpu.VMEM((12, 6, 2, games, 128), jnp.bfloat16),
            pltpu.VMEM((10, 5, 2, games, 128), jnp.bfloat16),
            pltpu.VMEM((1280, 128), jnp.bfloat16),
            pltpu.SemaphoreType.DMA,
        ],
        compiler_params=pltpu.CompilerParams(vmem_limit_bytes=32 * 1024 * 1024),
        cost_estimate=pl.CostEstimate(
            flops=8 * 10**9, bytes_accessed=4 * 10**6, transcendentals=30000
        ),
        name="act",
    )(role, mine, other, boards, heads8)


def column_of(row):
    size = row.shape[1]
    across = lax.broadcasted_iota(jnp.int32, (size, size), 1)
    down = lax.broadcasted_iota(jnp.int32, (size, size), 0)
    spread = jnp.broadcast_to(row, (size, size))
    return jnp.sum(jnp.where(across == down, spread, jnp.zeros_like(spread)), axis=1, keepdims=True)


def later(x, reach):
    return jnp.concatenate([x[reach:], jnp.zeros((reach, x.shape[1]), x.dtype)], axis=0)


def learner_kernel(
    count, role, length, boards_in, actions_in, behaviour_in, regular_in, rewards_in, weights_in,
    heads8, grad,
    boards, weights, actions, behaviour, regular, rewards, pairs, back_pairs, middle, last, masks,
    slope, done,
):
    slots = boards.shape[3]
    moves = [
        (weights_in.at[0:ROWS], weights.at[0:ROWS]),
        (boards_in, inner_cells(boards)),
        (weights_in.at[ROWS : 2 * ROWS], weights.at[ROWS : 2 * ROWS]),
        (actions_in, actions),
        (behaviour_in, behaviour),
        (regular_in, regular),
        (rewards_in, rewards),
    ]
    copies = [pltpu.make_async_copy(a, b, done.at[k]) for k, (a, b) in enumerate(moves)]
    for copy in copies:
        copy.start()
    eight = heads8[...].astype(jnp.bfloat16).astype(jnp.float32)
    heads_t = jnp.concatenate(
        [eight, eight, eight, jnp.zeros((104, 128), jnp.float32)], axis=0
    ).astype(jnp.bfloat16)
    clear_border(boards)
    copies[0].wait()

    for layer in range(2):
        if layer == 1:
            copies[2].wait()

        def kernel_of(p, q, layer=layer):
            at = layer * ROWS + (3 * p + q) * 128
            return weights[at : at + 128, :].astype(jnp.bfloat16)

        def store(block, value, layer=layer):
            pairs[layer, block * 128 : (block + 1) * 128, :] = value

        pair_kernels(kernel_of, store)
    clear_border(middle)
    clear_border(slope)
    copies[1].wait()

    def run_layer(layer, source, emit):
        for first in range(0, 10, count):
            pre = conv_pairs(source, pairs[layer], first, count)
            for parity in range(2):
                part = pre[:, parity * 128 : (parity + 1) * 128].reshape(count, 5, slots, 128)
                before = residual(source, first, count, parity).astype(jnp.float32)
                emit(first, parity, (before + jnp.maximum(part, 0.0)).astype(jnp.bfloat16))
                masks[layer, first : first + count, :, parity] = (part > 0).astype(jnp.bfloat16)

    run_layer(0, boards, lambda first, parity, value: put_cells(middle, first, count, parity, value))

    def to_last(first, parity, value):
        last[pl.ds(first, count), :, parity] = value

    run_layer(1, middle, to_last)

    for copy in copies[3:]:
        copy.wait()

    scores = lax.dot_general(
        last[...].reshape(-1, 128), heads_t, (((1,), (1,)), ((), ())),
        preferred_element_type=jnp.float32,
    ).reshape(100, slots, 128)
    lane = lax.broadcasted_iota(jnp.int32, (slots, 128), 1)
    weights_sum = jnp.sum(jnp.where(lane < 4, jnp.exp(scores), 0.0), axis=0)
    log_total = jnp.log(jnp.sum(weights_sum, axis=1, keepdims=True))
    action = column_of(actions[...])
    direction = action // 100
    cell = action - 100 * direction
    cells = lax.broadcasted_iota(jnp.int32, (100, slots, 128), 0)
    taken = (cells == cell[None]) & (lane % 8 == direction)[None]
    picked = jnp.sum(
        jnp.sum(jnp.where(taken & (lane < 4)[None], scores, 0.0), axis=0), axis=1, keepdims=True
    )
    value_sum = jnp.sum(scores, axis=0)
    value = jnp.tanh(
        jnp.sum(jnp.where(lane == 4, value_sum, 0.0), axis=1, keepdims=True) / 100.0
    )
    log_policy = picked - log_total

    positions = lax.broadcasted_iota(jnp.int32, (slots, 1), 0)
    live = (positions < length[0]).astype(jnp.float32)
    next_live = (positions + 1 < length[0]).astype(jnp.float32)
    ratio = jnp.minimum(1.0, jnp.exp(log_policy - column_of(behaviour[...])))
    shaped = column_of(rewards[...]) - ETA * (log_policy - column_of(regular[...]))
    next_values = later(value, 1) * next_live
    correction = live * ratio * (shaped + next_values - value)
    decay = live * ratio
    reach = 1
    while reach < slots:
        correction = correction + decay * later(correction, reach)
        decay = decay * later(decay, reach)
        reach *= 2
    targets = value + correction
    next_targets = later(targets, 1) * next_live
    policy_grad = -live * ratio * (shaped + next_targets - value)
    value_grad = -live * (targets - value)

    value_cell = value_grad * (1.0 - value * value) / 100.0
    by_policy = policy_grad[None] * (taken.astype(jnp.float32) - jnp.exp(scores - log_total[None]))
    in_policy = (lane % 8 < 4) & (lane < 24)
    in_value = (lane % 8 == 4) & (lane < 24)
    by_score = jnp.where(
        in_policy[None], by_policy, jnp.where(in_value, value_cell, 0.0)[None]
    )
    high = by_score.astype(jnp.bfloat16)
    rest = by_score - high.astype(jnp.float32)
    mid = rest.astype(jnp.bfloat16)
    low = rest - mid.astype(jnp.float32)
    parts = jnp.where(
        (lane < 8)[None],
        high.astype(jnp.float32),
        jnp.where((lane < 16)[None], mid.astype(jnp.float32), low),
    ).astype(jnp.bfloat16)
    out_grad = jnp.dot(
        parts.reshape(-1, 128), heads_t, preferred_element_type=jnp.float32
    )
    act_grad = (out_grad * masks[1].reshape(-1, 128).astype(jnp.float32)).astype(jnp.bfloat16)

    def kernel_gradients(source, act_grad):
        turned = act_grad.T
        windows = []
        for p in range(3):
            for q in range(3):
                cols = [source[p : p + 10, (j + q) // 2, (j + q) % 2] for j in range(10)]
                windows.append(jnp.stack(cols, axis=1).reshape(-1, 128))
        for offset in range(9):
            block = jnp.dot(turned, windows[offset], preferred_element_type=jnp.float32)
            grad[offset * 128 : (offset + 1) * 128, :] = block.T

    @pl.when(role[0] == 1)
    def _():
        kernel_gradients(middle, act_grad)

    @pl.when(role[0] == 0)
    def _():
        def kernel_of(p, q):
            at = ROWS + (8 - (3 * p + q)) * 128
            return weights[at : at + 128, :].T.astype(jnp.bfloat16)

        def store(block, value):
            back_pairs[block * 128 : (block + 1) * 128, :] = value

        pair_kernels(kernel_of, store)
        act_cells = act_grad.reshape(10, 5, 2, slots, 128)
        put_cells(slope, 0, 10, 0, act_cells[:, :, 0])
        put_cells(slope, 0, 10, 1, act_cells[:, :, 1])
        out_cells = out_grad.reshape(10, 5, 2, slots, 128)
        for first in range(0, 10, count):
            back = conv_pairs(slope, back_pairs[...], first, count)
            for parity in range(2):
                part = back[:, parity * 128 : (parity + 1) * 128].reshape(count, 5, slots, 128)
                total = out_cells[first : first + count, :, parity] + part
                gate = masks[0, first : first + count, :, parity].astype(jnp.float32)
                last[pl.ds(first, count), :, parity] = (total * gate).astype(jnp.bfloat16)
        kernel_gradients(boards, last[...].reshape(-1, 128))


def head_rows(policy_head, value_head):
    five = jnp.concatenate([policy_head.T, value_head[None]]).astype(jnp.float32)
    return jnp.pad(five, ((0, 3), (0, 0)))


def learn(role, length, boards, actions, behaviour, regular, rewards, weights, heads8, count=5):
    slots = boards.shape[2]
    smem = pl.BlockSpec(memory_space=pltpu.SMEM)
    vmem = pl.BlockSpec(memory_space=pltpu.VMEM)
    anywhere = pl.BlockSpec(memory_space=pltpu.HBM)
    cells = (10, 5, 2, slots, 128)
    around = (12, 6, 2, slots, 128)
    return pl.pallas_call(
        functools.partial(learner_kernel, count),
        out_shape=jax.ShapeDtypeStruct((ROWS, 128), jnp.float32),
        in_specs=[smem, smem] + [anywhere] * 6 + [vmem],
        out_specs=vmem,
        scratch_shapes=[
            pltpu.VMEM(around, jnp.bfloat16),
            pltpu.VMEM((2 * ROWS, 128), jnp.float32),
            pltpu.VMEM((1, slots), jnp.int32),
            pltpu.VMEM((1, slots), jnp.float32),
            pltpu.VMEM((1, slots), jnp.float32),
            pltpu.VMEM((1, slots), jnp.float32),
            pltpu.VMEM((2, 1536, 256), jnp.bfloat16),
            pltpu.VMEM((1536, 256), jnp.bfloat16),
            pltpu.VMEM(around, jnp.bfloat16),
            pltpu.VMEM(cells, jnp.bfloat16),
            pltpu.VMEM((2,) + cells, jnp.bfloat16),
            pltpu.VMEM(around, jnp.bfloat16),
            pltpu.SemaphoreType.DMA((7,)),
        ],
        compiler_params=pltpu.CompilerParams(vmem_limit_bytes=60 * 1024 * 1024),
        cost_estimate=pl.CostEstimate(
            flops=4 * 10**9, bytes_accessed=3 * 10**6, transcendentals=10000
        ),
        name="learn",
    )(role, length, boards, actions, behaviour, regular, rewards, weights, heads8)


PLANES = [[LINE * k + z for k in range(LINE * LINE)] for z in range(LINE)]


def shifted_z(x, step):
    pairs = [(d, d - d % LINE + (d + step) % LINE) for d in range(LINE**3)]
    return lax.ppermute(x, "dp", pairs)


def line_total(x):
    return (x + shifted_z(x, 2)) + (shifted_z(x, 1) + shifted_z(x, 3))


def plane_exchange(x):
    return lax.all_to_all(x, "dp", 0, 0, axis_index_groups=PLANES)


def plane_gather(x):
    return plane_exchange(jnp.broadcast_to(x, (LINE * LINE,) + x.shape))


def role_swap(x):
    return lax.ppermute(x, "role", [(0, 1), (1, 0)])


def share_moments(first_moment, second_moment, z):
    both = jnp.stack([first_moment, second_moment])
    got = []
    for k in range(2):
        pairs = []
        for role in range(2):
            for d in range(LINE**3):
                z_of = d % LINE
                owner = 32 * role + 2 * (d // LINE) + (k + z_of) % 2
                pairs.append(((z_of // 2) * LINE**3 + owner, role * LINE**3 + d))
        got.append(lax.ppermute(both, ("role", "dp"), pairs))
    even = z % 2 == 0
    low = jnp.where(even, got[0], got[1])
    high = jnp.where(even, got[1], got[0])
    return jnp.concatenate([low, high], axis=1)


def body(
    board_now,
    traj_boards,
    actions,
    lengths,
    behaviour,
    regular,
    rewards,
    torso,
    policy_head,
    value_head,
    first_moment,
    second_moment,
):
    role = lax.axis_index("role")
    dp = lax.axis_index("dp")
    role_box = jnp.full((1,), role, jnp.int32)
    heads8 = head_rows(policy_head, value_head)
    moments = share_moments(first_moment, second_moment, dp % LINE)
    gradient = learn(
        role_box,
        lengths,
        by_cell(traj_boards[0]),
        actions,
        behaviour,
        regular,
        rewards,
        torso,
        heads8,
    )
    share = jnp.sum(plane_exchange(gradient.reshape(LINE * LINE, SHARE, 128)), axis=0)
    share = line_total(share)
    squares = jnp.sum(share * share, axis=0, keepdims=True)
    squares = plane_gather(squares + role_swap(squares))
    square_sum = jnp.sum(squares)
    factor = jnp.minimum(1.0, jnp.sqrt(float(torso.size)) / jnp.sqrt(square_sum + NORM_EPS))
    clipped = share * factor
    moment_one = BETA_ONE * moments[0] + (1.0 - BETA_ONE) * clipped
    moment_two = BETA_TWO * moments[1] + (1.0 - BETA_TWO) * clipped * clipped
    old_share = lax.dynamic_slice_in_dim(torso, role * ROWS + dp // LINE * SHARE, SHARE, 0)
    weight_share = old_share - LEARN_RATE * moment_one / (jnp.sqrt(moment_two) + ADAM_EPS)
    mine = plane_gather(weight_share).reshape(ROWS, 128)
    other = role_swap(mine)
    move_logp = act(role_box, mine, other, by_cell(board_now), heads8)
    out_rows = first_moment.shape[0]
    layer = dp // (LINE**3 // 2)
    at = dp % (LINE**3 // 2) * out_rows
    new_share = jnp.where(
        role == layer,
        lax.dynamic_slice_in_dim(mine, at, out_rows, 0),
        lax.dynamic_slice_in_dim(other, at, out_rows, 0),
    )
    return (new_share, move_logp)


def solution(mesh):
    return jax.shard_map(
        body,
        mesh=mesh,
        in_specs=(
            P("dp", None, None, None),
            P("dp", None, None, None, None),
            P("dp", None),
            P("dp"),
            P("dp", None),
            P("dp", None),
            P("dp", None),
            P(),
            P(),
            P(),
            P("dp", None),
            P("dp", None),
        ),
        out_specs=(P("dp", None), P("dp", None)),
        check_vma=False,
    )
```

```python
import functools

import jax
import jax.numpy as jnp
from jax import lax
from jax.experimental import pallas as pl
from jax.experimental.pallas import tpu as pltpu
from jax.sharding import PartitionSpec as P

ETA = 0.2
LEARN_RATE = 0.03
BETA_ONE = 0.9
BETA_TWO = 0.999
ADAM_EPS = 1e-08
NORM_EPS = 1e-12
ROWS = 1152
LINE = 4
SHARE = ROWS // (LINE * LINE)


def by_cell(boards):
    return jnp.transpose(boards, (1, 2, 0, 3))


def inner_cells(ref):
    return ref.reshape((12, 12) + ref.shape[3:]).at[1:11, 1:11]


def clear_border(ref):
    zero_row = jnp.zeros(ref.shape[1:], ref.dtype)
    ref[0] = zero_row
    ref[11] = zero_row
    zero_col = jnp.zeros((12,) + ref.shape[3:], ref.dtype)
    ref[:, 0, 0] = zero_col
    ref[:, 5, 1] = zero_col


def pair_kernels(kernel_of, store):
    nothing = jnp.zeros((128, 128), jnp.bfloat16)
    for p in range(3):
        row = [kernel_of(p, q) for q in range(3)]
        for q in range(4):
            left = row[q] if q < 3 else nothing
            right = row[q - 1] if q > 0 else nothing
            store(4 * p + q, jnp.concatenate([left, right], axis=1))


def conv_pairs(source, pair_weights, first, count):
    windows = []
    for p in range(3):
        for q in range(4):
            window = source[pl.ds(first + p, count), q // 2 : q // 2 + 5, q % 2]
            windows.append(window.reshape(-1, 128))
    return jnp.dot(
        jnp.concatenate(windows, axis=1), pair_weights, preferred_element_type=jnp.float32
    )


def residual(source, first, count, parity):
    if parity == 0:
        window = source[pl.ds(first + 1, count), 0:5, 1]
    else:
        window = source[pl.ds(first + 1, count), 1:6, 0]
    return window


def put_cells(target, first, count, parity, value):
    if parity == 0:
        target[pl.ds(first + 1, count), 0:5, 1] = value
    else:
        target[pl.ds(first + 1, count), 1:6, 0] = value


def actor_kernel(
    count, unroll, role, mine, other, boards_in, heads8, out, boards, pairs, middle, last, heads, done
):
    games = boards.shape[3]
    fetch = pltpu.make_async_copy(boards_in, inner_cells(boards), done)
    fetch.start()
    spread = lax.broadcasted_iota(jnp.int32, (8, 1280), 1)
    row = lax.broadcasted_iota(jnp.int32, (8, 1280), 0)
    spread = ((spread % 128 == 10 * row + spread // 128) & (row < 4)).astype(jnp.float32)
    by_column = lax.dot_general(
        heads8[...], spread, (((0,), (0,)), ((), ())), preferred_element_type=jnp.float32
    )
    for j in range(10):
        heads[128 * j : 128 * j + 128, :] = by_column[:, 128 * j : 128 * j + 128].astype(jnp.bfloat16)
    for layer in range(2):
        def kernel_of(p, q, layer=layer):
            at = (3 * p + q) * 128
            block = jnp.where(role[0] == layer, mine[at : at + 128, :], other[at : at + 128, :])
            return block.astype(jnp.bfloat16)

        def store(block, value, layer=layer):
            pairs[layer, block * 128 : (block + 1) * 128, :] = value

        pair_kernels(kernel_of, store)
    clear_border(middle)
    clear_border(boards)
    fetch.wait()

    def run_layer(layer, source, emit):
        def step(at, carry):
            first = at * count
            pre = conv_pairs(source, pairs[layer], first, count)
            for parity in range(2):
                part = pre[:, parity * 128 : (parity + 1) * 128].reshape(count, 5, games, 128)
                before = residual(source, first, count, parity).astype(jnp.float32)
                emit(first, parity, (before + jnp.maximum(part, 0.0)).astype(jnp.bfloat16))
            return carry

        lax.fori_loop(0, 10 // count, step, 0, unroll=unroll)

    run_layer(0, boards, lambda first, parity, value: put_cells(middle, first, count, parity, value))

    def to_last(first, parity, value):
        last[pl.ds(first, count), :, parity] = value

    run_layer(1, middle, to_last)
    cells = [last[:, j // 2, j % 2].reshape(-1, 128) for j in range(10)]
    logits = jnp.dot(jnp.concatenate(cells, axis=1), heads[...], preferred_element_type=jnp.float32)
    logits = logits.reshape(10, games, 128)
    lanes = lax.broadcasted_iota(jnp.int32, (games, 128), 1)
    moves = []
    total = jnp.zeros((games, 1), jnp.float32)
    for d in range(4):
        gathered = jnp.zeros((games, 128), jnp.float32)
        for i in range(10):
            turned = pltpu.roll(logits[i], (10 * i - 10 * d) % 128, 1)
            gathered = jnp.where((lanes >= 10 * i) & (lanes < 10 * i + 10), turned, gathered)
        moves.append(gathered)
        total = total + jnp.sum(
            jnp.where(lanes < 100, jnp.exp(gathered), 0.0), axis=1, keepdims=True
        )
    log_total = jnp.log(total)
    for d in range(4):
        out[:, 100 * d : 100 * d + 100] = (moves[d] - log_total)[:, :100]


def act(role, mine, other, boards, heads8, count=2, unroll=1):
    games = boards.shape[2]
    vmem = pl.BlockSpec(memory_space=pltpu.VMEM)
    return pl.pallas_call(
        functools.partial(actor_kernel, count, unroll),
        out_shape=jax.ShapeDtypeStruct((games, 400), jnp.float32),
        in_specs=[
            pl.BlockSpec(memory_space=pltpu.SMEM), vmem, vmem, pl.BlockSpec(memory_space=pltpu.HBM), vmem
        ],
        out_specs=vmem,
        scratch_shapes=[
            pltpu.VMEM((12, 6, 2, games, 128), jnp.bfloat16),
            pltpu.VMEM((2, 1536, 256), jnp.bfloat16),
            pltpu.VMEM((12, 6, 2, games, 128), jnp.bfloat16),
            pltpu.VMEM((10, 5, 2, games, 128), jnp.bfloat16),
            pltpu.VMEM((1280, 128), jnp.bfloat16),
            pltpu.SemaphoreType.DMA,
        ],
        compiler_params=pltpu.CompilerParams(vmem_limit_bytes=32 * 1024 * 1024),
        cost_estimate=pl.CostEstimate(
            flops=8 * 10**9, bytes_accessed=4 * 10**6, transcendentals=30000
        ),
        name="act",
    )(role, mine, other, boards, heads8)


def column_of(row):
    size = row.shape[1]
    across = lax.broadcasted_iota(jnp.int32, (size, size), 1)
    down = lax.broadcasted_iota(jnp.int32, (size, size), 0)
    spread = jnp.broadcast_to(row, (size, size))
    return jnp.sum(jnp.where(across == down, spread, jnp.zeros_like(spread)), axis=1, keepdims=True)


def later(x, reach):
    return jnp.concatenate([x[reach:], jnp.zeros((reach, x.shape[1]), x.dtype)], axis=0)


def learner_kernel(
    count, role, length, boards_in, actions_in, behaviour_in, regular_in, rewards_in, weights_in,
    heads8, grad,
    boards, weights, actions, behaviour, regular, rewards, pairs, back_pairs, middle, last, masks,
    slope, done,
):
    slots = boards.shape[3]
    moves = [
        (weights_in.at[0:ROWS], weights.at[0:ROWS]),
        (boards_in, inner_cells(boards)),
        (weights_in.at[ROWS : 2 * ROWS], weights.at[ROWS : 2 * ROWS]),
        (actions_in, actions),
        (behaviour_in, behaviour),
        (regular_in, regular),
        (rewards_in, rewards),
    ]
    copies = [pltpu.make_async_copy(a, b, done.at[k]) for k, (a, b) in enumerate(moves)]
    for copy in copies:
        copy.start()
    eight = heads8[...].astype(jnp.bfloat16).astype(jnp.float32)
    heads_t = jnp.concatenate(
        [eight, eight, eight, jnp.zeros((104, 128), jnp.float32)], axis=0
    ).astype(jnp.bfloat16)
    clear_border(boards)
    copies[0].wait()

    for layer in range(2):
        if layer == 1:
            copies[2].wait()

        def kernel_of(p, q, layer=layer):
            at = layer * ROWS + (3 * p + q) * 128
            return weights[at : at + 128, :].astype(jnp.bfloat16)

        def store(block, value, layer=layer):
            pairs[layer, block * 128 : (block + 1) * 128, :] = value

        pair_kernels(kernel_of, store)
    clear_border(middle)
    clear_border(slope)
    copies[1].wait()

    def run_layer(layer, source, emit):
        for first in range(0, 10, count):
            pre = conv_pairs(source, pairs[layer], first, count)
            for parity in range(2):
                part = pre[:, parity * 128 : (parity + 1) * 128].reshape(count, 5, slots, 128)
                before = residual(source, first, count, parity).astype(jnp.float32)
                emit(first, parity, (before + jnp.maximum(part, 0.0)).astype(jnp.bfloat16))
                masks[layer, first : first + count, :, parity] = (part > 0).astype(jnp.bfloat16)

    run_layer(0, boards, lambda first, parity, value: put_cells(middle, first, count, parity, value))

    def to_last(first, parity, value):
        last[pl.ds(first, count), :, parity] = value

    run_layer(1, middle, to_last)

    for copy in copies[3:]:
        copy.wait()

    scores = lax.dot_general(
        last[...].reshape(-1, 128), heads_t, (((1,), (1,)), ((), ())),
        preferred_element_type=jnp.float32,
    ).reshape(100, slots, 128)
    lane = lax.broadcasted_iota(jnp.int32, (slots, 128), 1)
    weights_sum = jnp.sum(jnp.where(lane < 4, jnp.exp(scores), 0.0), axis=0)
    log_total = jnp.log(jnp.sum(weights_sum, axis=1, keepdims=True))
    action = column_of(actions[...])
    direction = action // 100
    cell = action - 100 * direction
    cells = lax.broadcasted_iota(jnp.int32, (100, slots, 128), 0)
    taken = (cells == cell[None]) & (lane % 8 == direction)[None]
    picked = jnp.sum(
        jnp.sum(jnp.where(taken & (lane < 4)[None], scores, 0.0), axis=0), axis=1, keepdims=True
    )
    value_sum = jnp.sum(scores, axis=0)
    value = jnp.tanh(
        jnp.sum(jnp.where(lane == 4, value_sum, 0.0), axis=1, keepdims=True) / 100.0
    )
    log_policy = picked - log_total

    positions = lax.broadcasted_iota(jnp.int32, (slots, 1), 0)
    live = (positions < length[0]).astype(jnp.float32)
    next_live = (positions + 1 < length[0]).astype(jnp.float32)
    ratio = jnp.minimum(1.0, jnp.exp(log_policy - column_of(behaviour[...])))
    shaped = column_of(rewards[...]) - ETA * (log_policy - column_of(regular[...]))
    next_values = later(value, 1) * next_live
    correction = live * ratio * (shaped + next_values - value)
    decay = live * ratio
    reach = 1
    while reach < slots:
        correction = correction + decay * later(correction, reach)
        decay = decay * later(decay, reach)
        reach *= 2
    targets = value + correction
    next_targets = later(targets, 1) * next_live
    policy_grad = -live * ratio * (shaped + next_targets - value)
    value_grad = -live * (targets - value)

    value_cell = value_grad * (1.0 - value * value) / 100.0
    by_policy = policy_grad[None] * (taken.astype(jnp.float32) - jnp.exp(scores - log_total[None]))
    in_policy = (lane % 8 < 4) & (lane < 24)
    in_value = (lane % 8 == 4) & (lane < 24)
    by_score = jnp.where(
        in_policy[None], by_policy, jnp.where(in_value, value_cell, 0.0)[None]
    )
    high = by_score.astype(jnp.bfloat16)
    rest = by_score - high.astype(jnp.float32)
    mid = rest.astype(jnp.bfloat16)
    low = rest - mid.astype(jnp.float32)
    parts = jnp.where(
        (lane < 8)[None],
        high.astype(jnp.float32),
        jnp.where((lane < 16)[None], mid.astype(jnp.float32), low),
    ).astype(jnp.bfloat16)
    out_grad = jnp.dot(
        parts.reshape(-1, 128), heads_t, preferred_element_type=jnp.float32
    )
    act_grad = (out_grad * masks[1].reshape(-1, 128).astype(jnp.float32)).astype(jnp.bfloat16)

    def kernel_gradients(source, act_grad):
        turned = act_grad.T
        windows = []
        for p in range(3):
            for q in range(3):
                cols = [source[p : p + 10, (j + q) // 2, (j + q) % 2] for j in range(10)]
                windows.append(jnp.stack(cols, axis=1).reshape(-1, 128))
        for offset in range(9):
            block = jnp.dot(turned, windows[offset], preferred_element_type=jnp.float32)
            grad[offset * 128 : (offset + 1) * 128, :] = block.T

    @pl.when(role[0] == 1)
    def _():
        kernel_gradients(middle, act_grad)

    @pl.when(role[0] == 0)
    def _():
        def kernel_of(p, q):
            at = ROWS + (8 - (3 * p + q)) * 128
            return weights[at : at + 128, :].T.astype(jnp.bfloat16)

        def store(block, value):
            back_pairs[block * 128 : (block + 1) * 128, :] = value

        pair_kernels(kernel_of, store)
        act_cells = act_grad.reshape(10, 5, 2, slots, 128)
        put_cells(slope, 0, 10, 0, act_cells[:, :, 0])
        put_cells(slope, 0, 10, 1, act_cells[:, :, 1])
        out_cells = out_grad.reshape(10, 5, 2, slots, 128)
        for first in range(0, 10, count):
            back = conv_pairs(slope, back_pairs[...], first, count)
            for parity in range(2):
                part = back[:, parity * 128 : (parity + 1) * 128].reshape(count, 5, slots, 128)
                total = out_cells[first : first + count, :, parity] + part
                gate = masks[0, first : first + count, :, parity].astype(jnp.float32)
                last[pl.ds(first, count), :, parity] = (total * gate).astype(jnp.bfloat16)
        kernel_gradients(boards, last[...].reshape(-1, 128))


def head_rows(policy_head, value_head):
    five = jnp.concatenate([policy_head.T, value_head[None]]).astype(jnp.float32)
    return jnp.pad(five, ((0, 3), (0, 0)))


def learn(role, length, boards, actions, behaviour, regular, rewards, weights, heads8, count=5):
    slots = boards.shape[2]
    smem = pl.BlockSpec(memory_space=pltpu.SMEM)
    vmem = pl.BlockSpec(memory_space=pltpu.VMEM)
    anywhere = pl.BlockSpec(memory_space=pltpu.HBM)
    cells = (10, 5, 2, slots, 128)
    around = (12, 6, 2, slots, 128)
    return pl.pallas_call(
        functools.partial(learner_kernel, count),
        out_shape=jax.ShapeDtypeStruct((ROWS, 128), jnp.float32),
        in_specs=[smem, smem] + [anywhere] * 6 + [vmem],
        out_specs=vmem,
        scratch_shapes=[
            pltpu.VMEM(around, jnp.bfloat16),
            pltpu.VMEM((2 * ROWS, 128), jnp.float32),
            pltpu.VMEM((1, slots), jnp.int32),
            pltpu.VMEM((1, slots), jnp.float32),
            pltpu.VMEM((1, slots), jnp.float32),
            pltpu.VMEM((1, slots), jnp.float32),
            pltpu.VMEM((2, 1536, 256), jnp.bfloat16),
            pltpu.VMEM((1536, 256), jnp.bfloat16),
            pltpu.VMEM(around, jnp.bfloat16),
            pltpu.VMEM(cells, jnp.bfloat16),
            pltpu.VMEM((2,) + cells, jnp.bfloat16),
            pltpu.VMEM(around, jnp.bfloat16),
            pltpu.SemaphoreType.DMA((7,)),
        ],
        compiler_params=pltpu.CompilerParams(vmem_limit_bytes=60 * 1024 * 1024),
        cost_estimate=pl.CostEstimate(
            flops=4 * 10**9, bytes_accessed=3 * 10**6, transcendentals=10000
        ),
        name="learn",
    )(role, length, boards, actions, behaviour, regular, rewards, weights, heads8)


PLANES = [[LINE * k + z for k in range(LINE * LINE)] for z in range(LINE)]


def shifted_z(x, step):
    pairs = [(d, d - d % LINE + (d + step) % LINE) for d in range(LINE**3)]
    return lax.ppermute(x, "dp", pairs)


def line_total(x):
    return (x + shifted_z(x, 2)) + (shifted_z(x, 1) + shifted_z(x, 3))


def plane_exchange(x):
    return lax.all_to_all(x, "dp", 0, 0, axis_index_groups=PLANES)


def plane_gather(x):
    return plane_exchange(jnp.broadcast_to(x, (LINE * LINE,) + x.shape))


def role_swap(x):
    return lax.ppermute(x, "role", [(0, 1), (1, 0)])


def share_moments(first_moment, second_moment, z):
    both = jnp.stack([first_moment, second_moment])
    got = []
    for k in range(2):
        pairs = []
        for role in range(2):
            for d in range(LINE**3):
                z_of = d % LINE
                owner = 32 * role + 2 * (d // LINE) + (k + z_of) % 2
                pairs.append(((z_of // 2) * LINE**3 + owner, role * LINE**3 + d))
        got.append(lax.ppermute(both, ("role", "dp"), pairs))
    even = z % 2 == 0
    low = jnp.where(even, got[0], got[1])
    high = jnp.where(even, got[1], got[0])
    return jnp.concatenate([low, high], axis=1)


def body(
    board_now,
    traj_boards,
    actions,
    lengths,
    behaviour,
    regular,
    rewards,
    torso,
    policy_head,
    value_head,
    first_moment,
    second_moment,
):
    role = lax.axis_index("role")
    dp = lax.axis_index("dp")
    role_box = jnp.full((1,), role, jnp.int32)
    heads8 = head_rows(policy_head, value_head)
    moments = share_moments(first_moment, second_moment, dp % LINE)
    gradient = learn(
        role_box,
        lengths,
        by_cell(traj_boards[0]),
        actions,
        behaviour,
        regular,
        rewards,
        torso,
        heads8,
    )
    moments = lax.all_gather(moments, "dp", axis_index_groups=PLANES)
    share = jnp.sum(plane_exchange(gradient.reshape(LINE * LINE, SHARE, 128)), axis=0)
    share = line_total(share)
    squares = jnp.sum(share * share, axis=0, keepdims=True)
    squares = squares + role_swap(squares)
    gathered = plane_gather(jnp.concatenate([share, jnp.pad(squares, ((0, 7), (0, 0)))]))
    summed = gathered[:, :SHARE].reshape(ROWS, 128)
    square_sum = jnp.sum(gathered[:, SHARE])
    factor = jnp.minimum(1.0, jnp.sqrt(float(torso.size)) / jnp.sqrt(square_sum + NORM_EPS))
    clipped = summed * factor
    first = moments[:, 0].reshape(ROWS, 128)
    second = moments[:, 1].reshape(ROWS, 128)
    moment_one = BETA_ONE * first + (1.0 - BETA_ONE) * clipped
    moment_two = BETA_TWO * second + (1.0 - BETA_TWO) * clipped * clipped
    old = lax.dynamic_slice_in_dim(torso, role * ROWS, ROWS, 0)
    mine = old - LEARN_RATE * moment_one / (jnp.sqrt(moment_two) + ADAM_EPS)
    other = role_swap(mine)
    move_logp = act(role_box, mine, other, by_cell(board_now), heads8)
    out_rows = first_moment.shape[0]
    layer = dp // (LINE**3 // 2)
    at = dp % (LINE**3 // 2) * out_rows
    new_share = jnp.where(
        role == layer,
        lax.dynamic_slice_in_dim(mine, at, out_rows, 0),
        lax.dynamic_slice_in_dim(other, at, out_rows, 0),
    )
    return (new_share, move_logp)


def solution(mesh):
    return jax.shard_map(
        body,
        mesh=mesh,
        in_specs=(
            P("dp", None, None, None),
            P("dp", None, None, None, None),
            P("dp", None),
            P("dp"),
            P("dp", None),
            P("dp", None),
            P("dp", None),
            P(),
            P(),
            P(),
            P("dp", None),
            P("dp", None),
        ),
        out_specs=(P("dp", None), P("dp", None)),
        check_vma=False,
    )
```

```python
import functools

import jax
import jax.numpy as jnp
from jax import lax
from jax.experimental import pallas as pl
from jax.experimental.pallas import tpu as pltpu
from jax.sharding import PartitionSpec as P

ETA = 0.2
LEARN_RATE = 0.03
BETA_ONE = 0.9
BETA_TWO = 0.999
ADAM_EPS = 1e-08
NORM_EPS = 1e-12
ROWS = 1152
LINE = 4
SHARE = ROWS // (LINE * LINE)


def by_cell(boards):
    return jnp.transpose(boards, (1, 2, 0, 3))


def inner_cells(ref):
    return ref.reshape((12, 12) + ref.shape[3:]).at[1:11, 1:11]


def clear_border(ref):
    zero_row = jnp.zeros(ref.shape[1:], ref.dtype)
    ref[0] = zero_row
    ref[11] = zero_row
    zero_col = jnp.zeros((12,) + ref.shape[3:], ref.dtype)
    ref[:, 0, 0] = zero_col
    ref[:, 5, 1] = zero_col


def pair_kernels(kernel_of, store):
    nothing = jnp.zeros((128, 128), jnp.bfloat16)
    for p in range(3):
        row = [kernel_of(p, q) for q in range(3)]
        for q in range(4):
            left = row[q] if q < 3 else nothing
            right = row[q - 1] if q > 0 else nothing
            store(4 * p + q, jnp.concatenate([left, right], axis=1))


def conv_pairs(source, pair_weights, first, count):
    windows = []
    for p in range(3):
        for q in range(4):
            window = source[pl.ds(first + p, count), q // 2 : q // 2 + 5, q % 2]
            windows.append(window.reshape(-1, 128))
    return jnp.dot(
        jnp.concatenate(windows, axis=1), pair_weights, preferred_element_type=jnp.float32
    )


def residual(source, first, count, parity):
    if parity == 0:
        window = source[pl.ds(first + 1, count), 0:5, 1]
    else:
        window = source[pl.ds(first + 1, count), 1:6, 0]
    return window


def put_cells(target, first, count, parity, value):
    if parity == 0:
        target[pl.ds(first + 1, count), 0:5, 1] = value
    else:
        target[pl.ds(first + 1, count), 1:6, 0] = value


def actor_kernel(
    count, unroll, role, mine, other, boards_in, heads8, out, boards, pairs, middle, last, heads, done
):
    games = boards.shape[3]
    half = pl.ds(pl.multiple_of(role[0] * games, games), games)
    fetch = pltpu.make_async_copy(boards_in.at[:, :, half], inner_cells(boards), done)
    fetch.start()
    spread = lax.broadcasted_iota(jnp.int32, (8, 1280), 1)
    row = lax.broadcasted_iota(jnp.int32, (8, 1280), 0)
    spread = ((spread % 128 == 10 * row + spread // 128) & (row < 4)).astype(jnp.float32)
    by_column = lax.dot_general(
        heads8[...], spread, (((0,), (0,)), ((), ())), preferred_element_type=jnp.float32
    )
    for j in range(10):
        heads[128 * j : 128 * j + 128, :] = by_column[:, 128 * j : 128 * j + 128].astype(jnp.bfloat16)
    for layer in range(2):
        def kernel_of(p, q, layer=layer):
            at = (3 * p + q) * 128
            block = jnp.where(role[0] == layer, mine[at : at + 128, :], other[at : at + 128, :])
            return block.astype(jnp.bfloat16)

        def store(block, value, layer=layer):
            pairs[layer, block * 128 : (block + 1) * 128, :] = value

        pair_kernels(kernel_of, store)
    clear_border(middle)
    clear_border(boards)
    fetch.wait()

    def run_layer(layer, source, emit):
        def step(at, carry):
            first = at * count
            pre = conv_pairs(source, pairs[layer], first, count)
            for parity in range(2):
                part = pre[:, parity * 128 : (parity + 1) * 128].reshape(count, 5, games, 128)
                before = residual(source, first, count, parity).astype(jnp.float32)
                emit(first, parity, (before + jnp.maximum(part, 0.0)).astype(jnp.bfloat16))
            return carry

        lax.fori_loop(0, 10 // count, step, 0, unroll=unroll)

    run_layer(0, boards, lambda first, parity, value: put_cells(middle, first, count, parity, value))

    def to_last(first, parity, value):
        last[pl.ds(first, count), :, parity] = value

    run_layer(1, middle, to_last)
    cells = [last[:, j // 2, j % 2].reshape(-1, 128) for j in range(10)]
    logits = jnp.dot(jnp.concatenate(cells, axis=1), heads[...], preferred_element_type=jnp.float32)
    logits = logits.reshape(10, games, 128)
    lanes = lax.broadcasted_iota(jnp.int32, (games, 128), 1)
    moves = []
    total = jnp.zeros((games, 1), jnp.float32)
    for d in range(4):
        gathered = jnp.zeros((games, 128), jnp.float32)
        for i in range(10):
            turned = pltpu.roll(logits[i], (10 * i - 10 * d) % 128, 1)
            gathered = jnp.where((lanes >= 10 * i) & (lanes < 10 * i + 10), turned, gathered)
        moves.append(gathered)
        total = total + jnp.sum(
            jnp.where(lanes < 100, jnp.exp(gathered), 0.0), axis=1, keepdims=True
        )
    log_total = jnp.log(total)
    for d in range(4):
        out[:, 100 * d : 100 * d + 100] = (moves[d] - log_total)[:, :100]


def act(role, mine, other, boards, heads8, count=2, unroll=1):
    games = boards.shape[2] // 2
    vmem = pl.BlockSpec(memory_space=pltpu.VMEM)
    return pl.pallas_call(
        functools.partial(actor_kernel, count, unroll),
        out_shape=jax.ShapeDtypeStruct((games, 400), jnp.float32),
        in_specs=[
            pl.BlockSpec(memory_space=pltpu.SMEM), vmem, vmem, pl.BlockSpec(memory_space=pltpu.HBM), vmem
        ],
        out_specs=vmem,
        scratch_shapes=[
            pltpu.VMEM((12, 6, 2, games, 128), jnp.bfloat16),
            pltpu.VMEM((2, 1536, 256), jnp.bfloat16),
            pltpu.VMEM((12, 6, 2, games, 128), jnp.bfloat16),
            pltpu.VMEM((10, 5, 2, games, 128), jnp.bfloat16),
            pltpu.VMEM((1280, 128), jnp.bfloat16),
            pltpu.SemaphoreType.DMA,
        ],
        compiler_params=pltpu.CompilerParams(vmem_limit_bytes=32 * 1024 * 1024),
        cost_estimate=pl.CostEstimate(
            flops=8 * 10**9, bytes_accessed=4 * 10**6, transcendentals=30000
        ),
        name="act",
    )(role, mine, other, boards, heads8)


def column_of(row):
    size = row.shape[1]
    across = lax.broadcasted_iota(jnp.int32, (size, size), 1)
    down = lax.broadcasted_iota(jnp.int32, (size, size), 0)
    spread = jnp.broadcast_to(row, (size, size))
    return jnp.sum(jnp.where(across == down, spread, jnp.zeros_like(spread)), axis=1, keepdims=True)


def later(x, reach):
    return jnp.concatenate([x[reach:], jnp.zeros((reach, x.shape[1]), x.dtype)], axis=0)


def learner_kernel(
    count, role, length, boards_in, actions_in, behaviour_in, regular_in, rewards_in, weights_in,
    heads8, grad,
    boards, weights, actions, behaviour, regular, rewards, pairs, back_pairs, middle, last, masks,
    slope, done,
):
    slots = boards.shape[3]
    moves = [
        (weights_in.at[0:ROWS], weights.at[0:ROWS]),
        (boards_in, inner_cells(boards)),
        (weights_in.at[ROWS : 2 * ROWS], weights.at[ROWS : 2 * ROWS]),
        (actions_in, actions),
        (behaviour_in, behaviour),
        (regular_in, regular),
        (rewards_in, rewards),
    ]
    copies = [pltpu.make_async_copy(a, b, done.at[k]) for k, (a, b) in enumerate(moves)]
    for copy in copies:
        copy.start()
    eight = heads8[...].astype(jnp.bfloat16).astype(jnp.float32)
    heads_t = jnp.concatenate(
        [eight, eight, eight, jnp.zeros((104, 128), jnp.float32)], axis=0
    ).astype(jnp.bfloat16)
    clear_border(boards)
    copies[0].wait()

    for layer in range(2):
        if layer == 1:
            copies[2].wait()

        def kernel_of(p, q, layer=layer):
            at = layer * ROWS + (3 * p + q) * 128
            return weights[at : at + 128, :].astype(jnp.bfloat16)

        def store(block, value, layer=layer):
            pairs[layer, block * 128 : (block + 1) * 128, :] = value

        pair_kernels(kernel_of, store)
    clear_border(middle)
    clear_border(slope)
    copies[1].wait()

    def run_layer(layer, source, emit):
        for first in range(0, 10, count):
            pre = conv_pairs(source, pairs[layer], first, count)
            for parity in range(2):
                part = pre[:, parity * 128 : (parity + 1) * 128].reshape(count, 5, slots, 128)
                before = residual(source, first, count, parity).astype(jnp.float32)
                emit(first, parity, (before + jnp.maximum(part, 0.0)).astype(jnp.bfloat16))
                masks[layer, first : first + count, :, parity] = (part > 0).astype(jnp.bfloat16)

    run_layer(0, boards, lambda first, parity, value: put_cells(middle, first, count, parity, value))

    def to_last(first, parity, value):
        last[pl.ds(first, count), :, parity] = value

    run_layer(1, middle, to_last)

    for copy in copies[3:]:
        copy.wait()

    scores = lax.dot_general(
        last[...].reshape(-1, 128), heads_t, (((1,), (1,)), ((), ())),
        preferred_element_type=jnp.float32,
    ).reshape(100, slots, 128)
    lane = lax.broadcasted_iota(jnp.int32, (slots, 128), 1)
    weights_sum = jnp.sum(jnp.where(lane < 4, jnp.exp(scores), 0.0), axis=0)
    log_total = jnp.log(jnp.sum(weights_sum, axis=1, keepdims=True))
    action = column_of(actions[...])
    direction = action // 100
    cell = action - 100 * direction
    cells = lax.broadcasted_iota(jnp.int32, (100, slots, 128), 0)
    taken = (cells == cell[None]) & (lane % 8 == direction)[None]
    picked = jnp.sum(
        jnp.sum(jnp.where(taken & (lane < 4)[None], scores, 0.0), axis=0), axis=1, keepdims=True
    )
    value_sum = jnp.sum(scores, axis=0)
    value = jnp.tanh(
        jnp.sum(jnp.where(lane == 4, value_sum, 0.0), axis=1, keepdims=True) / 100.0
    )
    log_policy = picked - log_total

    positions = lax.broadcasted_iota(jnp.int32, (slots, 1), 0)
    live = (positions < length[0]).astype(jnp.float32)
    next_live = (positions + 1 < length[0]).astype(jnp.float32)
    ratio = jnp.minimum(1.0, jnp.exp(log_policy - column_of(behaviour[...])))
    shaped = column_of(rewards[...]) - ETA * (log_policy - column_of(regular[...]))
    next_values = later(value, 1) * next_live
    correction = live * ratio * (shaped + next_values - value)
    decay = live * ratio
    reach = 1
    while reach < slots:
        correction = correction + decay * later(correction, reach)
        decay = decay * later(decay, reach)
        reach *= 2
    targets = value + correction
    next_targets = later(targets, 1) * next_live
    policy_grad = -live * ratio * (shaped + next_targets - value)
    value_grad = -live * (targets - value)

    value_cell = value_grad * (1.0 - value * value) / 100.0
    by_policy = policy_grad[None] * (taken.astype(jnp.float32) - jnp.exp(scores - log_total[None]))
    in_policy = (lane % 8 < 4) & (lane < 24)
    in_value = (lane % 8 == 4) & (lane < 24)
    by_score = jnp.where(
        in_policy[None], by_policy, jnp.where(in_value, value_cell, 0.0)[None]
    )
    high = by_score.astype(jnp.bfloat16)
    rest = by_score - high.astype(jnp.float32)
    mid = rest.astype(jnp.bfloat16)
    low = rest - mid.astype(jnp.float32)
    parts = jnp.where(
        (lane < 8)[None],
        high.astype(jnp.float32),
        jnp.where((lane < 16)[None], mid.astype(jnp.float32), low),
    ).astype(jnp.bfloat16)
    out_grad = jnp.dot(
        parts.reshape(-1, 128), heads_t, preferred_element_type=jnp.float32
    )
    act_grad = (out_grad * masks[1].reshape(-1, 128).astype(jnp.float32)).astype(jnp.bfloat16)

    def kernel_gradients(source, act_grad):
        turned = act_grad.T
        windows = []
        for p in range(3):
            for q in range(3):
                cols = [source[p : p + 10, (j + q) // 2, (j + q) % 2] for j in range(10)]
                windows.append(jnp.stack(cols, axis=1).reshape(-1, 128))
        for offset in range(9):
            block = jnp.dot(turned, windows[offset], preferred_element_type=jnp.float32)
            grad[offset * 128 : (offset + 1) * 128, :] = block.T

    @pl.when(role[0] == 1)
    def _():
        kernel_gradients(middle, act_grad)

    @pl.when(role[0] == 0)
    def _():
        def kernel_of(p, q):
            at = ROWS + (8 - (3 * p + q)) * 128
            return weights[at : at + 128, :].T.astype(jnp.bfloat16)

        def store(block, value):
            back_pairs[block * 128 : (block + 1) * 128, :] = value

        pair_kernels(kernel_of, store)
        act_cells = act_grad.reshape(10, 5, 2, slots, 128)
        put_cells(slope, 0, 10, 0, act_cells[:, :, 0])
        put_cells(slope, 0, 10, 1, act_cells[:, :, 1])
        out_cells = out_grad.reshape(10, 5, 2, slots, 128)
        for first in range(0, 10, count):
            back = conv_pairs(slope, back_pairs[...], first, count)
            for parity in range(2):
                part = back[:, parity * 128 : (parity + 1) * 128].reshape(count, 5, slots, 128)
                total = out_cells[first : first + count, :, parity] + part
                gate = masks[0, first : first + count, :, parity].astype(jnp.float32)
                last[pl.ds(first, count), :, parity] = (total * gate).astype(jnp.bfloat16)
        kernel_gradients(boards, last[...].reshape(-1, 128))


def head_rows(policy_head, value_head):
    five = jnp.concatenate([policy_head.T, value_head[None]]).astype(jnp.float32)
    return jnp.pad(five, ((0, 3), (0, 0)))


def learn(role, length, boards, actions, behaviour, regular, rewards, weights, heads8, count=5):
    slots = boards.shape[2]
    smem = pl.BlockSpec(memory_space=pltpu.SMEM)
    vmem = pl.BlockSpec(memory_space=pltpu.VMEM)
    anywhere = pl.BlockSpec(memory_space=pltpu.HBM)
    cells = (10, 5, 2, slots, 128)
    around = (12, 6, 2, slots, 128)
    return pl.pallas_call(
        functools.partial(learner_kernel, count),
        out_shape=jax.ShapeDtypeStruct((ROWS, 128), jnp.float32),
        in_specs=[smem, smem] + [anywhere] * 6 + [vmem],
        out_specs=vmem,
        scratch_shapes=[
            pltpu.VMEM(around, jnp.bfloat16),
            pltpu.VMEM((2 * ROWS, 128), jnp.float32),
            pltpu.VMEM((1, slots), jnp.int32),
            pltpu.VMEM((1, slots), jnp.float32),
            pltpu.VMEM((1, slots), jnp.float32),
            pltpu.VMEM((1, slots), jnp.float32),
            pltpu.VMEM((2, 1536, 256), jnp.bfloat16),
            pltpu.VMEM((1536, 256), jnp.bfloat16),
            pltpu.VMEM(around, jnp.bfloat16),
            pltpu.VMEM(cells, jnp.bfloat16),
            pltpu.VMEM((2,) + cells, jnp.bfloat16),
            pltpu.VMEM(around, jnp.bfloat16),
            pltpu.SemaphoreType.DMA((7,)),
        ],
        compiler_params=pltpu.CompilerParams(vmem_limit_bytes=60 * 1024 * 1024),
        cost_estimate=pl.CostEstimate(
            flops=4 * 10**9, bytes_accessed=3 * 10**6, transcendentals=10000
        ),
        name="learn",
    )(role, length, boards, actions, behaviour, regular, rewards, weights, heads8)


PLANES = [[LINE * k + z for k in range(LINE * LINE)] for z in range(LINE)]


def shifted(x, axis, step):
    stride = {"y": LINE * LINE, "x": LINE, "z": 1}[axis]
    pairs = []
    for d in range(LINE**3):
        at = d // stride % LINE
        pairs.append((d, d + ((at + step) % LINE - at) * stride))
    return lax.ppermute(x, "dp", pairs)


def line_total(x, axis):
    return (x + shifted(x, axis, 2)) + (shifted(x, axis, 1) + shifted(x, axis, 3))


def plane_exchange(x):
    return lax.all_to_all(x, "dp", 0, 0, axis_index_groups=PLANES)


def plane_gather(x):
    return plane_exchange(jnp.broadcast_to(x, (LINE * LINE,) + x.shape))


def role_swap(x):
    return lax.ppermute(x, "role", [(0, 1), (1, 0)])


def half_moments(first_moment, second_moment):
    pairs = []
    for role in range(2):
        for d in range(LINE**3):
            z = d % LINE
            owner = 32 * role + 2 * (d // LINE) + z % 2
            pairs.append(((z // 2) * LINE**3 + owner, role * LINE**3 + d))
    both = jnp.concatenate([first_moment, second_moment])
    return lax.ppermute(both, ("role", "dp"), pairs)


def line_exchange(share, half, z):
    near = shifted(jnp.concatenate([share, half]), "z", 1)
    total = (share + shifted(share, "z", 2)) + (near[:SHARE] + shifted(share, "z", 3))
    rows = SHARE // 2
    low = jnp.where(z % 2 == 0, half, near[SHARE:])
    high = jnp.where(z % 2 == 0, near[SHARE:], half)
    return (
        total,
        jnp.concatenate([low[:rows], high[:rows]]),
        jnp.concatenate([low[rows:], high[rows:]]),
    )


def body(
    board_now,
    traj_boards,
    actions,
    lengths,
    behaviour,
    regular,
    rewards,
    torso,
    policy_head,
    value_head,
    first_moment,
    second_moment,
):
    role = lax.axis_index("role")
    dp = lax.axis_index("dp")
    role_box = jnp.full((1,), role, jnp.int32)
    heads8 = head_rows(policy_head, value_head)
    half = half_moments(first_moment, second_moment)
    gradient = learn(
        role_box,
        lengths,
        by_cell(traj_boards[0]),
        actions,
        behaviour,
        regular,
        rewards,
        torso,
        heads8,
    )
    share = jnp.sum(plane_exchange(gradient.reshape(LINE * LINE, SHARE, 128)), axis=0)
    share, first, second = line_exchange(share, half, dp % LINE)
    squares = jnp.sum(share * share, axis=0, keepdims=True)
    squares = squares + role_swap(squares)
    squares = line_total(line_total(squares, "x"), "y")
    square_sum = jnp.sum(squares)
    factor = jnp.minimum(1.0, jnp.sqrt(float(torso.size)) / jnp.sqrt(square_sum + NORM_EPS))
    clipped = share * factor
    moment_one = BETA_ONE * first + (1.0 - BETA_ONE) * clipped
    moment_two = BETA_TWO * second + (1.0 - BETA_TWO) * clipped * clipped
    old_share = lax.dynamic_slice_in_dim(torso, role * ROWS + dp // LINE * SHARE, SHARE, 0)
    weight_share = old_share - LEARN_RATE * moment_one / (jnp.sqrt(moment_two) + ADAM_EPS)
    mine = plane_gather(weight_share).reshape(ROWS, 128)
    other = role_swap(mine)
    here = act(role_box, mine, other, by_cell(board_now), heads8)
    there = role_swap(here)
    out_rows = first_moment.shape[0]
    layer = dp // (LINE**3 // 2)
    at = dp % (LINE**3 // 2) * out_rows
    new_share = jnp.where(
        role == layer,
        lax.dynamic_slice_in_dim(mine, at, out_rows, 0),
        lax.dynamic_slice_in_dim(other, at, out_rows, 0),
    )
    move_logp = jnp.concatenate([jnp.where(role == 0, here, there), jnp.where(role == 0, there, here)])
    return (new_share, move_logp)


def solution(mesh):
    return jax.shard_map(
        body,
        mesh=mesh,
        in_specs=(
            P("dp", None, None, None),
            P("dp", None, None, None, None),
            P("dp", None),
            P("dp"),
            P("dp", None),
            P("dp", None),
            P("dp", None),
            P(),
            P(),
            P(),
            P("dp", None),
            P("dp", None),
        ),
        out_specs=(P("dp", None), P("dp", None)),
        check_vma=False,
    )
```

```python
import functools

import jax
import jax.numpy as jnp
from jax import lax
from jax.experimental import pallas as pl
from jax.experimental.pallas import tpu as pltpu
from jax.sharding import PartitionSpec as P

ETA = 0.2
LEARN_RATE = 0.03
BETA_ONE = 0.9
BETA_TWO = 0.999
ADAM_EPS = 1e-08
NORM_EPS = 1e-12
ROWS = 1152
LINE = 4
SHARE = ROWS // (LINE * LINE)


def by_cell(boards):
    return jnp.transpose(boards, (1, 2, 0, 3))


def inner_cells(ref):
    return ref.reshape((12, 12) + ref.shape[3:]).at[1:11, 1:11]


def clear_border(ref):
    zero_row = jnp.zeros(ref.shape[1:], ref.dtype)
    ref[0] = zero_row
    ref[11] = zero_row
    zero_col = jnp.zeros((12,) + ref.shape[3:], ref.dtype)
    ref[:, 0, 0] = zero_col
    ref[:, 5, 1] = zero_col


def pair_kernels(kernel_of, store):
    nothing = jnp.zeros((128, 128), jnp.bfloat16)
    for p in range(3):
        row = [kernel_of(p, q) for q in range(3)]
        for q in range(4):
            left = row[q] if q < 3 else nothing
            right = row[q - 1] if q > 0 else nothing
            store(4 * p + q, jnp.concatenate([left, right], axis=1))


def conv_pairs(source, pair_weights, first, count):
    windows = []
    for p in range(3):
        for q in range(4):
            window = source[pl.ds(first + p, count), q // 2 : q // 2 + 5, q % 2]
            windows.append(window.reshape(-1, 128))
    return jnp.dot(
        jnp.concatenate(windows, axis=1), pair_weights, preferred_element_type=jnp.float32
    )


def residual(source, first, count, parity):
    if parity == 0:
        window = source[pl.ds(first + 1, count), 0:5, 1]
    else:
        window = source[pl.ds(first + 1, count), 1:6, 0]
    return window


def put_cells(target, first, count, parity, value):
    if parity == 0:
        target[pl.ds(first + 1, count), 0:5, 1] = value
    else:
        target[pl.ds(first + 1, count), 1:6, 0] = value


def actor_kernel(
    count, unroll, role, mine, other, boards_in, policy_t, out, boards, pairs, middle, last, heads, done
):
    games = boards.shape[3]
    half = pl.ds(pl.multiple_of(role[0] * games, games), games)
    fetch = pltpu.make_async_copy(boards_in.at[:, :, half], inner_cells(boards), done)
    fetch.start()
    spread = lax.broadcasted_iota(jnp.int32, (4, 1280), 1)
    row = lax.broadcasted_iota(jnp.int32, (4, 1280), 0)
    spread = (spread % 128 == 10 * row + spread // 128).astype(jnp.float32)
    by_column = lax.dot_general(
        policy_t[...], spread, (((0,), (0,)), ((), ())), preferred_element_type=jnp.float32
    )
    for j in range(10):
        heads[128 * j : 128 * j + 128, :] = by_column[:, 128 * j : 128 * j + 128].astype(jnp.bfloat16)
    for layer in range(2):
        def kernel_of(p, q, layer=layer):
            at = (3 * p + q) * 128
            block = jnp.where(role[0] == layer, mine[at : at + 128, :], other[at : at + 128, :])
            return block.astype(jnp.bfloat16)

        def store(block, value, layer=layer):
            pairs[layer, block * 128 : (block + 1) * 128, :] = value

        pair_kernels(kernel_of, store)
    clear_border(middle)
    clear_border(boards)
    fetch.wait()

    def run_layer(layer, source, emit):
        def step(at, carry):
            first = at * count
            pre = conv_pairs(source, pairs[layer], first, count)
            for parity in range(2):
                part = pre[:, parity * 128 : (parity + 1) * 128].reshape(count, 5, games, 128)
                before = residual(source, first, count, parity).astype(jnp.float32)
                emit(first, parity, (before + jnp.maximum(part, 0.0)).astype(jnp.bfloat16))
            return carry

        lax.fori_loop(0, 10 // count, step, 0, unroll=unroll)

    run_layer(0, boards, lambda first, parity, value: put_cells(middle, first, count, parity, value))

    def to_last(first, parity, value):
        last[pl.ds(first, count), :, parity] = value

    run_layer(1, middle, to_last)
    cells = [last[:, j // 2, j % 2].reshape(-1, 128) for j in range(10)]
    logits = jnp.dot(jnp.concatenate(cells, axis=1), heads[...], preferred_element_type=jnp.float32)
    logits = logits.reshape(10, games, 128)
    lanes = lax.broadcasted_iota(jnp.int32, (games, 128), 1)
    moves = []
    total = jnp.zeros((games, 1), jnp.float32)
    for d in range(4):
        gathered = jnp.zeros((games, 128), jnp.float32)
        for i in range(10):
            turned = pltpu.roll(logits[i], (10 * i - 10 * d) % 128, 1)
            gathered = jnp.where((lanes >= 10 * i) & (lanes < 10 * i + 10), turned, gathered)
        moves.append(gathered)
        total = total + jnp.sum(
            jnp.where(lanes < 100, jnp.exp(gathered), 0.0), axis=1, keepdims=True
        )
    log_total = jnp.log(total)
    for d in range(4):
        out[:, 100 * d : 100 * d + 100] = (moves[d] - log_total)[:, :100]


def act(role, mine, other, boards, policy_t, count=2, unroll=1):
    games = boards.shape[2] // 2
    vmem = pl.BlockSpec(memory_space=pltpu.VMEM)
    return pl.pallas_call(
        functools.partial(actor_kernel, count, unroll),
        out_shape=jax.ShapeDtypeStruct((games, 400), jnp.float32),
        in_specs=[
            pl.BlockSpec(memory_space=pltpu.SMEM), vmem, vmem, pl.BlockSpec(memory_space=pltpu.HBM), vmem
        ],
        out_specs=vmem,
        scratch_shapes=[
            pltpu.VMEM((12, 6, 2, games, 128), jnp.bfloat16),
            pltpu.VMEM((2, 1536, 256), jnp.bfloat16),
            pltpu.VMEM((12, 6, 2, games, 128), jnp.bfloat16),
            pltpu.VMEM((10, 5, 2, games, 128), jnp.bfloat16),
            pltpu.VMEM((1280, 128), jnp.bfloat16),
            pltpu.SemaphoreType.DMA,
        ],
        compiler_params=pltpu.CompilerParams(vmem_limit_bytes=32 * 1024 * 1024),
        cost_estimate=pl.CostEstimate(
            flops=8 * 10**9, bytes_accessed=4 * 10**6, transcendentals=30000
        ),
        name="act",
    )(role, mine, other, boards, policy_t)


def column_of(row):
    size = row.shape[1]
    across = lax.broadcasted_iota(jnp.int32, (size, size), 1)
    down = lax.broadcasted_iota(jnp.int32, (size, size), 0)
    spread = jnp.broadcast_to(row, (size, size))
    return jnp.sum(jnp.where(across == down, spread, jnp.zeros_like(spread)), axis=1, keepdims=True)


def later(x, reach):
    return jnp.concatenate([x[reach:], jnp.zeros((reach, x.shape[1]), x.dtype)], axis=0)


def learner_kernel(
    count, role, length, boards_in, actions_in, behaviour_in, regular_in, rewards_in, weights_in,
    policy_in, value_in, grad,
    boards, weights, actions, behaviour, regular, rewards, policy_t, value_t, pairs, back_pairs,
    middle, last, masks, slope, done,
):
    slots = boards.shape[3]
    moves = [
        (weights_in.at[0:ROWS], weights.at[0:ROWS]),
        (boards_in, inner_cells(boards)),
        (weights_in.at[ROWS : 2 * ROWS], weights.at[ROWS : 2 * ROWS]),
        (actions_in, actions),
        (behaviour_in, behaviour),
        (regular_in, regular),
        (rewards_in, rewards),
        (policy_in, policy_t),
        (value_in, value_t),
    ]
    copies = [pltpu.make_async_copy(a, b, done.at[k]) for k, (a, b) in enumerate(moves)]
    for copy in copies:
        copy.start()
    clear_border(boards)
    copies[0].wait()

    for layer in range(2):
        if layer == 1:
            copies[2].wait()

        def kernel_of(p, q, layer=layer):
            at = layer * ROWS + (3 * p + q) * 128
            return weights[at : at + 128, :].astype(jnp.bfloat16)

        def store(block, value, layer=layer):
            pairs[layer, block * 128 : (block + 1) * 128, :] = value

        pair_kernels(kernel_of, store)
    clear_border(middle)
    clear_border(slope)
    copies[1].wait()

    def run_layer(layer, source, emit):
        for first in range(0, 10, count):
            pre = conv_pairs(source, pairs[layer], first, count)
            for parity in range(2):
                part = pre[:, parity * 128 : (parity + 1) * 128].reshape(count, 5, slots, 128)
                before = residual(source, first, count, parity).astype(jnp.float32)
                emit(first, parity, (before + jnp.maximum(part, 0.0)).astype(jnp.bfloat16))
                masks[layer, first : first + count, :, parity] = (part > 0).astype(jnp.bfloat16)

    run_layer(0, boards, lambda first, parity, value: put_cells(middle, first, count, parity, value))

    def to_last(first, parity, value):
        last[pl.ds(first, count), :, parity] = value

    run_layer(1, middle, to_last)

    for copy in copies[3:]:
        copy.wait()

    eight = jnp.concatenate(
        [
            policy_t[...].astype(jnp.float32),
            value_t[...].astype(jnp.float32),
            jnp.zeros((3, 128), jnp.float32),
        ],
        axis=0,
    )
    heads_t = jnp.concatenate(
        [eight, eight, eight, jnp.zeros((104, 128), jnp.float32)], axis=0
    ).astype(jnp.bfloat16)

    scores = lax.dot_general(
        last[...].reshape(-1, 128), heads_t, (((1,), (1,)), ((), ())),
        preferred_element_type=jnp.float32,
    ).reshape(100, slots, 128)
    lane = lax.broadcasted_iota(jnp.int32, (slots, 128), 1)
    weights_sum = jnp.sum(jnp.where(lane < 4, jnp.exp(scores), 0.0), axis=0)
    log_total = jnp.log(jnp.sum(weights_sum, axis=1, keepdims=True))
    action = column_of(actions[...])
    direction = action // 100
    cell = action - 100 * direction
    cells = lax.broadcasted_iota(jnp.int32, (100, slots, 128), 0)
    taken = (cells == cell[None]) & (lane % 8 == direction)[None]
    picked = jnp.sum(
        jnp.sum(jnp.where(taken & (lane < 4)[None], scores, 0.0), axis=0), axis=1, keepdims=True
    )
    value_sum = jnp.sum(scores, axis=0)
    value = jnp.tanh(
        jnp.sum(jnp.where(lane == 4, value_sum, 0.0), axis=1, keepdims=True) / 100.0
    )
    log_policy = picked - log_total

    positions = lax.broadcasted_iota(jnp.int32, (slots, 1), 0)
    live = (positions < length[0]).astype(jnp.float32)
    next_live = (positions + 1 < length[0]).astype(jnp.float32)
    ratio = jnp.minimum(1.0, jnp.exp(log_policy - column_of(behaviour[...])))
    shaped = column_of(rewards[...]) - ETA * (log_policy - column_of(regular[...]))
    next_values = later(value, 1) * next_live
    correction = live * ratio * (shaped + next_values - value)
    decay = live * ratio
    reach = 1
    while reach < slots:
        correction = correction + decay * later(correction, reach)
        decay = decay * later(decay, reach)
        reach *= 2
    targets = value + correction
    next_targets = later(targets, 1) * next_live
    policy_grad = -live * ratio * (shaped + next_targets - value)
    value_grad = -live * (targets - value)

    value_cell = value_grad * (1.0 - value * value) / 100.0
    by_policy = policy_grad[None] * (taken.astype(jnp.float32) - jnp.exp(scores - log_total[None]))
    in_policy = (lane % 8 < 4) & (lane < 24)
    in_value = (lane % 8 == 4) & (lane < 24)
    by_score = jnp.where(
        in_policy[None], by_policy, jnp.where(in_value, value_cell, 0.0)[None]
    )
    high = by_score.astype(jnp.bfloat16)
    rest = by_score - high.astype(jnp.float32)
    mid = rest.astype(jnp.bfloat16)
    low = rest - mid.astype(jnp.float32)
    parts = jnp.where(
        (lane < 8)[None],
        high.astype(jnp.float32),
        jnp.where((lane < 16)[None], mid.astype(jnp.float32), low),
    ).astype(jnp.bfloat16)
    out_grad = jnp.dot(
        parts.reshape(-1, 128), heads_t, preferred_element_type=jnp.float32
    )
    act_grad = (out_grad * masks[1].reshape(-1, 128).astype(jnp.float32)).astype(jnp.bfloat16)

    def kernel_gradients(source, act_grad):
        turned = act_grad.T
        windows = []
        for p in range(3):
            for q in range(3):
                cols = [source[p : p + 10, (j + q) // 2, (j + q) % 2] for j in range(10)]
                windows.append(jnp.stack(cols, axis=1).reshape(-1, 128))
        for offset in range(9):
            block = jnp.dot(turned, windows[offset], preferred_element_type=jnp.float32)
            grad[offset * 128 : (offset + 1) * 128, :] = block.T

    @pl.when(role[0] == 1)
    def _():
        kernel_gradients(middle, act_grad)

    @pl.when(role[0] == 0)
    def _():
        def kernel_of(p, q):
            at = ROWS + (8 - (3 * p + q)) * 128
            return weights[at : at + 128, :].T.astype(jnp.bfloat16)

        def store(block, value):
            back_pairs[block * 128 : (block + 1) * 128, :] = value

        pair_kernels(kernel_of, store)
        act_cells = act_grad.reshape(10, 5, 2, slots, 128)
        put_cells(slope, 0, 10, 0, act_cells[:, :, 0])
        put_cells(slope, 0, 10, 1, act_cells[:, :, 1])
        out_cells = out_grad.reshape(10, 5, 2, slots, 128)
        for first in range(0, 10, count):
            back = conv_pairs(slope, back_pairs[...], first, count)
            for parity in range(2):
                part = back[:, parity * 128 : (parity + 1) * 128].reshape(count, 5, slots, 128)
                total = out_cells[first : first + count, :, parity] + part
                gate = masks[0, first : first + count, :, parity].astype(jnp.float32)
                last[pl.ds(first, count), :, parity] = (total * gate).astype(jnp.bfloat16)
        kernel_gradients(boards, last[...].reshape(-1, 128))


def learn(
    role, length, boards, actions, behaviour, regular, rewards, weights, policy_t, value_t, count=5
):
    slots = boards.shape[2]
    smem = pl.BlockSpec(memory_space=pltpu.SMEM)
    vmem = pl.BlockSpec(memory_space=pltpu.VMEM)
    anywhere = pl.BlockSpec(memory_space=pltpu.HBM)
    cells = (10, 5, 2, slots, 128)
    around = (12, 6, 2, slots, 128)
    return pl.pallas_call(
        functools.partial(learner_kernel, count),
        out_shape=jax.ShapeDtypeStruct((ROWS, 128), jnp.float32),
        in_specs=[smem, smem] + [anywhere] * 8,
        out_specs=vmem,
        scratch_shapes=[
            pltpu.VMEM(around, jnp.bfloat16),
            pltpu.VMEM((2 * ROWS, 128), jnp.float32),
            pltpu.VMEM((1, slots), jnp.int32),
            pltpu.VMEM((1, slots), jnp.float32),
            pltpu.VMEM((1, slots), jnp.float32),
            pltpu.VMEM((1, slots), jnp.float32),
            pltpu.VMEM(policy_t.shape, policy_t.dtype),
            pltpu.VMEM(value_t.shape, value_t.dtype),
            pltpu.VMEM((2, 1536, 256), jnp.bfloat16),
            pltpu.VMEM((1536, 256), jnp.bfloat16),
            pltpu.VMEM(around, jnp.bfloat16),
            pltpu.VMEM(cells, jnp.bfloat16),
            pltpu.VMEM((2,) + cells, jnp.bfloat16),
            pltpu.VMEM(around, jnp.bfloat16),
            pltpu.SemaphoreType.DMA((9,)),
        ],
        compiler_params=pltpu.CompilerParams(vmem_limit_bytes=60 * 1024 * 1024),
        cost_estimate=pl.CostEstimate(
            flops=4 * 10**9, bytes_accessed=3 * 10**6, transcendentals=10000
        ),
        name="learn",
    )(role, length, boards, actions, behaviour, regular, rewards, weights, policy_t, value_t)


def update_kernel(role, gathered, torso_in, mine, old, done):
    fetch = pltpu.make_async_copy(
        torso_in.at[pl.ds(pl.multiple_of(role[0] * ROWS, ROWS), ROWS)], old, done
    )
    fetch.start()
    squares = jnp.sum(gathered[:, 3 * SHARE], axis=0, keepdims=True)
    square_sum = jnp.sum(squares, axis=1, keepdims=True)
    factor = jnp.minimum(1.0, jnp.sqrt(256.0 * ROWS) / jnp.sqrt(square_sum + NORM_EPS))
    fetch.wait()

    for k in range(LINE * LINE):
        clipped = gathered[k, 0:SHARE] * factor
        first = gathered[k, SHARE : 2 * SHARE]
        second = gathered[k, 2 * SHARE : 3 * SHARE]
        first = BETA_ONE * first + (1.0 - BETA_ONE) * clipped
        second = BETA_TWO * second + (1.0 - BETA_TWO) * clipped * clipped
        rows = slice(k * SHARE, (k + 1) * SHARE)
        mine[rows] = old[rows] - LEARN_RATE * first / (jnp.sqrt(second) + ADAM_EPS)


def update(role, gathered, torso):
    vmem = pl.BlockSpec(memory_space=pltpu.VMEM)
    return pl.pallas_call(
        update_kernel,
        out_shape=jax.ShapeDtypeStruct((ROWS, 128), jnp.float32),
        in_specs=[
            pl.BlockSpec(memory_space=pltpu.SMEM), vmem, pl.BlockSpec(memory_space=pltpu.HBM)
        ],
        out_specs=vmem,
        scratch_shapes=[pltpu.VMEM((ROWS, 128), jnp.float32), pltpu.SemaphoreType.DMA],
        compiler_params=pltpu.CompilerParams(vmem_limit_bytes=16 * 1024 * 1024),
        name="update",
    )(role, gathered, torso)


PLANES = [[LINE * k + z for k in range(LINE * LINE)] for z in range(LINE)]


def shifted(x, axis, step):
    stride = {"y": LINE * LINE, "x": LINE, "z": 1}[axis]
    pairs = []
    for d in range(LINE**3):
        at = d // stride % LINE
        pairs.append((d, d + ((at + step) % LINE - at) * stride))
    return lax.ppermute(x, "dp", pairs)


def line_total(x, axis):
    return (x + shifted(x, axis, 2)) + (shifted(x, axis, 1) + shifted(x, axis, 3))


def plane_exchange(x):
    return lax.all_to_all(x, "dp", 0, 0, axis_index_groups=PLANES)


def plane_gather(x):
    return plane_exchange(jnp.broadcast_to(x, (LINE * LINE,) + x.shape))


def role_swap(x):
    return lax.ppermute(x, "role", [(0, 1), (1, 0)])


def half_moments(first_moment, second_moment):
    pairs = []
    for role in range(2):
        for d in range(LINE**3):
            z = d % LINE
            owner = 32 * role + 2 * (d // LINE) + z % 2
            pairs.append(((z // 2) * LINE**3 + owner, role * LINE**3 + d))
    both = jnp.concatenate([first_moment, second_moment])
    return lax.ppermute(both, ("role", "dp"), pairs)


def line_exchange(share, half, z):
    near = shifted(jnp.concatenate([share, half]), "z", 1)
    total = (share + shifted(share, "z", 2)) + (near[:SHARE] + shifted(share, "z", 3))
    rows = SHARE // 2
    low = jnp.where(z % 2 == 0, half, near[SHARE:])
    high = jnp.where(z % 2 == 0, near[SHARE:], half)
    return (
        total,
        jnp.concatenate([low[:rows], high[:rows]]),
        jnp.concatenate([low[rows:], high[rows:]]),
    )


def body(
    board_now,
    traj_boards,
    actions,
    lengths,
    behaviour,
    regular,
    rewards,
    torso,
    policy_head,
    value_head,
    first_moment,
    second_moment,
):
    role = lax.axis_index("role")
    dp = lax.axis_index("dp")
    role_box = jnp.full((1,), role, jnp.int32)
    half = half_moments(first_moment, second_moment)
    gradient = learn(
        role_box,
        lengths,
        by_cell(traj_boards[0]),
        actions,
        behaviour,
        regular,
        rewards,
        torso,
        policy_head.T,
        value_head[None],
    )
    share = jnp.sum(plane_exchange(gradient.reshape(LINE * LINE, SHARE, 128)), axis=0)
    share, first, second = line_exchange(share, half, dp % LINE)
    squares = jnp.sum(share * share, axis=0, keepdims=True)
    squares = squares + role_swap(squares)
    squares = jnp.pad(squares, ((0, 7), (0, 0)))
    gathered = plane_gather(jnp.concatenate([share, first, second, squares]))
    mine = update(role_box, gathered, torso)
    other = role_swap(mine)
    here = act(role_box, mine, other, by_cell(board_now), policy_head.T.astype(jnp.float32))
    there = role_swap(here)
    out_rows = first_moment.shape[0]
    layer = dp // (LINE**3 // 2)
    at = dp % (LINE**3 // 2) * out_rows
    new_share = jnp.where(
        role == layer,
        lax.dynamic_slice_in_dim(mine, at, out_rows, 0),
        lax.dynamic_slice_in_dim(other, at, out_rows, 0),
    )
    move_logp = jnp.concatenate([jnp.where(role == 0, here, there), jnp.where(role == 0, there, here)])
    return (new_share, move_logp)


def solution(mesh):
    return jax.shard_map(
        body,
        mesh=mesh,
        in_specs=(
            P("dp", None, None, None),
            P("dp", None, None, None, None),
            P("dp", None),
            P("dp"),
            P("dp", None),
            P("dp", None),
            P("dp", None),
            P(),
            P(),
            P(),
            P("dp", None),
            P("dp", None),
        ),
        out_specs=(P("dp", None), P("dp", None)),
        check_vma=False,
    )
```

```python
import functools

import jax
import jax.numpy as jnp
from jax import lax
from jax.experimental import pallas as pl
from jax.experimental.pallas import tpu as pltpu
from jax.sharding import PartitionSpec as P

ETA = 0.2
LEARN_RATE = 0.03
BETA_ONE = 0.9
BETA_TWO = 0.999
ADAM_EPS = 1e-08
NORM_EPS = 1e-12
ROWS = 1152
LINE = 4
SEGMENT = 2 * ROWS // (2 * LINE)
PIECE = SEGMENT // 8


def by_cell(boards):
    return jnp.transpose(boards, (1, 2, 0, 3))


def inner_cells(ref):
    return ref.reshape((12, 12) + ref.shape[3:]).at[1:11, 1:11]


def segment_parts(layer, offset):
    start = layer * ROWS + offset * 128
    at, parts = start, []
    while at < start + 128:
        segment = at // SEGMENT
        end = min(start + 128, (segment + 1) * SEGMENT)
        parts.append((segment, at - segment * SEGMENT, end - segment * SEGMENT, at - start))
        at = end
    return parts


def clear_border(ref):
    zero_row = jnp.zeros(ref.shape[1:], ref.dtype)
    ref[0] = zero_row
    ref[11] = zero_row
    zero_col = jnp.zeros((12,) + ref.shape[3:], ref.dtype)
    ref[:, 0, 0] = zero_col
    ref[:, 5, 1] = zero_col


def pair_kernels(kernel_of, store):
    nothing = jnp.zeros((128, 128), jnp.bfloat16)
    for p in range(3):
        row = [kernel_of(p, q) for q in range(3)]
        for q in range(4):
            left = row[q] if q < 3 else nothing
            right = row[q - 1] if q > 0 else nothing
            store(4 * p + q, jnp.concatenate([left, right], axis=1))


def conv_pairs(source, pair_weights, first, count):
    windows = []
    for p in range(3):
        for q in range(4):
            window = source[pl.ds(first + p, count), q // 2 : q // 2 + 5, q % 2]
            windows.append(window.reshape(-1, 128))
    return jnp.dot(
        jnp.concatenate(windows, axis=1), pair_weights, preferred_element_type=jnp.float32
    )


def residual(source, first, count, parity):
    if parity == 0:
        window = source[pl.ds(first + 1, count), 0:5, 1]
    else:
        window = source[pl.ds(first + 1, count), 1:6, 0]
    return window


def put_cells(target, first, count, parity, value):
    if parity == 0:
        target[pl.ds(first + 1, count), 0:5, 1] = value
    else:
        target[pl.ds(first + 1, count), 1:6, 0] = value


def actor_kernel(
    count, unroll, role, mine, other, boards_in, policy_t, out, boards, pairs, middle, last, heads, done
):
    games = boards.shape[3]
    half = pl.ds(pl.multiple_of(role[0] * games, games), games)
    fetch = pltpu.make_async_copy(boards_in.at[:, :, half], inner_cells(boards), done)
    fetch.start()
    spread = lax.broadcasted_iota(jnp.int32, (4, 1280), 1)
    row = lax.broadcasted_iota(jnp.int32, (4, 1280), 0)
    spread = (spread % 128 == 10 * row + spread // 128).astype(jnp.float32)
    by_column = lax.dot_general(
        policy_t[...], spread, (((0,), (0,)), ((), ())), preferred_element_type=jnp.float32
    )
    for j in range(10):
        heads[128 * j : 128 * j + 128, :] = by_column[:, 128 * j : 128 * j + 128].astype(jnp.bfloat16)
    for layer in range(2):
        def kernel_of(p, q, layer=layer):
            parts = []
            for segment, first, last_row, _ in segment_parts(layer, 3 * p + q):
                y, owner = segment // 2, segment % 2
                rows = slice(first, last_row)
                parts.append(jnp.where(role[0] == owner, mine[y, rows], other[y, rows]))
            return jnp.concatenate(parts, axis=0).astype(jnp.bfloat16)

        def store(block, value, layer=layer):
            pairs[layer, block * 128 : (block + 1) * 128, :] = value

        pair_kernels(kernel_of, store)
    clear_border(middle)
    clear_border(boards)
    fetch.wait()

    def run_layer(layer, source, emit):
        def step(at, carry):
            first = at * count
            pre = conv_pairs(source, pairs[layer], first, count)
            for parity in range(2):
                part = pre[:, parity * 128 : (parity + 1) * 128].reshape(count, 5, games, 128)
                before = residual(source, first, count, parity).astype(jnp.float32)
                emit(first, parity, (before + jnp.maximum(part, 0.0)).astype(jnp.bfloat16))
            return carry

        lax.fori_loop(0, 10 // count, step, 0, unroll=unroll)

    run_layer(0, boards, lambda first, parity, value: put_cells(middle, first, count, parity, value))

    def to_last(first, parity, value):
        last[pl.ds(first, count), :, parity] = value

    run_layer(1, middle, to_last)
    cells = [last[:, j // 2, j % 2].reshape(-1, 128) for j in range(10)]
    logits = jnp.dot(jnp.concatenate(cells, axis=1), heads[...], preferred_element_type=jnp.float32)
    logits = logits.reshape(10, games, 128)
    lanes = lax.broadcasted_iota(jnp.int32, (games, 128), 1)
    moves = []
    total = jnp.zeros((games, 1), jnp.float32)
    for d in range(4):
        gathered = jnp.zeros((games, 128), jnp.float32)
        for i in range(10):
            turned = pltpu.roll(logits[i], (10 * i - 10 * d) % 128, 1)
            gathered = jnp.where((lanes >= 10 * i) & (lanes < 10 * i + 10), turned, gathered)
        moves.append(gathered)
        total = total + jnp.sum(
            jnp.where(lanes < 100, jnp.exp(gathered), 0.0), axis=1, keepdims=True
        )
    log_total = jnp.log(total)
    for d in range(4):
        out[:, 100 * d : 100 * d + 100] = (moves[d] - log_total)[:, :100]


def act(role, mine, other, boards, policy_t, count=2, unroll=1):
    games = boards.shape[2] // 2
    vmem = pl.BlockSpec(memory_space=pltpu.VMEM)
    return pl.pallas_call(
        functools.partial(actor_kernel, count, unroll),
        out_shape=jax.ShapeDtypeStruct((games, 400), jnp.float32),
        in_specs=[
            pl.BlockSpec(memory_space=pltpu.SMEM), vmem, vmem, pl.BlockSpec(memory_space=pltpu.HBM), vmem
        ],
        out_specs=vmem,
        scratch_shapes=[
            pltpu.VMEM((12, 6, 2, games, 128), jnp.bfloat16),
            pltpu.VMEM((2, 1536, 256), jnp.bfloat16),
            pltpu.VMEM((12, 6, 2, games, 128), jnp.bfloat16),
            pltpu.VMEM((10, 5, 2, games, 128), jnp.bfloat16),
            pltpu.VMEM((1280, 128), jnp.bfloat16),
            pltpu.SemaphoreType.DMA,
        ],
        compiler_params=pltpu.CompilerParams(vmem_limit_bytes=32 * 1024 * 1024),
        cost_estimate=pl.CostEstimate(
            flops=8 * 10**9, bytes_accessed=4 * 10**6, transcendentals=30000
        ),
        name="act",
    )(role, mine, other, boards, policy_t)


def column_of(row):
    size = row.shape[1]
    across = lax.broadcasted_iota(jnp.int32, (size, size), 1)
    down = lax.broadcasted_iota(jnp.int32, (size, size), 0)
    spread = jnp.broadcast_to(row, (size, size))
    return jnp.sum(jnp.where(across == down, spread, jnp.zeros_like(spread)), axis=1, keepdims=True)


def later(x, reach):
    return jnp.concatenate([x[reach:], jnp.zeros((reach, x.shape[1]), x.dtype)], axis=0)


def learner_kernel(
    count, role, length, boards_in, actions_in, behaviour_in, regular_in, rewards_in, weights_in,
    policy_in, value_in, grad,
    boards, weights, actions, behaviour, regular, rewards, policy_t, value_t, pairs, back_pairs,
    middle, last, masks, slope, turned, done,
):
    slots = boards.shape[3]
    moves = [
        (weights_in.at[0:ROWS], weights.at[0:ROWS]),
        (boards_in, inner_cells(boards)),
        (weights_in.at[ROWS : 2 * ROWS], weights.at[ROWS : 2 * ROWS]),
        (actions_in, actions),
        (behaviour_in, behaviour),
        (regular_in, regular),
        (rewards_in, rewards),
        (policy_in, policy_t),
        (value_in, value_t),
    ]
    copies = [pltpu.make_async_copy(a, b, done.at[k]) for k, (a, b) in enumerate(moves)]
    for copy in copies:
        copy.start()
    clear_border(boards)
    copies[0].wait()

    for layer in range(2):
        if layer == 1:
            copies[2].wait()

        def kernel_of(p, q, layer=layer):
            at = layer * ROWS + (3 * p + q) * 128
            return weights[at : at + 128, :].astype(jnp.bfloat16)

        def store(block, value, layer=layer):
            pairs[layer, block * 128 : (block + 1) * 128, :] = value

        pair_kernels(kernel_of, store)
    clear_border(middle)
    clear_border(slope)
    copies[1].wait()

    def run_layer(layer, source, emit):
        for first in range(0, 10, count):
            pre = conv_pairs(source, pairs[layer], first, count)
            for parity in range(2):
                part = pre[:, parity * 128 : (parity + 1) * 128].reshape(count, 5, slots, 128)
                before = residual(source, first, count, parity).astype(jnp.float32)
                emit(first, parity, (before + jnp.maximum(part, 0.0)).astype(jnp.bfloat16))
                masks[layer, first : first + count, :, parity] = (part > 0).astype(jnp.bfloat16)

    run_layer(0, boards, lambda first, parity, value: put_cells(middle, first, count, parity, value))

    def to_last(first, parity, value):
        last[pl.ds(first, count), :, parity] = value

    run_layer(1, middle, to_last)

    for copy in copies[3:]:
        copy.wait()

    eight = jnp.concatenate(
        [
            policy_t[...].astype(jnp.float32),
            value_t[...].astype(jnp.float32),
            jnp.zeros((3, 128), jnp.float32),
        ],
        axis=0,
    )
    heads_t = jnp.concatenate(
        [eight, eight, eight, jnp.zeros((104, 128), jnp.float32)], axis=0
    ).astype(jnp.bfloat16)

    scores = lax.dot_general(
        last[...].reshape(-1, 128), heads_t, (((1,), (1,)), ((), ())),
        preferred_element_type=jnp.float32,
    ).reshape(100, slots, 128)
    lane = lax.broadcasted_iota(jnp.int32, (slots, 128), 1)
    weights_sum = jnp.sum(jnp.where(lane < 4, jnp.exp(scores), 0.0), axis=0)
    log_total = jnp.log(jnp.sum(weights_sum, axis=1, keepdims=True))
    action = column_of(actions[...])
    direction = action // 100
    cell = action - 100 * direction
    cells = lax.broadcasted_iota(jnp.int32, (100, slots, 128), 0)
    taken = (cells == cell[None]) & (lane % 8 == direction)[None]
    picked = jnp.sum(
        jnp.sum(jnp.where(taken & (lane < 4)[None], scores, 0.0), axis=0), axis=1, keepdims=True
    )
    value_sum = jnp.sum(scores, axis=0)
    value = jnp.tanh(
        jnp.sum(jnp.where(lane == 4, value_sum, 0.0), axis=1, keepdims=True) / 100.0
    )
    log_policy = picked - log_total

    positions = lax.broadcasted_iota(jnp.int32, (slots, 1), 0)
    live = (positions < length[0]).astype(jnp.float32)
    next_live = (positions + 1 < length[0]).astype(jnp.float32)
    ratio = jnp.minimum(1.0, jnp.exp(log_policy - column_of(behaviour[...])))
    shaped = column_of(rewards[...]) - ETA * (log_policy - column_of(regular[...]))
    next_values = later(value, 1) * next_live
    correction = live * ratio * (shaped + next_values - value)
    decay = live * ratio
    reach = 1
    while reach < slots:
        correction = correction + decay * later(correction, reach)
        decay = decay * later(decay, reach)
        reach *= 2
    targets = value + correction
    next_targets = later(targets, 1) * next_live
    policy_grad = -live * ratio * (shaped + next_targets - value)
    value_grad = -live * (targets - value)

    value_cell = value_grad * (1.0 - value * value) / 100.0
    by_policy = policy_grad[None] * (taken.astype(jnp.float32) - jnp.exp(scores - log_total[None]))
    in_policy = (lane % 8 < 4) & (lane < 24)
    in_value = (lane % 8 == 4) & (lane < 24)
    by_score = jnp.where(
        in_policy[None], by_policy, jnp.where(in_value, value_cell, 0.0)[None]
    )
    high = by_score.astype(jnp.bfloat16)
    rest = by_score - high.astype(jnp.float32)
    mid = rest.astype(jnp.bfloat16)
    low = rest - mid.astype(jnp.float32)
    parts = jnp.where(
        (lane < 8)[None],
        high.astype(jnp.float32),
        jnp.where((lane < 16)[None], mid.astype(jnp.float32), low),
    ).astype(jnp.bfloat16)
    out_grad = jnp.dot(
        parts.reshape(-1, 128), heads_t, preferred_element_type=jnp.float32
    )
    act_grad = (out_grad * masks[1].reshape(-1, 128).astype(jnp.float32)).astype(jnp.bfloat16)

    def kernel_of(p, q):
        at = ROWS + (8 - (3 * p + q)) * 128
        return weights[at : at + 128, :].T.astype(jnp.bfloat16)

    def store(block, value):
        back_pairs[block * 128 : (block + 1) * 128, :] = value

    pair_kernels(kernel_of, store)
    act_cells = act_grad.reshape(10, 5, 2, slots, 128)
    put_cells(slope, 0, 10, 0, act_cells[:, :, 0])
    put_cells(slope, 0, 10, 1, act_cells[:, :, 1])
    out_cells = out_grad.reshape(10, 5, 2, slots, 128)
    for first in range(0, 10, count):
        back = conv_pairs(slope, back_pairs[...], first, count)
        for parity in range(2):
            part = back[:, parity * 128 : (parity + 1) * 128].reshape(count, 5, slots, 128)
            total = out_cells[first : first + count, :, parity] + part
            gate = masks[0, first : first + count, :, parity].astype(jnp.float32)
            last[pl.ds(first, count), :, parity] = (total * gate).astype(jnp.bfloat16)
    turned[1] = act_grad.T
    turned[0] = last[...].reshape(-1, 128).T

    for core in range(2):

        @pl.when(role[0] == core)
        def _(core=core):
            for layer, source in ((1, middle), (0, boards)):
                across = turned[layer]
                for offset in range(9):
                    parts = [x for x in segment_parts(layer, offset) if x[0] % 2 == core]
                    if parts:
                        p, q = offset // 3, offset % 3
                        cols = [source[p : p + 10, (j + q) // 2, (j + q) % 2] for j in range(10)]
                        window = jnp.stack(cols, axis=1).reshape(-1, 128)
                        block = jnp.dot(across, window, preferred_element_type=jnp.float32).T
                        for segment, first, end, at in parts:
                            grad[segment // 2, first:end] = block[at : at + end - first]


def learn(
    role, length, boards, actions, behaviour, regular, rewards, weights, policy_t, value_t, count=5
):
    slots = boards.shape[2]
    smem = pl.BlockSpec(memory_space=pltpu.SMEM)
    vmem = pl.BlockSpec(memory_space=pltpu.VMEM)
    anywhere = pl.BlockSpec(memory_space=pltpu.HBM)
    cells = (10, 5, 2, slots, 128)
    around = (12, 6, 2, slots, 128)
    return pl.pallas_call(
        functools.partial(learner_kernel, count),
        out_shape=jax.ShapeDtypeStruct((LINE, SEGMENT, 128), jnp.float32),
        in_specs=[smem, smem] + [anywhere] * 8,
        out_specs=vmem,
        scratch_shapes=[
            pltpu.VMEM(around, jnp.bfloat16),
            pltpu.VMEM((2 * ROWS, 128), jnp.float32),
            pltpu.VMEM((1, slots), jnp.int32),
            pltpu.VMEM((1, slots), jnp.float32),
            pltpu.VMEM((1, slots), jnp.float32),
            pltpu.VMEM((1, slots), jnp.float32),
            pltpu.VMEM(policy_t.shape, policy_t.dtype),
            pltpu.VMEM(value_t.shape, value_t.dtype),
            pltpu.VMEM((2, 1536, 256), jnp.bfloat16),
            pltpu.VMEM((1536, 256), jnp.bfloat16),
            pltpu.VMEM(around, jnp.bfloat16),
            pltpu.VMEM(cells, jnp.bfloat16),
            pltpu.VMEM((2,) + cells, jnp.bfloat16),
            pltpu.VMEM(around, jnp.bfloat16),
            pltpu.VMEM((2, 128, 100 * slots), jnp.bfloat16),
            pltpu.SemaphoreType.DMA((9,)),
        ],
        compiler_params=pltpu.CompilerParams(vmem_limit_bytes=60 * 1024 * 1024),
        cost_estimate=pl.CostEstimate(
            flops=4 * 10**9, bytes_accessed=3 * 10**6, transcendentals=10000
        ),
        name="learn",
    )(role, length, boards, actions, behaviour, regular, rewards, weights, policy_t, value_t)


def update_kernel(place, summed, squares, moments, torso_in, fresh, old, first, second, done):
    start = pl.multiple_of(place[1] * (2 * SEGMENT) + place[0] * SEGMENT, SEGMENT)
    fetch = pltpu.make_async_copy(torso_in.at[pl.ds(start, SEGMENT)], old, done)
    fetch.start()
    square_sum = jnp.sum(squares[...], axis=1, keepdims=True)
    factor = jnp.minimum(1.0, jnp.sqrt(256.0 * ROWS) / jnp.sqrt(square_sum + NORM_EPS))
    for x in range(2):
        for z in range(LINE):
            rows = slice((LINE * x + z) * PIECE, (LINE * x + z + 1) * PIECE)
            first[rows] = moments[z, x, 0:PIECE]
            second[rows] = moments[z, x, PIECE : 2 * PIECE]
    fetch.wait()
    clipped = summed[...] * factor
    moment_one = BETA_ONE * first[...] + (1.0 - BETA_ONE) * clipped
    moment_two = BETA_TWO * second[...] + (1.0 - BETA_TWO) * clipped * clipped
    fresh[...] = old[...] - LEARN_RATE * moment_one / (jnp.sqrt(moment_two) + ADAM_EPS)


def update(place, summed, squares, moments, torso):
    vmem = pl.BlockSpec(memory_space=pltpu.VMEM)
    rows = pltpu.VMEM((SEGMENT, 128), jnp.float32)
    return pl.pallas_call(
        update_kernel,
        out_shape=jax.ShapeDtypeStruct((SEGMENT, 128), jnp.float32),
        in_specs=[
            pl.BlockSpec(memory_space=pltpu.SMEM), vmem, vmem, vmem,
            pl.BlockSpec(memory_space=pltpu.HBM),
        ],
        out_specs=vmem,
        scratch_shapes=[rows, rows, rows, pltpu.SemaphoreType.DMA],
        compiler_params=pltpu.CompilerParams(vmem_limit_bytes=16 * 1024 * 1024),
        name="update",
    )(place, summed, squares, moments, torso)


def shifted(x, axis, step):
    stride = {"y": LINE * LINE, "x": LINE, "z": 1}[axis]
    pairs = []
    for d in range(LINE**3):
        at = d // stride % LINE
        pairs.append((d, d + ((at + step) % LINE - at) * stride))
    return lax.ppermute(x, "dp", pairs)


def line_total(x, axis):
    return (x + shifted(x, axis, 2)) + (shifted(x, axis, 1) + shifted(x, axis, 3))


def line_scatter(chunks, axis, at):
    def chunk(step):
        return lax.dynamic_index_in_dim(chunks, (at + step) % LINE, 0, keepdims=False)

    return (chunk(0) + shifted(chunk(2), axis, 2)) + (
        shifted(chunk(1), axis, 1) + shifted(chunk(3), axis, 3)
    )


def line_place(pieces, at):
    whole = jnp.zeros((LINE,) + pieces[0].shape, pieces[0].dtype)
    for step, piece in enumerate(pieces):
        whole = lax.dynamic_update_index_in_dim(whole, piece, (at - step) % LINE, 0)
    return whole


def line_gather(x, axis, at):
    return line_place([x] + [shifted(x, axis, step) for step in range(1, LINE)], at)


def line_exchange(summed, moments, axis, at):
    rows = summed.shape[0]
    both = jnp.concatenate([summed, moments])
    got = [both] + [shifted(both, axis, step) for step in range(1, LINE)]
    total = (got[0][:rows] + got[2][:rows]) + (got[1][:rows] + got[3][:rows])
    return total, line_place([x[rows:] for x in got], at)


def role_swap(x):
    return lax.ppermute(x, "role", [(0, 1), (1, 0)])


def body(
    board_now,
    traj_boards,
    actions,
    lengths,
    behaviour,
    regular,
    rewards,
    torso,
    policy_head,
    value_head,
    first_moment,
    second_moment,
):
    role = lax.axis_index("role")
    dp = lax.axis_index("dp")
    y, x, z = dp // (LINE * LINE), dp // LINE % LINE, dp % LINE
    place = jnp.stack([role, y]).astype(jnp.int32)
    gradient = learn(
        place,
        lengths,
        by_cell(traj_boards[0]),
        actions,
        behaviour,
        regular,
        rewards,
        torso,
        policy_head.T,
        value_head[None],
    )
    summed = line_scatter(gradient, "y", y)
    summed, moments = line_exchange(summed, jnp.concatenate([first_moment, second_moment]), "x", x)
    moments = lax.dynamic_slice_in_dim(moments, 2 * role, 2, 0)
    summed, moments = line_exchange(summed, moments.reshape(-1, 128), "z", z)
    squares = jnp.sum(summed * summed, axis=0, keepdims=True)
    squares = line_total(squares + role_swap(squares), "y")
    fresh = update(place, summed, squares, moments.reshape(LINE, 2, 2 * PIECE, 128), torso)
    mine = line_gather(fresh, "y", y)
    other = role_swap(mine)
    here = act(place, mine, other, by_cell(board_now), policy_head.T.astype(jnp.float32))
    there = role_swap(here)
    at = (LINE * x + z) % (2 * LINE) * PIECE
    new_share = jnp.where(
        role == x // 2,
        lax.dynamic_slice(mine, (y, at, 0), (1, PIECE, 128))[0],
        lax.dynamic_slice(other, (y, at, 0), (1, PIECE, 128))[0],
    )
    move_logp = jnp.concatenate([jnp.where(role == 0, here, there), jnp.where(role == 0, there, here)])
    return (new_share, move_logp)


def solution(mesh):
    return jax.shard_map(
        body,
        mesh=mesh,
        in_specs=(
            P("dp", None, None, None),
            P("dp", None, None, None, None),
            P("dp", None),
            P("dp"),
            P("dp", None),
            P("dp", None),
            P("dp", None),
            P(),
            P(),
            P(),
            P("dp", None),
            P("dp", None),
        ),
        out_specs=(P("dp", None), P("dp", None)),
        check_vma=False,
    )
```

```python
import functools

import jax
import jax.numpy as jnp
from jax import lax
from jax.experimental import pallas as pl
from jax.experimental.pallas import tpu as pltpu
from jax.sharding import PartitionSpec as P

ETA = 0.2
LEARN_RATE = 0.03
BETA_ONE = 0.9
BETA_TWO = 0.999
ADAM_EPS = 1e-08
NORM_EPS = 1e-12
ROWS = 1152
LINE = 4
SEGMENT = 2 * ROWS // (2 * LINE)
PIECE = SEGMENT // 8


def by_cell(boards):
    return jnp.transpose(boards, (1, 2, 0, 3))


def inner_cells(ref):
    return ref.reshape((12, 12) + ref.shape[3:]).at[1:11, 1:11]


def segment_parts(layer, offset):
    start = layer * ROWS + offset * 128
    at, parts = start, []
    while at < start + 128:
        segment = at // SEGMENT
        end = min(start + 128, (segment + 1) * SEGMENT)
        parts.append((segment, at - segment * SEGMENT, end - segment * SEGMENT, at - start))
        at = end
    return parts


def clear_border(ref):
    zero_row = jnp.zeros(ref.shape[1:], ref.dtype)
    ref[0] = zero_row
    ref[11] = zero_row
    zero_col = jnp.zeros((12,) + ref.shape[3:], ref.dtype)
    ref[:, 0, 0] = zero_col
    ref[:, 5, 1] = zero_col


def pair_kernels(kernel_of, store):
    nothing = jnp.zeros((128, 128), jnp.bfloat16)
    for p in range(3):
        row = [kernel_of(p, q) for q in range(3)]
        for q in range(4):
            left = row[q] if q < 3 else nothing
            right = row[q - 1] if q > 0 else nothing
            store(4 * p + q, jnp.concatenate([left, right], axis=1))


def conv_pairs(source, pair_weights, first, count):
    windows = []
    for p in range(3):
        for q in range(4):
            window = source[pl.ds(first + p, count), q // 2 : q // 2 + 5, q % 2]
            windows.append(window.reshape(-1, 128))
    return jnp.dot(
        jnp.concatenate(windows, axis=1), pair_weights, preferred_element_type=jnp.float32
    )


def residual(source, first, count, parity):
    if parity == 0:
        window = source[pl.ds(first + 1, count), 0:5, 1]
    else:
        window = source[pl.ds(first + 1, count), 1:6, 0]
    return window


def put_cells(target, first, count, parity, value):
    if parity == 0:
        target[pl.ds(first + 1, count), 0:5, 1] = value
    else:
        target[pl.ds(first + 1, count), 1:6, 0] = value


def stage_kernel(mine, boards_in, policy_t, boards, heads, done):
    games = boards.shape[3]
    half = pl.ds(pl.multiple_of(lax.axis_index("role") * games, games), games)
    fetch = pltpu.make_async_copy(boards_in.at[:, :, half], inner_cells(boards), done)
    fetch.start()
    clear_border(boards)
    spread = lax.broadcasted_iota(jnp.int32, (4, 1280), 1)
    row = lax.broadcasted_iota(jnp.int32, (4, 1280), 0)
    spread = (spread % 128 == 10 * row + spread // 128).astype(jnp.float32)
    by_column = lax.dot_general(
        policy_t[...], spread, (((0,), (0,)), ((), ())), preferred_element_type=jnp.float32
    )
    for j in range(10):
        heads[128 * j : 128 * j + 128, :] = by_column[:, 128 * j : 128 * j + 128].astype(jnp.bfloat16)
    fetch.wait()


def stage(mine, boards, policy_t):
    games = boards.shape[2] // 2
    vmem = pl.BlockSpec(memory_space=pltpu.VMEM)
    anywhere = pl.BlockSpec(memory_space=pltpu.HBM)
    return pl.pallas_call(
        stage_kernel,
        out_shape=[
            jax.ShapeDtypeStruct((12, 6, 2, games, 128), jnp.bfloat16),
            jax.ShapeDtypeStruct((1280, 128), jnp.bfloat16),
        ],
        in_specs=[anywhere, anywhere, vmem],
        out_specs=[vmem, vmem],
        scratch_shapes=[pltpu.SemaphoreType.DMA],
        compiler_params=pltpu.CompilerParams(vmem_limit_bytes=16 * 1024 * 1024),
        cost_estimate=pl.CostEstimate(
            flops=10**9, bytes_accessed=4 * 10**6, transcendentals=0
        ),
        name="stage",
    )(mine, boards, policy_t)


def actor_kernel(count, unroll, mine, other, boards, heads, out, pairs, middle, last):
    games = boards.shape[3]
    role = lax.axis_index("role")
    for layer in range(2):
        def kernel_of(p, q, layer=layer):
            parts = []
            for segment, first, last_row, _ in segment_parts(layer, 3 * p + q):
                y, owner = segment // 2, segment % 2
                rows = slice(first, last_row)
                parts.append(jnp.where(role == owner, mine[y, rows], other[y, rows]))
            return jnp.concatenate(parts, axis=0).astype(jnp.bfloat16)

        def store(block, value, layer=layer):
            pairs[layer, block * 128 : (block + 1) * 128, :] = value

        pair_kernels(kernel_of, store)
    clear_border(middle)

    def run_layer(layer, source, emit):
        def step(at, carry):
            first = at * count
            pre = conv_pairs(source, pairs[layer], first, count)
            for parity in range(2):
                part = pre[:, parity * 128 : (parity + 1) * 128].reshape(count, 5, games, 128)
                before = residual(source, first, count, parity).astype(jnp.float32)
                emit(first, parity, (before + jnp.maximum(part, 0.0)).astype(jnp.bfloat16))
            return carry

        lax.fori_loop(0, 10 // count, step, 0, unroll=unroll)

    run_layer(0, boards, lambda first, parity, value: put_cells(middle, first, count, parity, value))

    def to_last(first, parity, value):
        last[pl.ds(first, count), :, parity] = value

    run_layer(1, middle, to_last)
    cells = [last[:, j // 2, j % 2].reshape(-1, 128) for j in range(10)]
    logits = jnp.dot(jnp.concatenate(cells, axis=1), heads[...], preferred_element_type=jnp.float32)
    logits = logits.reshape(10, games, 128)
    lanes = lax.broadcasted_iota(jnp.int32, (games, 128), 1)
    moves = []
    total = jnp.zeros((games, 1), jnp.float32)
    for d in range(4):
        gathered = jnp.zeros((games, 128), jnp.float32)
        for i in range(10):
            turned = pltpu.roll(logits[i], (10 * i - 10 * d) % 128, 1)
            gathered = jnp.where((lanes >= 10 * i) & (lanes < 10 * i + 10), turned, gathered)
        moves.append(gathered)
        total = total + jnp.sum(
            jnp.where(lanes < 100, jnp.exp(gathered), 0.0), axis=1, keepdims=True
        )
    log_total = jnp.log(total)
    for d in range(4):
        out[:, 100 * d : 100 * d + 100] = (moves[d] - log_total)[:, :100]


def act(mine, other, boards, heads, count=2, unroll=1):
    games = boards.shape[3]
    vmem = pl.BlockSpec(memory_space=pltpu.VMEM)
    return pl.pallas_call(
        functools.partial(actor_kernel, count, unroll),
        out_shape=jax.ShapeDtypeStruct((games, 400), jnp.float32),
        in_specs=[vmem] * 4,
        out_specs=vmem,
        scratch_shapes=[
            pltpu.VMEM((2, 1536, 256), jnp.bfloat16),
            pltpu.VMEM((12, 6, 2, games, 128), jnp.bfloat16),
            pltpu.VMEM((10, 5, 2, games, 128), jnp.bfloat16),
        ],
        compiler_params=pltpu.CompilerParams(vmem_limit_bytes=32 * 1024 * 1024),
        cost_estimate=pl.CostEstimate(
            flops=8 * 10**9, bytes_accessed=4 * 10**6, transcendentals=30000
        ),
        name="act",
    )(mine, other, boards, heads)


def column_of(row):
    size = row.shape[1]
    across = lax.broadcasted_iota(jnp.int32, (size, size), 1)
    down = lax.broadcasted_iota(jnp.int32, (size, size), 0)
    spread = jnp.broadcast_to(row, (size, size))
    return jnp.sum(jnp.where(across == down, spread, jnp.zeros_like(spread)), axis=1, keepdims=True)


def later(x, reach):
    return jnp.concatenate([x[reach:], jnp.zeros((reach, x.shape[1]), x.dtype)], axis=0)


def learner_kernel(
    count, length, boards_in, actions_in, behaviour_in, regular_in, rewards_in, weights_in,
    policy_in, value_in, own, next1, next2, next3,
    grad, boards, weights, actions, behaviour, regular, rewards, policy_t, value_t, pairs, back_pairs,
    middle, last, masks, slope, turned, done,
):
    slots = boards.shape[3]
    role = lax.axis_index("role")
    y = lax.axis_index("dp") // (LINE * LINE)
    moves = [
        (weights_in.at[0:ROWS], weights.at[0:ROWS]),
        (boards_in, inner_cells(boards)),
        (weights_in.at[ROWS : 2 * ROWS], weights.at[ROWS : 2 * ROWS]),
        (actions_in, actions),
        (behaviour_in, behaviour),
        (regular_in, regular),
        (rewards_in, rewards),
        (policy_in, policy_t),
        (value_in, value_t),
    ]
    copies = [pltpu.make_async_copy(a, b, done.at[k]) for k, (a, b) in enumerate(moves)]
    for copy in copies:
        copy.start()
    clear_border(boards)
    copies[0].wait()

    for layer in range(2):
        if layer == 1:
            copies[2].wait()

        def kernel_of(p, q, layer=layer):
            at = layer * ROWS + (3 * p + q) * 128
            return weights[at : at + 128, :].astype(jnp.bfloat16)

        def store(block, value, layer=layer):
            pairs[layer, block * 128 : (block + 1) * 128, :] = value

        pair_kernels(kernel_of, store)
    clear_border(middle)
    clear_border(slope)
    copies[1].wait()

    def run_layer(layer, source, emit):
        for first in range(0, 10, count):
            pre = conv_pairs(source, pairs[layer], first, count)
            for parity in range(2):
                part = pre[:, parity * 128 : (parity + 1) * 128].reshape(count, 5, slots, 128)
                before = residual(source, first, count, parity).astype(jnp.float32)
                emit(first, parity, (before + jnp.maximum(part, 0.0)).astype(jnp.bfloat16))
                masks[layer, first : first + count, :, parity] = (part > 0).astype(jnp.bfloat16)

    run_layer(0, boards, lambda first, parity, value: put_cells(middle, first, count, parity, value))

    def to_last(first, parity, value):
        last[pl.ds(first, count), :, parity] = value

    run_layer(1, middle, to_last)

    for copy in copies[3:]:
        copy.wait()

    eight = jnp.concatenate(
        [
            policy_t[...].astype(jnp.float32),
            value_t[...].astype(jnp.float32),
            jnp.zeros((3, 128), jnp.float32),
        ],
        axis=0,
    )
    heads_t = jnp.concatenate(
        [eight, eight, eight, jnp.zeros((104, 128), jnp.float32)], axis=0
    ).astype(jnp.bfloat16)

    scores = lax.dot_general(
        last[...].reshape(-1, 128), heads_t, (((1,), (1,)), ((), ())),
        preferred_element_type=jnp.float32,
    ).reshape(100, slots, 128)
    lane = lax.broadcasted_iota(jnp.int32, (slots, 128), 1)
    weights_sum = jnp.sum(jnp.where(lane < 4, jnp.exp(scores), 0.0), axis=0)
    log_total = jnp.log(jnp.sum(weights_sum, axis=1, keepdims=True))
    action = column_of(actions[...])
    direction = action // 100
    cell = action - 100 * direction
    cells = lax.broadcasted_iota(jnp.int32, (100, slots, 128), 0)
    taken = (cells == cell[None]) & (lane % 8 == direction)[None]
    picked = jnp.sum(
        jnp.sum(jnp.where(taken & (lane < 4)[None], scores, 0.0), axis=0), axis=1, keepdims=True
    )
    value_sum = jnp.sum(scores, axis=0)
    value = jnp.tanh(
        jnp.sum(jnp.where(lane == 4, value_sum, 0.0), axis=1, keepdims=True) / 100.0
    )
    log_policy = picked - log_total

    positions = lax.broadcasted_iota(jnp.int32, (slots, 1), 0)
    live = (positions < length[0]).astype(jnp.float32)
    next_live = (positions + 1 < length[0]).astype(jnp.float32)
    ratio = jnp.minimum(1.0, jnp.exp(log_policy - column_of(behaviour[...])))
    shaped = column_of(rewards[...]) - ETA * (log_policy - column_of(regular[...]))
    next_values = later(value, 1) * next_live
    correction = live * ratio * (shaped + next_values - value)
    decay = live * ratio
    reach = 1
    while reach < slots:
        correction = correction + decay * later(correction, reach)
        decay = decay * later(decay, reach)
        reach *= 2
    targets = value + correction
    next_targets = later(targets, 1) * next_live
    policy_grad = -live * ratio * (shaped + next_targets - value)
    value_grad = -live * (targets - value)

    value_cell = value_grad * (1.0 - value * value) / 100.0
    by_policy = policy_grad[None] * (taken.astype(jnp.float32) - jnp.exp(scores - log_total[None]))
    in_policy = (lane % 8 < 4) & (lane < 24)
    in_value = (lane % 8 == 4) & (lane < 24)
    by_score = jnp.where(
        in_policy[None], by_policy, jnp.where(in_value, value_cell, 0.0)[None]
    )
    high = by_score.astype(jnp.bfloat16)
    rest = by_score - high.astype(jnp.float32)
    mid = rest.astype(jnp.bfloat16)
    low = rest - mid.astype(jnp.float32)
    parts = jnp.where(
        (lane < 8)[None],
        high.astype(jnp.float32),
        jnp.where((lane < 16)[None], mid.astype(jnp.float32), low),
    ).astype(jnp.bfloat16)
    out_grad = jnp.dot(
        parts.reshape(-1, 128), heads_t, preferred_element_type=jnp.float32
    )
    act_grad = (out_grad * masks[1].reshape(-1, 128).astype(jnp.float32)).astype(jnp.bfloat16)

    def kernel_of(p, q):
        at = ROWS + (8 - (3 * p + q)) * 128
        return weights[at : at + 128, :].T.astype(jnp.bfloat16)

    def store(block, value):
        back_pairs[block * 128 : (block + 1) * 128, :] = value

    pair_kernels(kernel_of, store)
    act_cells = act_grad.reshape(10, 5, 2, slots, 128)
    put_cells(slope, 0, 10, 0, act_cells[:, :, 0])
    put_cells(slope, 0, 10, 1, act_cells[:, :, 1])
    out_cells = out_grad.reshape(10, 5, 2, slots, 128)
    for first in range(0, 10, count):
        back = conv_pairs(slope, back_pairs[...], first, count)
        for parity in range(2):
            part = back[:, parity * 128 : (parity + 1) * 128].reshape(count, 5, slots, 128)
            total = out_cells[first : first + count, :, parity] + part
            gate = masks[0, first : first + count, :, parity].astype(jnp.float32)
            last[pl.ds(first, count), :, parity] = (total * gate).astype(jnp.bfloat16)
    turned[1] = act_grad.T
    turned[0] = last[...].reshape(-1, 128).T

    for core in range(2):

        @pl.when(role == core)
        def _(core=core):
            for layer, source in ((1, middle), (0, boards)):
                across = turned[layer]
                for offset in range(9):
                    parts = [x for x in segment_parts(layer, offset) if x[0] % 2 == core]
                    if parts:
                        p, q = offset // 3, offset % 3
                        cols = [source[p : p + 10, (j + q) // 2, (j + q) % 2] for j in range(10)]
                        window = jnp.stack(cols, axis=1).reshape(-1, 128)
                        block = jnp.dot(across, window, preferred_element_type=jnp.float32).T
                        for segment, first, end, at in parts:
                            grad[segment // 2, first:end] = block[at : at + end - first]

    sends = [
        pltpu.make_async_copy(grad.at[lax.rem(y + k, LINE)], out, done.at[k])
        for k, out in enumerate((own, next1, next2, next3))
    ]
    for copy in sends:
        copy.start()
    for copy in sends:
        copy.wait()


def learn(
    length, boards, actions, behaviour, regular, rewards, weights, policy_t, value_t, count=5
):
    slots = boards.shape[2]
    smem = pl.BlockSpec(memory_space=pltpu.SMEM)
    anywhere = pl.BlockSpec(memory_space=pltpu.HBM)
    cells = (10, 5, 2, slots, 128)
    around = (12, 6, 2, slots, 128)
    return pl.pallas_call(
        functools.partial(learner_kernel, count),
        out_shape=[jax.ShapeDtypeStruct((SEGMENT, 128), jnp.float32)] * LINE,
        in_specs=[smem] + [anywhere] * 8,
        out_specs=[anywhere] * LINE,
        scratch_shapes=[
            pltpu.VMEM((LINE, SEGMENT, 128), jnp.float32),
            pltpu.VMEM(around, jnp.bfloat16),
            pltpu.VMEM((2 * ROWS, 128), jnp.float32),
            pltpu.VMEM((1, slots), jnp.int32),
            pltpu.VMEM((1, slots), jnp.float32),
            pltpu.VMEM((1, slots), jnp.float32),
            pltpu.VMEM((1, slots), jnp.float32),
            pltpu.VMEM(policy_t.shape, policy_t.dtype),
            pltpu.VMEM(value_t.shape, value_t.dtype),
            pltpu.VMEM((2, 1536, 256), jnp.bfloat16),
            pltpu.VMEM((1536, 256), jnp.bfloat16),
            pltpu.VMEM(around, jnp.bfloat16),
            pltpu.VMEM(cells, jnp.bfloat16),
            pltpu.VMEM((2,) + cells, jnp.bfloat16),
            pltpu.VMEM(around, jnp.bfloat16),
            pltpu.VMEM((2, 128, 100 * slots), jnp.bfloat16),
            pltpu.SemaphoreType.DMA((9,)),
        ],
        compiler_params=pltpu.CompilerParams(vmem_limit_bytes=60 * 1024 * 1024),
        cost_estimate=pl.CostEstimate(
            flops=4 * 10**9, bytes_accessed=3 * 10**6, transcendentals=10000
        ),
        name="learn",
    )(length, boards, actions, behaviour, regular, rewards, weights, policy_t, value_t)


def update_kernel(summed, squares, moments, torso_in, fresh, old, first, second, done):
    y = lax.axis_index("dp") // (LINE * LINE)
    start = pl.multiple_of((2 * y + lax.axis_index("role")) * SEGMENT, SEGMENT)
    fetch = pltpu.make_async_copy(torso_in.at[pl.ds(start, SEGMENT)], old, done)
    fetch.start()
    square_sum = jnp.sum(squares[...], axis=1, keepdims=True)
    factor = jnp.minimum(1.0, jnp.sqrt(256.0 * ROWS) / jnp.sqrt(square_sum + NORM_EPS))
    for x in range(2):
        for z in range(LINE):
            rows = slice((LINE * x + z) * PIECE, (LINE * x + z + 1) * PIECE)
            first[rows] = moments[z, x, 0:PIECE]
            second[rows] = moments[z, x, PIECE : 2 * PIECE]
    fetch.wait()
    clipped = summed[...] * factor
    moment_one = BETA_ONE * first[...] + (1.0 - BETA_ONE) * clipped
    moment_two = BETA_TWO * second[...] + (1.0 - BETA_TWO) * clipped * clipped
    fresh[...] = old[...] - LEARN_RATE * moment_one / (jnp.sqrt(moment_two) + ADAM_EPS)


def update(summed, squares, moments, torso):
    vmem = pl.BlockSpec(memory_space=pltpu.VMEM)
    rows = pltpu.VMEM((SEGMENT, 128), jnp.float32)
    return pl.pallas_call(
        update_kernel,
        out_shape=jax.ShapeDtypeStruct((SEGMENT, 128), jnp.float32),
        in_specs=[
            vmem, vmem, vmem, pl.BlockSpec(memory_space=pltpu.HBM)
        ],
        out_specs=vmem,
        scratch_shapes=[rows, rows, rows, pltpu.SemaphoreType.DMA],
        compiler_params=pltpu.CompilerParams(vmem_limit_bytes=16 * 1024 * 1024),
        name="update",
    )(summed, squares, moments, torso)


def shifted(x, axis, step):
    stride = {"y": LINE * LINE, "x": LINE, "z": 1}[axis]
    pairs = []
    for d in range(LINE**3):
        at = d // stride % LINE
        pairs.append((d, d + ((at + step) % LINE - at) * stride))
    return lax.ppermute(x, "dp", pairs)


def line_total(x, axis):
    return (x + shifted(x, axis, 2)) + (shifted(x, axis, 1) + shifted(x, axis, 3))


def line_scatter(chunks, axis):
    return (chunks[0] + shifted(chunks[2], axis, 2)) + (
        shifted(chunks[1], axis, 1) + shifted(chunks[3], axis, 3)
    )


def line_place(pieces, at):
    whole = jnp.zeros((LINE,) + pieces[0].shape, pieces[0].dtype)
    for step, piece in enumerate(pieces):
        whole = lax.dynamic_update_index_in_dim(whole, piece, (at - step) % LINE, 0)
    return whole


def line_gather(x, axis, at):
    return line_place([x] + [shifted(x, axis, step) for step in range(1, LINE)], at)


def role_swap(x):
    return lax.ppermute(x, "role", [(0, 1), (1, 0)])


def body(
    board_now,
    traj_boards,
    actions,
    lengths,
    behaviour,
    regular,
    rewards,
    torso,
    policy_head,
    value_head,
    first_moment,
    second_moment,
):
    role = lax.axis_index("role")
    dp = lax.axis_index("dp")
    y, x, z = dp // (LINE * LINE), dp // LINE % LINE, dp % LINE
    moments = line_gather(jnp.concatenate([first_moment, second_moment]), "x", x)
    moments = lax.dynamic_slice_in_dim(moments, 2 * role, 2, 0).reshape(-1, 128)
    chunks = learn(
        lengths,
        by_cell(traj_boards[0]),
        actions,
        behaviour,
        regular,
        rewards,
        torso,
        policy_head.T,
        value_head[None],
    )
    chunks, moments = lax.optimization_barrier((chunks, moments))
    moments = line_gather(moments, "z", z)
    summed = line_total(line_total(line_scatter(chunks, "y"), "x"), "z")
    squares = jnp.sum(summed * summed, axis=0, keepdims=True)
    squares = line_total(squares + role_swap(squares), "y")
    fresh = update(summed, squares, moments.reshape(LINE, 2, 2 * PIECE, 128), torso)
    mine = line_gather(fresh, "y", y)
    other = role_swap(mine)
    boards, heads = stage(mine, by_cell(board_now), policy_head.T.astype(jnp.float32))
    here = act(mine, other, boards, heads)
    there = role_swap(here)
    at = (LINE * x + z) % (2 * LINE) * PIECE
    new_share = jnp.where(
        role == x // 2,
        lax.dynamic_slice(mine, (y, at, 0), (1, PIECE, 128))[0],
        lax.dynamic_slice(other, (y, at, 0), (1, PIECE, 128))[0],
    )
    move_logp = jnp.concatenate([jnp.where(role == 0, here, there), jnp.where(role == 0, there, here)])
    return (new_share, move_logp)


def solution(mesh):
    return jax.shard_map(
        body,
        mesh=mesh,
        in_specs=(
            P("dp", None, None, None),
            P("dp", None, None, None, None),
            P("dp", None),
            P("dp"),
            P("dp", None),
            P("dp", None),
            P("dp", None),
            P(),
            P(),
            P(),
            P("dp", None),
            P("dp", None),
        ),
        out_specs=(P("dp", None), P("dp", None)),
        check_vma=False,
    )
```

```python
import functools

import jax
import jax.numpy as jnp
from jax import lax
from jax.experimental import pallas as pl
from jax.experimental.pallas import tpu as pltpu
from jax.sharding import PartitionSpec as P

ETA = 0.2
LEARN_RATE = 0.03
BETA_ONE = 0.9
BETA_TWO = 0.999
ADAM_EPS = 1e-08
NORM_EPS = 1e-12
ROWS = 1152
LINE = 4
SEGMENT = 2 * ROWS // (2 * LINE)
PIECE = SEGMENT // 8


def by_cell(boards):
    return jnp.transpose(boards, (1, 2, 0, 3))


def inner_cells(ref):
    return ref.reshape((12, 12) + ref.shape[3:]).at[1:11, 1:11]


def segment_parts(layer, offset):
    start = layer * ROWS + offset * 128
    at, parts = start, []
    while at < start + 128:
        segment = at // SEGMENT
        end = min(start + 128, (segment + 1) * SEGMENT)
        parts.append((segment, at - segment * SEGMENT, end - segment * SEGMENT, at - start))
        at = end
    return parts


def clear_border(ref):
    zero_row = jnp.zeros(ref.shape[1:], ref.dtype)
    ref[0] = zero_row
    ref[11] = zero_row
    zero_col = jnp.zeros((12,) + ref.shape[3:], ref.dtype)
    ref[:, 0, 0] = zero_col
    ref[:, 5, 1] = zero_col


def pair_kernels(kernel_of, store):
    nothing = jnp.zeros((128, 128), jnp.bfloat16)
    for p in range(3):
        row = [kernel_of(p, q) for q in range(3)]
        for q in range(4):
            left = row[q] if q < 3 else nothing
            right = row[q - 1] if q > 0 else nothing
            store(4 * p + q, jnp.concatenate([left, right], axis=1))


def conv_pairs(source, pair_weights, first, count):
    windows = []
    for p in range(3):
        for q in range(4):
            window = source[pl.ds(first + p, count), q // 2 : q // 2 + 5, q % 2]
            windows.append(window.reshape(-1, 128))
    return jnp.dot(
        jnp.concatenate(windows, axis=1), pair_weights, preferred_element_type=jnp.float32
    )


def residual(source, first, count, parity):
    if parity == 0:
        window = source[pl.ds(first + 1, count), 0:5, 1]
    else:
        window = source[pl.ds(first + 1, count), 1:6, 0]
    return window


def put_cells(target, first, count, parity, value):
    if parity == 0:
        target[pl.ds(first + 1, count), 0:5, 1] = value
    else:
        target[pl.ds(first + 1, count), 1:6, 0] = value


def stage_kernel(mine, boards_in, policy_t, boards, heads, done):
    games = boards.shape[3]
    half = pl.ds(pl.multiple_of(lax.axis_index("role") * games, games), games)
    fetch = pltpu.make_async_copy(boards_in.at[:, :, half], inner_cells(boards), done)
    fetch.start()
    clear_border(boards)
    spread = lax.broadcasted_iota(jnp.int32, (4, 1280), 1)
    row = lax.broadcasted_iota(jnp.int32, (4, 1280), 0)
    spread = (spread % 128 == 10 * row + spread // 128).astype(jnp.float32)
    by_column = lax.dot_general(
        policy_t[...], spread, (((0,), (0,)), ((), ())), preferred_element_type=jnp.float32
    )
    for j in range(10):
        heads[128 * j : 128 * j + 128, :] = by_column[:, 128 * j : 128 * j + 128].astype(jnp.bfloat16)
    fetch.wait()


def stage(mine, boards, policy_t):
    games = boards.shape[2] // 2
    vmem = pl.BlockSpec(memory_space=pltpu.VMEM)
    anywhere = pl.BlockSpec(memory_space=pltpu.HBM)
    return pl.pallas_call(
        stage_kernel,
        out_shape=[
            jax.ShapeDtypeStruct((12, 6, 2, games, 128), jnp.bfloat16),
            jax.ShapeDtypeStruct((1280, 128), jnp.bfloat16),
        ],
        in_specs=[anywhere, anywhere, vmem],
        out_specs=[vmem, vmem],
        scratch_shapes=[pltpu.SemaphoreType.DMA],
        compiler_params=pltpu.CompilerParams(vmem_limit_bytes=16 * 1024 * 1024),
        cost_estimate=pl.CostEstimate(
            flops=10**9, bytes_accessed=4 * 10**6, transcendentals=0
        ),
        name="stage",
    )(mine, boards, policy_t)


def actor_kernel(count, unroll, mine, other, boards, heads, out, pairs, middle, last):
    games = boards.shape[3]
    role = lax.axis_index("role")
    for layer in range(2):
        def kernel_of(p, q, layer=layer):
            parts = []
            for segment, first, last_row, _ in segment_parts(layer, 3 * p + q):
                y, owner = segment // 2, segment % 2
                rows = slice(first, last_row)
                parts.append(jnp.where(role == owner, mine[y, rows], other[y, rows]))
            return jnp.concatenate(parts, axis=0).astype(jnp.bfloat16)

        def store(block, value, layer=layer):
            pairs[layer, block * 128 : (block + 1) * 128, :] = value

        pair_kernels(kernel_of, store)
    clear_border(middle)

    def run_layer(layer, source, emit):
        def step(at, carry):
            first = at * count
            pre = conv_pairs(source, pairs[layer], first, count)
            for parity in range(2):
                part = pre[:, parity * 128 : (parity + 1) * 128].reshape(count, 5, games, 128)
                before = residual(source, first, count, parity).astype(jnp.float32)
                emit(first, parity, (before + jnp.maximum(part, 0.0)).astype(jnp.bfloat16))
            return carry

        lax.fori_loop(0, 10 // count, step, 0, unroll=unroll)

    run_layer(0, boards, lambda first, parity, value: put_cells(middle, first, count, parity, value))

    def to_last(first, parity, value):
        last[pl.ds(first, count), :, parity] = value

    run_layer(1, middle, to_last)
    cells = [last[:, j // 2, j % 2].reshape(-1, 128) for j in range(10)]
    logits = jnp.dot(jnp.concatenate(cells, axis=1), heads[...], preferred_element_type=jnp.float32)
    logits = logits.reshape(10, games, 128)
    lanes = lax.broadcasted_iota(jnp.int32, (games, 128), 1)
    moves = []
    total = jnp.zeros((games, 1), jnp.float32)
    for d in range(4):
        gathered = jnp.zeros((games, 128), jnp.float32)
        for i in range(10):
            turned = pltpu.roll(logits[i], (10 * i - 10 * d) % 128, 1)
            gathered = jnp.where((lanes >= 10 * i) & (lanes < 10 * i + 10), turned, gathered)
        moves.append(gathered)
        total = total + jnp.sum(
            jnp.where(lanes < 100, jnp.exp(gathered), 0.0), axis=1, keepdims=True
        )
    log_total = jnp.log(total)
    for d in range(4):
        out[:, 100 * d : 100 * d + 100] = (moves[d] - log_total)[:, :100]


def act(mine, other, boards, heads, count=2, unroll=1):
    games = boards.shape[3]
    vmem = pl.BlockSpec(memory_space=pltpu.VMEM)
    return pl.pallas_call(
        functools.partial(actor_kernel, count, unroll),
        out_shape=jax.ShapeDtypeStruct((games, 400), jnp.float32),
        in_specs=[vmem] * 4,
        out_specs=vmem,
        scratch_shapes=[
            pltpu.VMEM((2, 1536, 256), jnp.bfloat16),
            pltpu.VMEM((12, 6, 2, games, 128), jnp.bfloat16),
            pltpu.VMEM((10, 5, 2, games, 128), jnp.bfloat16),
        ],
        compiler_params=pltpu.CompilerParams(vmem_limit_bytes=32 * 1024 * 1024),
        cost_estimate=pl.CostEstimate(
            flops=8 * 10**9, bytes_accessed=4 * 10**6, transcendentals=30000
        ),
        name="act",
    )(mine, other, boards, heads)


def column_of(row):
    size = row.shape[1]
    across = lax.broadcasted_iota(jnp.int32, (size, size), 1)
    down = lax.broadcasted_iota(jnp.int32, (size, size), 0)
    spread = jnp.broadcast_to(row, (size, size))
    return jnp.sum(jnp.where(across == down, spread, jnp.zeros_like(spread)), axis=1, keepdims=True)


def later(x, reach):
    return jnp.concatenate([x[reach:], jnp.zeros((reach, x.shape[1]), x.dtype)], axis=0)


def learner_kernel(
    count, length_in, boards_in, actions_in, behaviour_in, regular_in, rewards_in, weights_in,
    policy_in, value_in, own, next1, next2, next3,
    grad, length, boards, weights, actions, behaviour, regular, rewards, policy_t, value_t, pairs, back_pairs,
    middle, last, masks, slope, turned, done,
):
    slots = boards.shape[3]
    role = lax.axis_index("role")
    y = lax.axis_index("dp") // (LINE * LINE)
    moves = [
        (weights_in.at[0:ROWS], weights.at[0:ROWS]),
        (boards_in, inner_cells(boards)),
        (weights_in.at[ROWS : 2 * ROWS], weights.at[ROWS : 2 * ROWS]),
        (actions_in, actions),
        (behaviour_in, behaviour),
        (regular_in, regular),
        (rewards_in, rewards),
        (policy_in, policy_t),
        (value_in, value_t),
        (length_in, length),
    ]
    copies = [pltpu.make_async_copy(a, b, done.at[k]) for k, (a, b) in enumerate(moves)]
    for copy in copies:
        copy.start()
    clear_border(boards)
    copies[0].wait()

    for layer in range(2):
        if layer == 1:
            copies[2].wait()

        def kernel_of(p, q, layer=layer):
            at = layer * ROWS + (3 * p + q) * 128
            return weights[at : at + 128, :].astype(jnp.bfloat16)

        def store(block, value, layer=layer):
            pairs[layer, block * 128 : (block + 1) * 128, :] = value

        pair_kernels(kernel_of, store)
    clear_border(middle)
    clear_border(slope)
    copies[1].wait()

    def run_layer(layer, source, emit):
        for first in range(0, 10, count):
            pre = conv_pairs(source, pairs[layer], first, count)
            for parity in range(2):
                part = pre[:, parity * 128 : (parity + 1) * 128].reshape(count, 5, slots, 128)
                before = residual(source, first, count, parity).astype(jnp.float32)
                emit(first, parity, (before + jnp.maximum(part, 0.0)).astype(jnp.bfloat16))
                masks[layer, first : first + count, :, parity] = (part > 0).astype(jnp.bfloat16)

    run_layer(0, boards, lambda first, parity, value: put_cells(middle, first, count, parity, value))

    def to_last(first, parity, value):
        last[pl.ds(first, count), :, parity] = value

    run_layer(1, middle, to_last)

    for copy in copies[3:]:
        copy.wait()

    eight = jnp.concatenate(
        [
            policy_t[...].astype(jnp.float32),
            value_t[...].astype(jnp.float32),
            jnp.zeros((3, 128), jnp.float32),
        ],
        axis=0,
    )
    heads_t = jnp.concatenate(
        [eight, eight, eight, jnp.zeros((104, 128), jnp.float32)], axis=0
    ).astype(jnp.bfloat16)

    scores = lax.dot_general(
        last[...].reshape(-1, 128), heads_t, (((1,), (1,)), ((), ())),
        preferred_element_type=jnp.float32,
    ).reshape(100, slots, 128)
    lane = lax.broadcasted_iota(jnp.int32, (slots, 128), 1)
    weights_sum = jnp.sum(jnp.where(lane < 4, jnp.exp(scores), 0.0), axis=0)
    log_total = jnp.log(jnp.sum(weights_sum, axis=1, keepdims=True))
    action = column_of(actions[...])
    direction = action // 100
    cell = action - 100 * direction
    cells = lax.broadcasted_iota(jnp.int32, (100, slots, 128), 0)
    taken = (cells == cell[None]) & (lane % 8 == direction)[None]
    picked = jnp.sum(
        jnp.sum(jnp.where(taken & (lane < 4)[None], scores, 0.0), axis=0), axis=1, keepdims=True
    )
    value_sum = jnp.sum(scores, axis=0)
    value = jnp.tanh(
        jnp.sum(jnp.where(lane == 4, value_sum, 0.0), axis=1, keepdims=True) / 100.0
    )
    log_policy = picked - log_total

    positions = lax.broadcasted_iota(jnp.int32, (slots, 1), 0)
    live = (positions < length[0]).astype(jnp.float32)
    next_live = (positions + 1 < length[0]).astype(jnp.float32)
    ratio = jnp.minimum(1.0, jnp.exp(log_policy - column_of(behaviour[...])))
    shaped = column_of(rewards[...]) - ETA * (log_policy - column_of(regular[...]))
    next_values = later(value, 1) * next_live
    correction = live * ratio * (shaped + next_values - value)
    decay = live * ratio
    reach = 1
    while reach < slots:
        correction = correction + decay * later(correction, reach)
        decay = decay * later(decay, reach)
        reach *= 2
    targets = value + correction
    next_targets = later(targets, 1) * next_live
    policy_grad = -live * ratio * (shaped + next_targets - value)
    value_grad = -live * (targets - value)

    value_cell = value_grad * (1.0 - value * value) / 100.0
    by_policy = policy_grad[None] * (taken.astype(jnp.float32) - jnp.exp(scores - log_total[None]))
    by_score = jnp.where((lane % 8 == 4)[None], value_cell[None], by_policy)
    high = by_score.astype(jnp.bfloat16)
    rest = by_score - high.astype(jnp.float32)
    mid = rest.astype(jnp.bfloat16)
    low = rest - mid.astype(jnp.float32)
    parts = jnp.where(
        (lane < 8)[None],
        high.astype(jnp.float32),
        jnp.where((lane < 16)[None], mid.astype(jnp.float32), low),
    ).astype(jnp.bfloat16)
    out_grad = jnp.dot(
        parts.reshape(-1, 128), heads_t, preferred_element_type=jnp.float32
    )
    act_grad = (out_grad * masks[1].reshape(-1, 128).astype(jnp.float32)).astype(jnp.bfloat16)

    def kernel_of(p, q):
        at = ROWS + (8 - (3 * p + q)) * 128
        return weights[at : at + 128, :].T.astype(jnp.bfloat16)

    def store(block, value):
        back_pairs[block * 128 : (block + 1) * 128, :] = value

    pair_kernels(kernel_of, store)
    act_cells = act_grad.reshape(10, 5, 2, slots, 128)
    put_cells(slope, 0, 10, 0, act_cells[:, :, 0])
    put_cells(slope, 0, 10, 1, act_cells[:, :, 1])
    out_cells = out_grad.reshape(10, 5, 2, slots, 128)
    for first in range(0, 10, count):
        back = conv_pairs(slope, back_pairs[...], first, count)
        for parity in range(2):
            part = back[:, parity * 128 : (parity + 1) * 128].reshape(count, 5, slots, 128)
            total = out_cells[first : first + count, :, parity] + part
            gate = masks[0, first : first + count, :, parity].astype(jnp.float32)
            last[pl.ds(first, count), :, parity] = (total * gate).astype(jnp.bfloat16)
    turned[1] = act_grad.T
    turned[0] = last[...].reshape(-1, 128).T

    for core in range(2):

        @pl.when(role == core)
        def _(core=core):
            for layer, source in ((1, middle), (0, boards)):
                kept = []
                for offset in range(9):
                    parts = [x for x in segment_parts(layer, offset) if x[0] % 2 == core]
                    if parts:
                        kept.append((offset, parts))
                windows = []
                for offset, _ in kept:
                    p, q = offset // 3, offset % 3
                    cols = [source[p : p + 10, (j + q) // 2, (j + q) % 2] for j in range(10)]
                    windows.append(jnp.stack(cols, axis=1).reshape(-1, 128))
                for pair in range(0, len(kept), 2):
                    blocks = jnp.dot(
                        turned[layer],
                        jnp.concatenate(windows[pair : pair + 2], axis=1),
                        preferred_element_type=jnp.float32,
                    )
                    for k in range(2):
                        block = blocks[:, 128 * k : 128 * k + 128].T
                        for segment, first, end, at in kept[pair + k][1]:
                            grad[segment // 2, first:end] = block[at : at + end - first]

    sends = [
        pltpu.make_async_copy(grad.at[lax.rem(y + k, LINE)], out, done.at[k])
        for k, out in enumerate((own, next1, next2, next3))
    ]
    for copy in sends:
        copy.start()
    for copy in sends:
        copy.wait()


def learn(
    length, boards, actions, behaviour, regular, rewards, weights, policy_t, value_t, count=5
):
    slots = boards.shape[2]
    anywhere = pl.BlockSpec(memory_space=pltpu.HBM)
    cells = (10, 5, 2, slots, 128)
    around = (12, 6, 2, slots, 128)
    return pl.pallas_call(
        functools.partial(learner_kernel, count),
        out_shape=[jax.ShapeDtypeStruct((SEGMENT, 128), jnp.float32)] * LINE,
        in_specs=[anywhere] * 9,
        out_specs=[pl.BlockSpec(memory_space=pl.ANY)] * LINE,
        scratch_shapes=[
            pltpu.VMEM((LINE, SEGMENT, 128), jnp.float32),
            pltpu.SMEM((1,), jnp.int32),
            pltpu.VMEM(around, jnp.bfloat16),
            pltpu.VMEM((2 * ROWS, 128), jnp.float32),
            pltpu.VMEM((1, slots), jnp.int32),
            pltpu.VMEM((1, slots), jnp.float32),
            pltpu.VMEM((1, slots), jnp.float32),
            pltpu.VMEM((1, slots), jnp.float32),
            pltpu.VMEM(policy_t.shape, policy_t.dtype),
            pltpu.VMEM(value_t.shape, value_t.dtype),
            pltpu.VMEM((2, 1536, 256), jnp.bfloat16),
            pltpu.VMEM((1536, 256), jnp.bfloat16),
            pltpu.VMEM(around, jnp.bfloat16),
            pltpu.VMEM(cells, jnp.bfloat16),
            pltpu.VMEM((2,) + cells, jnp.bfloat16),
            pltpu.VMEM(around, jnp.bfloat16),
            pltpu.VMEM((2, 128, 100 * slots), jnp.bfloat16),
            pltpu.SemaphoreType.DMA((10,)),
        ],
        compiler_params=pltpu.CompilerParams(vmem_limit_bytes=60 * 1024 * 1024),
        cost_estimate=pl.CostEstimate(
            flops=4 * 10**9, bytes_accessed=3 * 10**6, transcendentals=10000
        ),
        name="learn",
    )(length, boards, actions, behaviour, regular, rewards, weights, policy_t, value_t)


def update_kernel(summed, squares, moments, torso_in, fresh, old, first, second, done):
    y = lax.axis_index("dp") // (LINE * LINE)
    start = pl.multiple_of((2 * y + lax.axis_index("role")) * SEGMENT, SEGMENT)
    fetch = pltpu.make_async_copy(torso_in.at[pl.ds(start, SEGMENT)], old, done)
    fetch.start()
    square_sum = jnp.sum(squares[...], axis=1, keepdims=True)
    factor = jnp.minimum(1.0, jnp.sqrt(256.0 * ROWS) / jnp.sqrt(square_sum + NORM_EPS))
    for x in range(2):
        for z in range(LINE):
            rows = slice((LINE * x + z) * PIECE, (LINE * x + z + 1) * PIECE)
            first[rows] = moments[z, x, 0:PIECE]
            second[rows] = moments[z, x, PIECE : 2 * PIECE]
    fetch.wait()
    clipped = summed[...] * factor
    moment_one = BETA_ONE * first[...] + (1.0 - BETA_ONE) * clipped
    moment_two = BETA_TWO * second[...] + (1.0 - BETA_TWO) * clipped * clipped
    fresh[...] = old[...] - LEARN_RATE * moment_one / (jnp.sqrt(moment_two) + ADAM_EPS)


def update(summed, squares, moments, torso):
    vmem = pl.BlockSpec(memory_space=pltpu.VMEM)
    rows = pltpu.VMEM((SEGMENT, 128), jnp.float32)
    return pl.pallas_call(
        update_kernel,
        out_shape=jax.ShapeDtypeStruct((SEGMENT, 128), jnp.float32),
        in_specs=[
            vmem, vmem, vmem, pl.BlockSpec(memory_space=pltpu.HBM)
        ],
        out_specs=vmem,
        scratch_shapes=[rows, rows, rows, pltpu.SemaphoreType.DMA],
        compiler_params=pltpu.CompilerParams(vmem_limit_bytes=16 * 1024 * 1024),
        name="update",
    )(summed, squares, moments, torso)


def shifted(x, axis, step):
    stride = {"y": LINE * LINE, "x": LINE, "z": 1}[axis]
    pairs = []
    for d in range(LINE**3):
        at = d // stride % LINE
        pairs.append((d, d + ((at + step) % LINE - at) * stride))
    return lax.ppermute(x, "dp", pairs)


def line_total(x, axis):
    return (x + shifted(x, axis, 2)) + (shifted(x, axis, 1) + shifted(x, axis, 3))


def line_scatter(chunks, axis):
    return (chunks[0] + shifted(chunks[2], axis, 2)) + (
        shifted(chunks[1], axis, 1) + shifted(chunks[3], axis, 3)
    )


def line_place(pieces, at):
    whole = jnp.zeros((LINE,) + pieces[0].shape, pieces[0].dtype)
    for step, piece in enumerate(pieces):
        whole = lax.dynamic_update_index_in_dim(whole, piece, (at - step) % LINE, 0)
    return whole


def line_gather(x, axis, at):
    return line_place([x] + [shifted(x, axis, step) for step in range(1, LINE)], at)


def role_swap(x):
    return lax.ppermute(x, "role", [(0, 1), (1, 0)])


def body(
    board_now,
    traj_boards,
    actions,
    lengths,
    behaviour,
    regular,
    rewards,
    torso,
    policy_head,
    value_head,
    first_moment,
    second_moment,
):
    role = lax.axis_index("role")
    dp = lax.axis_index("dp")
    y, x, z = dp // (LINE * LINE), dp // LINE % LINE, dp % LINE
    chunks = learn(
        lengths,
        by_cell(traj_boards[0]),
        actions,
        behaviour,
        regular,
        rewards,
        torso,
        policy_head.T,
        value_head[None],
    )
    chunks, moments = lax.optimization_barrier(
        (chunks, jnp.concatenate([first_moment, second_moment]))
    )
    moments = line_gather(moments, "x", x)
    moments = lax.dynamic_slice_in_dim(moments, 2 * role, 2, 0).reshape(-1, 128)
    moments = line_gather(moments, "z", z)
    summed = line_total(line_total(line_scatter(chunks, "y"), "x"), "z")
    squares = jnp.sum(summed * summed, axis=0, keepdims=True)
    squares = line_total(squares + role_swap(squares), "y")
    fresh = update(summed, squares, moments.reshape(LINE, 2, 2 * PIECE, 128), torso)
    mine = line_gather(fresh, "y", y)
    other = role_swap(mine)
    boards, heads = stage(mine, by_cell(board_now), policy_head.T.astype(jnp.float32))
    here = act(mine, other, boards, heads)
    there = role_swap(here)
    at = (LINE * x + z) % (2 * LINE) * PIECE
    new_share = jnp.where(
        role == x // 2,
        lax.dynamic_slice(mine, (y, at, 0), (1, PIECE, 128))[0],
        lax.dynamic_slice(other, (y, at, 0), (1, PIECE, 128))[0],
    )
    move_logp = jnp.concatenate([jnp.where(role == 0, here, there), jnp.where(role == 0, there, here)])
    return (new_share, move_logp)


def solution(mesh):
    return jax.shard_map(
        body,
        mesh=mesh,
        in_specs=(
            P("dp", None, None, None),
            P("dp", None, None, None, None),
            P("dp", None),
            P("dp"),
            P("dp", None),
            P("dp", None),
            P("dp", None),
            P(),
            P(),
            P(),
            P("dp", None),
            P("dp", None),
        ),
        out_specs=(P("dp", None), P("dp", None)),
        check_vma=False,
    )
```

```python
import functools

import jax
import jax.numpy as jnp
from jax import lax
from jax.experimental import pallas as pl
from jax.experimental.pallas import tpu as pltpu
from jax.sharding import PartitionSpec as P

ETA = 0.2
LEARN_RATE = 0.03
BETA_ONE = 0.9
BETA_TWO = 0.999
ADAM_EPS = 1e-08
NORM_EPS = 1e-12
ROWS = 1152
LINE = 4
SEGMENT = 2 * ROWS // (2 * LINE)
PIECE = SEGMENT // 8


def by_cell(boards):
    return jnp.transpose(boards, (1, 2, 0, 3))


def inner_cells(ref):
    return ref.reshape((12, 12) + ref.shape[3:]).at[1:11, 1:11]


def segment_parts(layer, offset):
    start = layer * ROWS + offset * 128
    at, parts = start, []
    while at < start + 128:
        segment = at // SEGMENT
        end = min(start + 128, (segment + 1) * SEGMENT)
        parts.append((segment, at - segment * SEGMENT, end - segment * SEGMENT, at - start))
        at = end
    return parts


def clear_border(ref):
    zero_row = jnp.zeros(ref.shape[1:], ref.dtype)
    ref[0] = zero_row
    ref[11] = zero_row
    zero_col = jnp.zeros((12,) + ref.shape[3:], ref.dtype)
    ref[:, 0, 0] = zero_col
    ref[:, 5, 1] = zero_col


def pair_kernels(kernel_of, store):
    nothing = jnp.zeros((128, 128), jnp.bfloat16)
    for p in range(3):
        row = [kernel_of(p, q) for q in range(3)]
        for q in range(4):
            left = row[q] if q < 3 else nothing
            right = row[q - 1] if q > 0 else nothing
            store(4 * p + q, jnp.concatenate([left, right], axis=1))


def conv_pairs(source, pair_weights, first, count):
    windows = []
    for p in range(3):
        for q in range(4):
            window = source[pl.ds(first + p, count), q // 2 : q // 2 + 5, q % 2]
            windows.append(window.reshape(-1, 128))
    return jnp.dot(
        jnp.concatenate(windows, axis=1), pair_weights, preferred_element_type=jnp.float32
    )


def residual(source, first, count, parity):
    if parity == 0:
        window = source[pl.ds(first + 1, count), 0:5, 1]
    else:
        window = source[pl.ds(first + 1, count), 1:6, 0]
    return window


def put_cells(target, first, count, parity, value):
    if parity == 0:
        target[pl.ds(first + 1, count), 0:5, 1] = value
    else:
        target[pl.ds(first + 1, count), 1:6, 0] = value


def stage_kernel(mine, boards_in, policy_t, boards, heads, done):
    games = boards.shape[3]
    half = pl.ds(pl.multiple_of(lax.axis_index("role") * games, games), games)
    fetch = pltpu.make_async_copy(boards_in.at[:, :, half], inner_cells(boards), done)
    fetch.start()
    clear_border(boards)
    spread = lax.broadcasted_iota(jnp.int32, (4, 1280), 1)
    row = lax.broadcasted_iota(jnp.int32, (4, 1280), 0)
    spread = (spread % 128 == 10 * row + spread // 128).astype(jnp.float32)
    by_column = lax.dot_general(
        policy_t[...], spread, (((0,), (0,)), ((), ())), preferred_element_type=jnp.float32
    )
    for j in range(10):
        heads[128 * j : 128 * j + 128, :] = by_column[:, 128 * j : 128 * j + 128].astype(jnp.bfloat16)
    fetch.wait()


def stage(mine, boards, policy_t):
    games = boards.shape[2] // 2
    vmem = pl.BlockSpec(memory_space=pltpu.VMEM)
    anywhere = pl.BlockSpec(memory_space=pltpu.HBM)
    return pl.pallas_call(
        stage_kernel,
        out_shape=[
            jax.ShapeDtypeStruct((12, 6, 2, games, 128), jnp.bfloat16),
            jax.ShapeDtypeStruct((1280, 128), jnp.bfloat16),
        ],
        in_specs=[anywhere, anywhere, vmem],
        out_specs=[vmem, vmem],
        scratch_shapes=[pltpu.SemaphoreType.DMA],
        compiler_params=pltpu.CompilerParams(vmem_limit_bytes=16 * 1024 * 1024),
        cost_estimate=pl.CostEstimate(
            flops=10**9, bytes_accessed=4 * 10**6, transcendentals=0
        ),
        name="stage",
    )(mine, boards, policy_t)


def actor_kernel(count, unroll, mine, other, boards, heads, out, pairs, middle, last):
    games = boards.shape[3]
    role = lax.axis_index("role")
    for layer in range(2):
        def kernel_of(p, q, layer=layer):
            parts = []
            for segment, first, last_row, _ in segment_parts(layer, 3 * p + q):
                y, owner = segment // 2, segment % 2
                rows = slice(first, last_row)
                parts.append(jnp.where(role == owner, mine[y, rows], other[y, rows]))
            return jnp.concatenate(parts, axis=0).astype(jnp.bfloat16)

        def store(block, value, layer=layer):
            pairs[layer, block * 128 : (block + 1) * 128, :] = value

        pair_kernels(kernel_of, store)
    clear_border(middle)

    def run_layer(layer, source, emit):
        def step(at, carry):
            first = at * count
            pre = conv_pairs(source, pairs[layer], first, count)
            for parity in range(2):
                part = pre[:, parity * 128 : (parity + 1) * 128].reshape(count, 5, games, 128)
                before = residual(source, first, count, parity).astype(jnp.float32)
                emit(first, parity, (before + jnp.maximum(part, 0.0)).astype(jnp.bfloat16))
            return carry

        lax.fori_loop(0, 10 // count, step, 0, unroll=unroll)

    run_layer(0, boards, lambda first, parity, value: put_cells(middle, first, count, parity, value))

    def to_last(first, parity, value):
        last[pl.ds(first, count), :, parity] = value

    run_layer(1, middle, to_last)
    cells = [last[:, j // 2, j % 2].reshape(-1, 128) for j in range(10)]
    logits = jnp.dot(jnp.concatenate(cells, axis=1), heads[...], preferred_element_type=jnp.float32)
    logits = logits.reshape(10, games, 128)
    lanes = lax.broadcasted_iota(jnp.int32, (games, 128), 1)
    moves = []
    total = jnp.zeros((games, 1), jnp.float32)
    for d in range(4):
        gathered = jnp.zeros((games, 128), jnp.float32)
        for i in range(10):
            turned = pltpu.roll(logits[i], (10 * i - 10 * d) % 128, 1)
            gathered = jnp.where((lanes >= 10 * i) & (lanes < 10 * i + 10), turned, gathered)
        moves.append(gathered)
        total = total + jnp.sum(
            jnp.where(lanes < 100, jnp.exp(gathered), 0.0), axis=1, keepdims=True
        )
    log_total = jnp.log(total)
    for d in range(4):
        out[:, 100 * d : 100 * d + 100] = (moves[d] - log_total)[:, :100]


def act(mine, other, boards, heads, count=2, unroll=1):
    games = boards.shape[3]
    vmem = pl.BlockSpec(memory_space=pltpu.VMEM)
    return pl.pallas_call(
        functools.partial(actor_kernel, count, unroll),
        out_shape=jax.ShapeDtypeStruct((games, 400), jnp.float32),
        in_specs=[vmem] * 4,
        out_specs=vmem,
        scratch_shapes=[
            pltpu.VMEM((2, 1536, 256), jnp.bfloat16),
            pltpu.VMEM((12, 6, 2, games, 128), jnp.bfloat16),
            pltpu.VMEM((10, 5, 2, games, 128), jnp.bfloat16),
        ],
        compiler_params=pltpu.CompilerParams(vmem_limit_bytes=32 * 1024 * 1024),
        cost_estimate=pl.CostEstimate(
            flops=8 * 10**9, bytes_accessed=4 * 10**6, transcendentals=30000
        ),
        name="act",
    )(mine, other, boards, heads)


def column_of(row):
    size = row.shape[1]
    across = lax.broadcasted_iota(jnp.int32, (size, size), 1)
    down = lax.broadcasted_iota(jnp.int32, (size, size), 0)
    spread = jnp.broadcast_to(row, (size, size))
    return jnp.sum(jnp.where(across == down, spread, jnp.zeros_like(spread)), axis=1, keepdims=True)


def later(x, reach):
    return jnp.concatenate([x[reach:], jnp.zeros((reach, x.shape[1]), x.dtype)], axis=0)


def learner_kernel(
    count, first_in, second_in, length_in, boards_in, actions_in, behaviour_in, regular_in, rewards_in, weights_in,
    policy_in, value_in, own, next1, next2, next3, both,
    first, second, grad, length, boards, weights, actions, behaviour, regular, rewards, policy_t, value_t, pairs, back_pairs,
    middle, last, masks, slope, turned, done,
):
    slots = boards.shape[3]
    role = lax.axis_index("role")
    y = lax.axis_index("dp") // (LINE * LINE)
    moves = [
        (weights_in.at[0:ROWS], weights.at[0:ROWS]),
        (boards_in, inner_cells(boards)),
        (weights_in.at[ROWS : 2 * ROWS], weights.at[ROWS : 2 * ROWS]),
        (actions_in, actions),
        (behaviour_in, behaviour),
        (regular_in, regular),
        (rewards_in, rewards),
        (policy_in, policy_t),
        (value_in, value_t),
        (length_in, length),
        (first_in, first),
        (second_in, second),
    ]
    copies = [pltpu.make_async_copy(a, b, done.at[k]) for k, (a, b) in enumerate(moves)]
    for copy in copies:
        copy.start()
    clear_border(boards)
    copies[0].wait()

    for layer in range(2):
        if layer == 1:
            copies[2].wait()

        def kernel_of(p, q, layer=layer):
            at = layer * ROWS + (3 * p + q) * 128
            return weights[at : at + 128, :].astype(jnp.bfloat16)

        def store(block, value, layer=layer):
            pairs[layer, block * 128 : (block + 1) * 128, :] = value

        pair_kernels(kernel_of, store)
    clear_border(middle)
    clear_border(slope)
    copies[1].wait()

    def run_layer(layer, source, emit):
        for first in range(0, 10, count):
            pre = conv_pairs(source, pairs[layer], first, count)
            for parity in range(2):
                part = pre[:, parity * 128 : (parity + 1) * 128].reshape(count, 5, slots, 128)
                before = residual(source, first, count, parity).astype(jnp.float32)
                emit(first, parity, (before + jnp.maximum(part, 0.0)).astype(jnp.bfloat16))
                masks[layer, first : first + count, :, parity] = (part > 0).astype(jnp.bfloat16)

    run_layer(0, boards, lambda first, parity, value: put_cells(middle, first, count, parity, value))

    def to_last(first, parity, value):
        last[pl.ds(first, count), :, parity] = value

    run_layer(1, middle, to_last)

    for copy in copies[3:]:
        copy.wait()
    both[0:PIECE] = first[...]
    both[PIECE : 2 * PIECE] = second[...]

    eight = jnp.concatenate(
        [
            policy_t[...].astype(jnp.float32),
            value_t[...].astype(jnp.float32),
            jnp.zeros((3, 128), jnp.float32),
        ],
        axis=0,
    )
    heads_t = jnp.concatenate(
        [eight, eight, eight, jnp.zeros((104, 128), jnp.float32)], axis=0
    ).astype(jnp.bfloat16)

    scores = lax.dot_general(
        last[...].reshape(-1, 128), heads_t, (((1,), (1,)), ((), ())),
        preferred_element_type=jnp.float32,
    ).reshape(100, slots, 128)
    lane = lax.broadcasted_iota(jnp.int32, (slots, 128), 1)
    weights_sum = jnp.sum(jnp.where(lane < 4, jnp.exp(scores), 0.0), axis=0)
    log_total = jnp.log(jnp.sum(weights_sum, axis=1, keepdims=True))
    action = column_of(actions[...])
    direction = action // 100
    cell = action - 100 * direction
    cells = lax.broadcasted_iota(jnp.int32, (100, slots, 128), 0)
    taken = (cells == cell[None]) & (lane % 8 == direction)[None]
    picked = jnp.sum(
        jnp.sum(jnp.where(taken & (lane < 4)[None], scores, 0.0), axis=0), axis=1, keepdims=True
    )
    value_sum = jnp.sum(scores, axis=0)
    value = jnp.tanh(
        jnp.sum(jnp.where(lane == 4, value_sum, 0.0), axis=1, keepdims=True) / 100.0
    )
    log_policy = picked - log_total

    positions = lax.broadcasted_iota(jnp.int32, (slots, 1), 0)
    live = (positions < length[0]).astype(jnp.float32)
    next_live = (positions + 1 < length[0]).astype(jnp.float32)
    ratio = jnp.minimum(1.0, jnp.exp(log_policy - column_of(behaviour[...])))
    shaped = column_of(rewards[...]) - ETA * (log_policy - column_of(regular[...]))
    next_values = later(value, 1) * next_live
    correction = live * ratio * (shaped + next_values - value)
    decay = live * ratio
    reach = 1
    while reach < slots:
        correction = correction + decay * later(correction, reach)
        decay = decay * later(decay, reach)
        reach *= 2
    targets = value + correction
    next_targets = later(targets, 1) * next_live
    policy_grad = -live * ratio * (shaped + next_targets - value)
    value_grad = -live * (targets - value)

    value_cell = value_grad * (1.0 - value * value) / 100.0
    by_policy = policy_grad[None] * (taken.astype(jnp.float32) - jnp.exp(scores - log_total[None]))
    by_score = jnp.where((lane % 8 == 4)[None], value_cell[None], by_policy)
    high = by_score.astype(jnp.bfloat16)
    rest = by_score - high.astype(jnp.float32)
    mid = rest.astype(jnp.bfloat16)
    low = rest - mid.astype(jnp.float32)
    parts = jnp.where(
        (lane < 8)[None],
        high.astype(jnp.float32),
        jnp.where((lane < 16)[None], mid.astype(jnp.float32), low),
    ).astype(jnp.bfloat16)
    out_grad = jnp.dot(
        parts.reshape(-1, 128), heads_t, preferred_element_type=jnp.float32
    )
    act_grad = (out_grad * masks[1].reshape(-1, 128).astype(jnp.float32)).astype(jnp.bfloat16)

    def kernel_of(p, q):
        at = ROWS + (8 - (3 * p + q)) * 128
        return weights[at : at + 128, :].T.astype(jnp.bfloat16)

    def store(block, value):
        back_pairs[block * 128 : (block + 1) * 128, :] = value

    pair_kernels(kernel_of, store)
    act_cells = act_grad.reshape(10, 5, 2, slots, 128)
    put_cells(slope, 0, 10, 0, act_cells[:, :, 0])
    put_cells(slope, 0, 10, 1, act_cells[:, :, 1])
    out_cells = out_grad.reshape(10, 5, 2, slots, 128)
    for first in range(0, 10, count):
        back = conv_pairs(slope, back_pairs[...], first, count)
        for parity in range(2):
            part = back[:, parity * 128 : (parity + 1) * 128].reshape(count, 5, slots, 128)
            total = out_cells[first : first + count, :, parity] + part
            gate = masks[0, first : first + count, :, parity].astype(jnp.float32)
            last[pl.ds(first, count), :, parity] = (total * gate).astype(jnp.bfloat16)
    turned[1] = act_grad.T
    turned[0] = last[...].reshape(-1, 128).T

    for core in range(2):

        @pl.when(role == core)
        def _(core=core):
            for layer, source in ((1, middle), (0, boards)):
                kept = []
                for offset in range(9):
                    parts = [x for x in segment_parts(layer, offset) if x[0] % 2 == core]
                    if parts:
                        kept.append((offset, parts))
                windows = []
                for offset, _ in kept:
                    p, q = offset // 3, offset % 3
                    cols = [source[p : p + 10, (j + q) // 2, (j + q) % 2] for j in range(10)]
                    windows.append(jnp.stack(cols, axis=1).reshape(-1, 128))
                for pair in range(0, len(kept), 2):
                    blocks = jnp.dot(
                        turned[layer],
                        jnp.concatenate(windows[pair : pair + 2], axis=1),
                        preferred_element_type=jnp.float32,
                    )
                    for k in range(2):
                        block = blocks[:, 128 * k : 128 * k + 128].T
                        for segment, first, end, at in kept[pair + k][1]:
                            grad[segment // 2, first:end] = block[at : at + end - first]

    sends = [
        pltpu.make_async_copy(grad.at[lax.rem(y + k, LINE)], out, done.at[k])
        for k, out in ((1, next1), (2, next2), (3, next3))
    ]
    for copy in sends:
        copy.start()
    own[...] = grad[y]
    for copy in sends:
        copy.wait()


def learn(
    first, second, length, boards, actions, behaviour, regular, rewards, weights, policy_t, value_t,
    count=5,
):
    slots = boards.shape[2]
    vmem = pl.BlockSpec(memory_space=pltpu.VMEM)
    anywhere = pl.BlockSpec(memory_space=pltpu.HBM)
    cells = (10, 5, 2, slots, 128)
    around = (12, 6, 2, slots, 128)
    return pl.pallas_call(
        functools.partial(learner_kernel, count),
        out_shape=[jax.ShapeDtypeStruct((SEGMENT, 128), jnp.float32)] * LINE
        + [jax.ShapeDtypeStruct((2 * PIECE, 128), jnp.float32)],
        in_specs=[anywhere] * 11,
        out_specs=[vmem] + [anywhere] * (LINE - 1) + [vmem],
        scratch_shapes=[
            pltpu.VMEM((PIECE, 128), jnp.float32),
            pltpu.VMEM((PIECE, 128), jnp.float32),
            pltpu.VMEM((LINE, SEGMENT, 128), jnp.float32),
            pltpu.SMEM((1,), jnp.int32),
            pltpu.VMEM(around, jnp.bfloat16),
            pltpu.VMEM((2 * ROWS, 128), jnp.float32),
            pltpu.VMEM((1, slots), jnp.int32),
            pltpu.VMEM((1, slots), jnp.float32),
            pltpu.VMEM((1, slots), jnp.float32),
            pltpu.VMEM((1, slots), jnp.float32),
            pltpu.VMEM(policy_t.shape, policy_t.dtype),
            pltpu.VMEM(value_t.shape, value_t.dtype),
            pltpu.VMEM((2, 1536, 256), jnp.bfloat16),
            pltpu.VMEM((1536, 256), jnp.bfloat16),
            pltpu.VMEM(around, jnp.bfloat16),
            pltpu.VMEM(cells, jnp.bfloat16),
            pltpu.VMEM((2,) + cells, jnp.bfloat16),
            pltpu.VMEM(around, jnp.bfloat16),
            pltpu.VMEM((2, 128, 100 * slots), jnp.bfloat16),
            pltpu.SemaphoreType.DMA((12,)),
        ],
        compiler_params=pltpu.CompilerParams(vmem_limit_bytes=60 * 1024 * 1024),
        cost_estimate=pl.CostEstimate(
            flops=4 * 10**9, bytes_accessed=3 * 10**6, transcendentals=10000
        ),
        name="learn",
    )(first, second, length, boards, actions, behaviour, regular, rewards, weights, policy_t, value_t)


def update_kernel(summed, squares, moments, torso_in, fresh, old, first, second, done):
    y = lax.axis_index("dp") // (LINE * LINE)
    start = pl.multiple_of((2 * y + lax.axis_index("role")) * SEGMENT, SEGMENT)
    fetch = pltpu.make_async_copy(torso_in.at[pl.ds(start, SEGMENT)], old, done)
    fetch.start()
    square_sum = jnp.sum(squares[...], axis=1, keepdims=True)
    factor = jnp.minimum(1.0, jnp.sqrt(256.0 * ROWS) / jnp.sqrt(square_sum + NORM_EPS))
    for x in range(2):
        for z in range(LINE):
            rows = slice((LINE * x + z) * PIECE, (LINE * x + z + 1) * PIECE)
            first[rows] = moments[z, x, 0:PIECE]
            second[rows] = moments[z, x, PIECE : 2 * PIECE]
    fetch.wait()
    clipped = summed[...] * factor
    moment_one = BETA_ONE * first[...] + (1.0 - BETA_ONE) * clipped
    moment_two = BETA_TWO * second[...] + (1.0 - BETA_TWO) * clipped * clipped
    fresh[...] = old[...] - LEARN_RATE * moment_one / (jnp.sqrt(moment_two) + ADAM_EPS)


def update(summed, squares, moments, torso):
    vmem = pl.BlockSpec(memory_space=pltpu.VMEM)
    rows = pltpu.VMEM((SEGMENT, 128), jnp.float32)
    return pl.pallas_call(
        update_kernel,
        out_shape=jax.ShapeDtypeStruct((SEGMENT, 128), jnp.float32),
        in_specs=[
            vmem, vmem, vmem, pl.BlockSpec(memory_space=pltpu.HBM)
        ],
        out_specs=vmem,
        scratch_shapes=[rows, rows, rows, pltpu.SemaphoreType.DMA],
        compiler_params=pltpu.CompilerParams(vmem_limit_bytes=16 * 1024 * 1024),
        name="update",
    )(summed, squares, moments, torso)


def shifted(x, axis, step):
    stride = {"y": LINE * LINE, "x": LINE, "z": 1}[axis]
    pairs = []
    for d in range(LINE**3):
        at = d // stride % LINE
        pairs.append((d, d + ((at + step) % LINE - at) * stride))
    return lax.ppermute(x, "dp", pairs)


def line_total(x, axis):
    return (x + shifted(x, axis, 2)) + (shifted(x, axis, 1) + shifted(x, axis, 3))


def line_scatter(chunks, axis):
    return (chunks[0] + shifted(chunks[2], axis, 2)) + (
        shifted(chunks[1], axis, 1) + shifted(chunks[3], axis, 3)
    )


def line_place(pieces, at):
    whole = jnp.zeros((LINE,) + pieces[0].shape, pieces[0].dtype)
    for step, piece in enumerate(pieces):
        whole = lax.dynamic_update_index_in_dim(whole, piece, (at - step) % LINE, 0)
    return whole


def line_gather(x, axis, at):
    return line_place([x] + [shifted(x, axis, step) for step in range(1, LINE)], at)


def line_exchange(summed, moments, axis, at):
    rows = summed.shape[0]
    both = jnp.concatenate([summed, moments])
    got = [both] + [shifted(both, axis, step) for step in range(1, LINE)]
    total = (got[0][:rows] + got[2][:rows]) + (got[1][:rows] + got[3][:rows])
    return total, line_place([x[rows:] for x in got], at)


def swapped_z(x, bit):
    return lax.ppermute(x, "dp", [(d, d ^ bit) for d in range(LINE**3)])


def moments_along_z(x, z):
    near = swapped_z(x, 1)
    pair = jnp.where(z % 2 == 0, jnp.stack([x, near]), jnp.stack([near, x]))
    far = swapped_z(pair, 2)
    return jnp.where(z < 2, jnp.concatenate([pair, far]), jnp.concatenate([far, pair]))


def role_swap(x):
    return lax.ppermute(x, "role", [(0, 1), (1, 0)])


def body(
    board_now,
    traj_boards,
    actions,
    lengths,
    behaviour,
    regular,
    rewards,
    torso,
    policy_head,
    value_head,
    first_moment,
    second_moment,
):
    role = lax.axis_index("role")
    dp = lax.axis_index("dp")
    y, x, z = dp // (LINE * LINE), dp // LINE % LINE, dp % LINE
    own, next1, next2, next3, moments = learn(
        first_moment,
        second_moment,
        lengths,
        by_cell(traj_boards[0]),
        actions,
        behaviour,
        regular,
        rewards,
        torso,
        policy_head.T,
        value_head[None],
    )
    summed = line_scatter((own, next1, next2, next3), "y")
    summed, moments = line_exchange(summed, moments, "x", x)
    moments = lax.dynamic_slice_in_dim(moments, 2 * role, 2, 0).reshape(-1, 128)
    moments = moments_along_z(moments, z)
    summed = line_total(summed, "z")
    squares = jnp.sum(summed * summed, axis=0, keepdims=True)
    squares = line_total(squares + role_swap(squares), "y")
    fresh = update(summed, squares, moments.reshape(LINE, 2, 2 * PIECE, 128), torso)
    mine = line_gather(fresh, "y", y)
    other = role_swap(mine)
    boards, heads = stage(mine, by_cell(board_now), policy_head.T.astype(jnp.float32))
    here = act(mine, other, boards, heads)
    there = role_swap(here)
    at = (LINE * x + z) % (2 * LINE) * PIECE
    new_share = jnp.where(
        role == x // 2,
        lax.dynamic_slice(mine, (y, at, 0), (1, PIECE, 128))[0],
        lax.dynamic_slice(other, (y, at, 0), (1, PIECE, 128))[0],
    )
    move_logp = jnp.concatenate([jnp.where(role == 0, here, there), jnp.where(role == 0, there, here)])
    return (new_share, move_logp)


def solution(mesh):
    return jax.shard_map(
        body,
        mesh=mesh,
        in_specs=(
            P("dp", None, None, None),
            P("dp", None, None, None, None),
            P("dp", None),
            P("dp"),
            P("dp", None),
            P("dp", None),
            P("dp", None),
            P(),
            P(),
            P(),
            P("dp", None),
            P("dp", None),
        ),
        out_specs=(P("dp", None), P("dp", None)),
        check_vma=False,
    )
```

```python
import functools

import jax
import jax.numpy as jnp
from jax import lax
from jax.experimental import pallas as pl
from jax.experimental.pallas import tpu as pltpu
from jax.sharding import PartitionSpec as P

ETA = 0.2
LEARN_RATE = 0.03
BETA_ONE = 0.9
BETA_TWO = 0.999
ADAM_EPS = 1e-08
NORM_EPS = 1e-12
ROWS = 1152
LINE = 4
SEGMENT = 2 * ROWS // (2 * LINE)
PIECE = SEGMENT // 8


def by_cell(boards):
    return jnp.transpose(boards, (1, 2, 0, 3))


def inner_cells(ref):
    return ref.reshape((12, 12) + ref.shape[3:]).at[1:11, 1:11]


def segment_parts(layer, offset):
    start = layer * ROWS + offset * 128
    at, parts = start, []
    while at < start + 128:
        segment = at // SEGMENT
        end = min(start + 128, (segment + 1) * SEGMENT)
        parts.append((segment, at - segment * SEGMENT, end - segment * SEGMENT, at - start))
        at = end
    return parts


def clear_border(ref):
    zero_row = jnp.zeros(ref.shape[1:], ref.dtype)
    ref[0] = zero_row
    ref[11] = zero_row
    zero_col = jnp.zeros((12,) + ref.shape[3:], ref.dtype)
    ref[:, 0, 0] = zero_col
    ref[:, 5, 1] = zero_col


def pair_kernels(kernel_of, store):
    nothing = jnp.zeros((128, 128), jnp.bfloat16)
    for p in range(3):
        row = [kernel_of(p, q) for q in range(3)]
        for q in range(4):
            left = row[q] if q < 3 else nothing
            right = row[q - 1] if q > 0 else nothing
            store(4 * p + q, jnp.concatenate([left, right], axis=1))


def conv_pairs(source, pair_weights, first, count):
    windows = []
    for p in range(3):
        for q in range(4):
            window = source[pl.ds(first + p, count), q // 2 : q // 2 + 5, q % 2]
            windows.append(window.reshape(-1, 128))
    return jnp.dot(
        jnp.concatenate(windows, axis=1), pair_weights, preferred_element_type=jnp.float32
    )


def residual(source, first, count, parity):
    if parity == 0:
        window = source[pl.ds(first + 1, count), 0:5, 1]
    else:
        window = source[pl.ds(first + 1, count), 1:6, 0]
    return window


def put_cells(target, first, count, parity, value):
    if parity == 0:
        target[pl.ds(first + 1, count), 0:5, 1] = value
    else:
        target[pl.ds(first + 1, count), 1:6, 0] = value


def stage_kernel(mine, boards_in, policy_t, boards, heads, done):
    games = boards.shape[3]
    half = pl.ds(pl.multiple_of(lax.axis_index("role") * games, games), games)
    fetch = pltpu.make_async_copy(boards_in.at[:, :, half], inner_cells(boards), done)
    fetch.start()
    clear_border(boards)
    spread = lax.broadcasted_iota(jnp.int32, (4, 1280), 1)
    row = lax.broadcasted_iota(jnp.int32, (4, 1280), 0)
    spread = (spread % 128 == 10 * row + spread // 128).astype(jnp.float32)
    by_column = lax.dot_general(
        policy_t[...], spread, (((0,), (0,)), ((), ())), preferred_element_type=jnp.float32
    )
    for j in range(10):
        heads[128 * j : 128 * j + 128, :] = by_column[:, 128 * j : 128 * j + 128].astype(jnp.bfloat16)
    fetch.wait()


def stage(mine, boards, policy_t):
    games = boards.shape[2] // 2
    vmem = pl.BlockSpec(memory_space=pltpu.VMEM)
    anywhere = pl.BlockSpec(memory_space=pltpu.HBM)
    return pl.pallas_call(
        stage_kernel,
        out_shape=[
            jax.ShapeDtypeStruct((12, 6, 2, games, 128), jnp.bfloat16),
            jax.ShapeDtypeStruct((1280, 128), jnp.bfloat16),
        ],
        in_specs=[anywhere, anywhere, vmem],
        out_specs=[vmem, vmem],
        scratch_shapes=[pltpu.SemaphoreType.DMA],
        compiler_params=pltpu.CompilerParams(vmem_limit_bytes=16 * 1024 * 1024),
        cost_estimate=pl.CostEstimate(
            flops=10**9, bytes_accessed=4 * 10**6, transcendentals=0
        ),
        name="stage",
    )(mine, boards, policy_t)


def actor_kernel(count, unroll, mine, other, boards, heads, out, pairs, middle, last):
    games = boards.shape[3]
    role = lax.axis_index("role")
    for layer in range(2):
        def kernel_of(p, q, layer=layer):
            parts = []
            for segment, first, last_row, _ in segment_parts(layer, 3 * p + q):
                y, owner = segment // 2, segment % 2
                rows = slice(first, last_row)
                parts.append(jnp.where(role == owner, mine[y, rows], other[y, rows]))
            return jnp.concatenate(parts, axis=0).astype(jnp.bfloat16)

        def store(block, value, layer=layer):
            pairs[layer, block * 128 : (block + 1) * 128, :] = value

        pair_kernels(kernel_of, store)
    clear_border(middle)

    def run_layer(layer, source, emit):
        def step(at, carry):
            first = at * count
            pre = conv_pairs(source, pairs[layer], first, count)
            for parity in range(2):
                part = pre[:, parity * 128 : (parity + 1) * 128].reshape(count, 5, games, 128)
                before = residual(source, first, count, parity).astype(jnp.float32)
                emit(first, parity, (before + jnp.maximum(part, 0.0)).astype(jnp.bfloat16))
            return carry

        lax.fori_loop(0, 10 // count, step, 0, unroll=unroll)

    run_layer(0, boards, lambda first, parity, value: put_cells(middle, first, count, parity, value))

    def to_last(first, parity, value):
        last[pl.ds(first, count), :, parity] = value

    run_layer(1, middle, to_last)
    cells = [last[:, j // 2, j % 2].reshape(-1, 128) for j in range(10)]
    logits = jnp.dot(jnp.concatenate(cells, axis=1), heads[...], preferred_element_type=jnp.float32)
    logits = logits.reshape(10, games, 128)
    lanes = lax.broadcasted_iota(jnp.int32, (games, 128), 1)
    moves = []
    total = jnp.zeros((games, 1), jnp.float32)
    for d in range(4):
        gathered = jnp.zeros((games, 128), jnp.float32)
        for i in range(10):
            turned = pltpu.roll(logits[i], (10 * i - 10 * d) % 128, 1)
            gathered = jnp.where((lanes >= 10 * i) & (lanes < 10 * i + 10), turned, gathered)
        moves.append(gathered)
        total = total + jnp.sum(
            jnp.where(lanes < 100, jnp.exp(gathered), 0.0), axis=1, keepdims=True
        )
    log_total = jnp.log(total)
    for d in range(4):
        out[:, 100 * d : 100 * d + 100] = (moves[d] - log_total)[:, :100]


def act(mine, other, boards, heads, count=2, unroll=1):
    games = boards.shape[3]
    vmem = pl.BlockSpec(memory_space=pltpu.VMEM)
    return pl.pallas_call(
        functools.partial(actor_kernel, count, unroll),
        out_shape=jax.ShapeDtypeStruct((games, 400), jnp.float32),
        in_specs=[vmem] * 4,
        out_specs=vmem,
        scratch_shapes=[
            pltpu.VMEM((2, 1536, 256), jnp.bfloat16),
            pltpu.VMEM((12, 6, 2, games, 128), jnp.bfloat16),
            pltpu.VMEM((10, 5, 2, games, 128), jnp.bfloat16),
        ],
        compiler_params=pltpu.CompilerParams(vmem_limit_bytes=32 * 1024 * 1024),
        cost_estimate=pl.CostEstimate(
            flops=8 * 10**9, bytes_accessed=4 * 10**6, transcendentals=30000
        ),
        name="act",
    )(mine, other, boards, heads)


def column_of(row):
    size = row.shape[1]
    across = lax.broadcasted_iota(jnp.int32, (size, size), 1)
    down = lax.broadcasted_iota(jnp.int32, (size, size), 0)
    spread = jnp.broadcast_to(row, (size, size))
    return jnp.sum(jnp.where(across == down, spread, jnp.zeros_like(spread)), axis=1, keepdims=True)


def later(x, reach):
    return jnp.concatenate([x[reach:], jnp.zeros((reach, x.shape[1]), x.dtype)], axis=0)


def learner_kernel(
    count, length_in, boards_in, actions_in, behaviour_in, regular_in, rewards_in, weights_in,
    policy_in, value_in, own, next1, next2, next3,
    grad, length, boards, weights, actions, behaviour, regular, rewards, policy_t, value_t, pairs, back_pairs,
    middle, last, masks, slope, turned, done,
):
    slots = boards.shape[3]
    role = lax.axis_index("role")
    y = lax.axis_index("dp") // (LINE * LINE)
    moves = [
        (weights_in.at[0:ROWS], weights.at[0:ROWS]),
        (boards_in, inner_cells(boards)),
        (weights_in.at[ROWS : 2 * ROWS], weights.at[ROWS : 2 * ROWS]),
        (actions_in, actions),
        (behaviour_in, behaviour),
        (regular_in, regular),
        (rewards_in, rewards),
        (policy_in, policy_t),
        (value_in, value_t),
        (length_in, length),
    ]
    copies = [pltpu.make_async_copy(a, b, done.at[k]) for k, (a, b) in enumerate(moves)]
    for copy in copies:
        copy.start()
    clear_border(boards)
    copies[0].wait()

    for layer in range(2):
        if layer == 1:
            copies[2].wait()

        def kernel_of(p, q, layer=layer):
            at = layer * ROWS + (3 * p + q) * 128
            return weights[at : at + 128, :].astype(jnp.bfloat16)

        def store(block, value, layer=layer):
            pairs[layer, block * 128 : (block + 1) * 128, :] = value

        pair_kernels(kernel_of, store)
    clear_border(middle)
    clear_border(slope)
    copies[1].wait()

    def run_layer(layer, source, emit):
        for first in range(0, 10, count):
            pre = conv_pairs(source, pairs[layer], first, count)
            for parity in range(2):
                part = pre[:, parity * 128 : (parity + 1) * 128].reshape(count, 5, slots, 128)
                before = residual(source, first, count, parity).astype(jnp.float32)
                emit(first, parity, (before + jnp.maximum(part, 0.0)).astype(jnp.bfloat16))
                masks[layer, first : first + count, :, parity] = (part > 0).astype(jnp.bfloat16)

    run_layer(0, boards, lambda first, parity, value: put_cells(middle, first, count, parity, value))

    def to_last(first, parity, value):
        last[pl.ds(first, count), :, parity] = value

    run_layer(1, middle, to_last)

    for copy in copies[3:]:
        copy.wait()

    eight = jnp.concatenate(
        [
            policy_t[...].astype(jnp.float32),
            value_t[...].astype(jnp.float32),
            jnp.zeros((3, 128), jnp.float32),
        ],
        axis=0,
    )
    heads_t = jnp.concatenate(
        [eight, eight, eight, jnp.zeros((104, 128), jnp.float32)], axis=0
    ).astype(jnp.bfloat16)

    scores = lax.dot_general(
        last[...].reshape(-1, 128), heads_t, (((1,), (1,)), ((), ())),
        preferred_element_type=jnp.float32,
    ).reshape(100, slots, 128)
    lane = lax.broadcasted_iota(jnp.int32, (slots, 128), 1)
    weights_sum = jnp.sum(jnp.where(lane < 4, jnp.exp(scores), 0.0), axis=0)
    log_total = jnp.log(jnp.sum(weights_sum, axis=1, keepdims=True))
    action = column_of(actions[...])
    direction = action // 100
    cell = action - 100 * direction
    cells = lax.broadcasted_iota(jnp.int32, (100, slots, 128), 0)
    taken = (cells == cell[None]) & (lane % 8 == direction)[None]
    picked = jnp.sum(
        jnp.sum(jnp.where(taken & (lane < 4)[None], scores, 0.0), axis=0), axis=1, keepdims=True
    )
    value_sum = jnp.sum(scores, axis=0)
    value = jnp.tanh(
        jnp.sum(jnp.where(lane == 4, value_sum, 0.0), axis=1, keepdims=True) / 100.0
    )
    log_policy = picked - log_total

    positions = lax.broadcasted_iota(jnp.int32, (slots, 1), 0)
    live = (positions < length[0]).astype(jnp.float32)
    next_live = (positions + 1 < length[0]).astype(jnp.float32)
    ratio = jnp.minimum(1.0, jnp.exp(log_policy - column_of(behaviour[...])))
    shaped = column_of(rewards[...]) - ETA * (log_policy - column_of(regular[...]))
    next_values = later(value, 1) * next_live
    correction = live * ratio * (shaped + next_values - value)
    decay = live * ratio
    reach = 1
    while reach < slots:
        correction = correction + decay * later(correction, reach)
        decay = decay * later(decay, reach)
        reach *= 2
    targets = value + correction
    next_targets = later(targets, 1) * next_live
    policy_grad = -live * ratio * (shaped + next_targets - value)
    value_grad = -live * (targets - value)

    value_cell = value_grad * (1.0 - value * value) / 100.0
    by_policy = policy_grad[None] * (taken.astype(jnp.float32) - jnp.exp(scores - log_total[None]))
    by_score = jnp.where((lane % 8 == 4)[None], value_cell[None], by_policy)
    high = by_score.astype(jnp.bfloat16)
    rest = by_score - high.astype(jnp.float32)
    mid = rest.astype(jnp.bfloat16)
    low = rest - mid.astype(jnp.float32)
    parts = jnp.where(
        (lane < 8)[None],
        high.astype(jnp.float32),
        jnp.where((lane < 16)[None], mid.astype(jnp.float32), low),
    ).astype(jnp.bfloat16)
    out_grad = jnp.dot(
        parts.reshape(-1, 128), heads_t, preferred_element_type=jnp.float32
    )
    act_grad = (out_grad * masks[1].reshape(-1, 128).astype(jnp.float32)).astype(jnp.bfloat16)

    def kernel_of(p, q):
        at = ROWS + (8 - (3 * p + q)) * 128
        return weights[at : at + 128, :].T.astype(jnp.bfloat16)

    def store(block, value):
        back_pairs[block * 128 : (block + 1) * 128, :] = value

    pair_kernels(kernel_of, store)
    act_cells = act_grad.reshape(10, 5, 2, slots, 128)
    put_cells(slope, 0, 10, 0, act_cells[:, :, 0])
    put_cells(slope, 0, 10, 1, act_cells[:, :, 1])
    out_cells = out_grad.reshape(10, 5, 2, slots, 128)
    for first in range(0, 10, count):
        back = conv_pairs(slope, back_pairs[...], first, count)
        for parity in range(2):
            part = back[:, parity * 128 : (parity + 1) * 128].reshape(count, 5, slots, 128)
            total = out_cells[first : first + count, :, parity] + part
            gate = masks[0, first : first + count, :, parity].astype(jnp.float32)
            last[pl.ds(first, count), :, parity] = (total * gate).astype(jnp.bfloat16)
    turned[1] = act_grad.T
    turned[0] = last[...].reshape(-1, 128).T

    for core in range(2):

        @pl.when(role == core)
        def _(core=core):
            for layer, source in ((1, middle), (0, boards)):
                kept = []
                for offset in range(9):
                    parts = [x for x in segment_parts(layer, offset) if x[0] % 2 == core]
                    if parts:
                        kept.append((offset, parts))
                windows = []
                for offset, _ in kept:
                    p, q = offset // 3, offset % 3
                    cols = [source[p : p + 10, (j + q) // 2, (j + q) % 2] for j in range(10)]
                    windows.append(jnp.stack(cols, axis=1).reshape(-1, 128))
                for pair in range(0, len(kept), 2):
                    blocks = jnp.dot(
                        turned[layer],
                        jnp.concatenate(windows[pair : pair + 2], axis=1),
                        preferred_element_type=jnp.float32,
                    )
                    for k in range(2):
                        block = blocks[:, 128 * k : 128 * k + 128].T
                        for segment, first, end, at in kept[pair + k][1]:
                            grad[segment // 2, first:end] = block[at : at + end - first]

    sends = [
        pltpu.make_async_copy(grad.at[lax.rem(y + k, LINE)], out, done.at[k])
        for k, out in enumerate((own, next1, next2, next3))
    ]
    for copy in sends:
        copy.start()
    for copy in sends:
        copy.wait()


def learn(
    length, boards, actions, behaviour, regular, rewards, weights, policy_t, value_t, count=5
):
    slots = boards.shape[2]
    anywhere = pl.BlockSpec(memory_space=pltpu.HBM)
    cells = (10, 5, 2, slots, 128)
    around = (12, 6, 2, slots, 128)
    return pl.pallas_call(
        functools.partial(learner_kernel, count),
        out_shape=[jax.ShapeDtypeStruct((SEGMENT, 128), jnp.float32)] * LINE,
        in_specs=[anywhere] * 9,
        out_specs=[anywhere] * LINE,
        scratch_shapes=[
            pltpu.VMEM((LINE, SEGMENT, 128), jnp.float32),
            pltpu.SMEM((1,), jnp.int32),
            pltpu.VMEM(around, jnp.bfloat16),
            pltpu.VMEM((2 * ROWS, 128), jnp.float32),
            pltpu.VMEM((1, slots), jnp.int32),
            pltpu.VMEM((1, slots), jnp.float32),
            pltpu.VMEM((1, slots), jnp.float32),
            pltpu.VMEM((1, slots), jnp.float32),
            pltpu.VMEM(policy_t.shape, policy_t.dtype),
            pltpu.VMEM(value_t.shape, value_t.dtype),
            pltpu.VMEM((2, 1536, 256), jnp.bfloat16),
            pltpu.VMEM((1536, 256), jnp.bfloat16),
            pltpu.VMEM(around, jnp.bfloat16),
            pltpu.VMEM(cells, jnp.bfloat16),
            pltpu.VMEM((2,) + cells, jnp.bfloat16),
            pltpu.VMEM(around, jnp.bfloat16),
            pltpu.VMEM((2, 128, 100 * slots), jnp.bfloat16),
            pltpu.SemaphoreType.DMA((10,)),
        ],
        compiler_params=pltpu.CompilerParams(vmem_limit_bytes=60 * 1024 * 1024),
        cost_estimate=pl.CostEstimate(
            flops=4 * 10**9, bytes_accessed=3 * 10**6, transcendentals=10000
        ),
        name="learn",
    )(length, boards, actions, behaviour, regular, rewards, weights, policy_t, value_t)


def pull_kernel(own_in, first_in, second_in, own, both, first, second, done):
    moves = [(own_in, own), (first_in, first), (second_in, second)]
    copies = [pltpu.make_async_copy(a, b, done.at[k]) for k, (a, b) in enumerate(moves)]
    for copy in copies:
        copy.start()
    for copy in copies:
        copy.wait()
    both[0:PIECE] = first[...]
    both[PIECE : 2 * PIECE] = second[...]


def pull(own, first, second):
    vmem = pl.BlockSpec(memory_space=pltpu.VMEM)
    rows = pltpu.VMEM((PIECE, 128), jnp.float32)
    return pl.pallas_call(
        pull_kernel,
        out_shape=[
            jax.ShapeDtypeStruct((SEGMENT, 128), jnp.float32),
            jax.ShapeDtypeStruct((2 * PIECE, 128), jnp.float32),
        ],
        in_specs=[pl.BlockSpec(memory_space=pltpu.HBM)] * 3,
        out_specs=[vmem, vmem],
        scratch_shapes=[rows, rows, pltpu.SemaphoreType.DMA((3,))],
        compiler_params=pltpu.CompilerParams(vmem_limit_bytes=16 * 1024 * 1024),
        name="pull",
    )(own, first, second)


def update_kernel(summed, squares, moments, torso_in, fresh, old, first, second, done):
    y = lax.axis_index("dp") // (LINE * LINE)
    start = pl.multiple_of((2 * y + lax.axis_index("role")) * SEGMENT, SEGMENT)
    fetch = pltpu.make_async_copy(torso_in.at[pl.ds(start, SEGMENT)], old, done)
    fetch.start()
    square_sum = jnp.sum(squares[...], axis=1, keepdims=True)
    factor = jnp.minimum(1.0, jnp.sqrt(256.0 * ROWS) / jnp.sqrt(square_sum + NORM_EPS))
    for x in range(2):
        for z in range(LINE):
            rows = slice((LINE * x + z) * PIECE, (LINE * x + z + 1) * PIECE)
            first[rows] = moments[z, x, 0:PIECE]
            second[rows] = moments[z, x, PIECE : 2 * PIECE]
    fetch.wait()
    clipped = summed[...] * factor
    moment_one = BETA_ONE * first[...] + (1.0 - BETA_ONE) * clipped
    moment_two = BETA_TWO * second[...] + (1.0 - BETA_TWO) * clipped * clipped
    fresh[...] = old[...] - LEARN_RATE * moment_one / (jnp.sqrt(moment_two) + ADAM_EPS)


def update(summed, squares, moments, torso):
    vmem = pl.BlockSpec(memory_space=pltpu.VMEM)
    rows = pltpu.VMEM((SEGMENT, 128), jnp.float32)
    return pl.pallas_call(
        update_kernel,
        out_shape=jax.ShapeDtypeStruct((SEGMENT, 128), jnp.float32),
        in_specs=[
            vmem, vmem, vmem, pl.BlockSpec(memory_space=pltpu.HBM)
        ],
        out_specs=vmem,
        scratch_shapes=[rows, rows, rows, pltpu.SemaphoreType.DMA],
        compiler_params=pltpu.CompilerParams(vmem_limit_bytes=16 * 1024 * 1024),
        name="update",
    )(summed, squares, moments, torso)


def shifted(x, axis, step):
    stride = {"y": LINE * LINE, "x": LINE, "z": 1}[axis]
    pairs = []
    for d in range(LINE**3):
        at = d // stride % LINE
        pairs.append((d, d + ((at + step) % LINE - at) * stride))
    return lax.ppermute(x, "dp", pairs)


def line_total(x, axis):
    return (x + shifted(x, axis, 2)) + (shifted(x, axis, 1) + shifted(x, axis, 3))


def line_scatter(chunks, axis):
    return (chunks[0] + shifted(chunks[2], axis, 2)) + (
        shifted(chunks[1], axis, 1) + shifted(chunks[3], axis, 3)
    )


def line_place(pieces, at):
    whole = jnp.zeros((LINE,) + pieces[0].shape, pieces[0].dtype)
    for step, piece in enumerate(pieces):
        whole = lax.dynamic_update_index_in_dim(whole, piece, (at - step) % LINE, 0)
    return whole


def line_gather(x, axis, at):
    return line_place([x] + [shifted(x, axis, step) for step in range(1, LINE)], at)


def line_exchange(summed, moments, axis, at):
    rows = summed.shape[0]
    both = jnp.concatenate([summed, moments])
    got = [both] + [shifted(both, axis, step) for step in range(1, LINE)]
    total = (got[0][:rows] + got[2][:rows]) + (got[1][:rows] + got[3][:rows])
    return total, line_place([x[rows:] for x in got], at)


def swapped_z(x, bit):
    return lax.ppermute(x, "dp", [(d, d ^ bit) for d in range(LINE**3)])


def moments_along_z(x, z):
    near = swapped_z(x, 1)
    pair = jnp.where(z % 2 == 0, jnp.stack([x, near]), jnp.stack([near, x]))
    far = swapped_z(pair, 2)
    return jnp.where(z < 2, jnp.concatenate([pair, far]), jnp.concatenate([far, pair]))


def role_swap(x):
    return lax.ppermute(x, "role", [(0, 1), (1, 0)])


def body(
    board_now,
    traj_boards,
    actions,
    lengths,
    behaviour,
    regular,
    rewards,
    torso,
    policy_head,
    value_head,
    first_moment,
    second_moment,
):
    role = lax.axis_index("role")
    dp = lax.axis_index("dp")
    y, x, z = dp // (LINE * LINE), dp // LINE % LINE, dp % LINE
    own, next1, next2, next3 = learn(
        lengths,
        by_cell(traj_boards[0]),
        actions,
        behaviour,
        regular,
        rewards,
        torso,
        policy_head.T,
        value_head[None],
    )
    own, moments = pull(own, first_moment, second_moment)
    summed = line_scatter((own, next1, next2, next3), "y")
    summed, moments = line_exchange(summed, moments, "x", x)
    moments = lax.dynamic_slice_in_dim(moments, 2 * role, 2, 0).reshape(-1, 128)
    moments = moments_along_z(moments, z)
    summed = line_total(summed, "z")
    squares = jnp.sum(summed * summed, axis=0, keepdims=True)
    squares = line_total(squares + role_swap(squares), "y")
    fresh = update(summed, squares, moments.reshape(LINE, 2, 2 * PIECE, 128), torso)
    mine = line_gather(fresh, "y", y)
    other = role_swap(mine)
    boards, heads = stage(mine, by_cell(board_now), policy_head.T.astype(jnp.float32))
    here = act(mine, other, boards, heads)
    there = role_swap(here)
    at = (LINE * x + z) % (2 * LINE) * PIECE
    new_share = jnp.where(
        role == x // 2,
        lax.dynamic_slice(mine, (y, at, 0), (1, PIECE, 128))[0],
        lax.dynamic_slice(other, (y, at, 0), (1, PIECE, 128))[0],
    )
    move_logp = jnp.concatenate([jnp.where(role == 0, here, there), jnp.where(role == 0, there, here)])
    return (new_share, move_logp)


def solution(mesh):
    return jax.shard_map(
        body,
        mesh=mesh,
        in_specs=(
            P("dp", None, None, None),
            P("dp", None, None, None, None),
            P("dp", None),
            P("dp"),
            P("dp", None),
            P("dp", None),
            P("dp", None),
            P(),
            P(),
            P(),
            P("dp", None),
            P("dp", None),
        ),
        out_specs=(P("dp", None), P("dp", None)),
        check_vma=False,
    )
```

```python
import functools

import jax
import jax.numpy as jnp
from jax import lax
from jax.experimental import pallas as pl
from jax.experimental.pallas import tpu as pltpu
from jax.sharding import PartitionSpec as P

ETA = 0.2
LEARN_RATE = 0.03
BETA_ONE = 0.9
BETA_TWO = 0.999
ADAM_EPS = 1e-08
NORM_EPS = 1e-12
ROWS = 1152
LINE = 4
SEGMENT = 2 * ROWS // (2 * LINE)
PIECE = SEGMENT // 8


def by_cell(boards):
    return jnp.transpose(boards, (1, 2, 0, 3))


def inner_cells(ref):
    return ref.reshape((12, 12) + ref.shape[3:]).at[1:11, 1:11]


def segment_parts(layer, offset):
    start = layer * ROWS + offset * 128
    at, parts = start, []
    while at < start + 128:
        segment = at // SEGMENT
        end = min(start + 128, (segment + 1) * SEGMENT)
        parts.append((segment, at - segment * SEGMENT, end - segment * SEGMENT, at - start))
        at = end
    return parts


def clear_border(ref):
    zero_row = jnp.zeros(ref.shape[1:], ref.dtype)
    ref[0] = zero_row
    ref[11] = zero_row
    zero_col = jnp.zeros((12,) + ref.shape[3:], ref.dtype)
    ref[:, 0, 0] = zero_col
    ref[:, 5, 1] = zero_col


def pair_kernels(kernel_of, store):
    nothing = jnp.zeros((128, 128), jnp.bfloat16)
    for p in range(3):
        row = [kernel_of(p, q) for q in range(3)]
        for q in range(4):
            left = row[q] if q < 3 else nothing
            right = row[q - 1] if q > 0 else nothing
            store(4 * p + q, jnp.concatenate([left, right], axis=1))


def conv_pairs(source, pair_weights, first, count):
    windows = []
    for p in range(3):
        for q in range(4):
            window = source[pl.ds(first + p, count), q // 2 : q // 2 + 5, q % 2]
            windows.append(window.reshape(-1, 128))
    return jnp.dot(
        jnp.concatenate(windows, axis=1), pair_weights, preferred_element_type=jnp.float32
    )


def residual(source, first, count, parity):
    if parity == 0:
        window = source[pl.ds(first + 1, count), 0:5, 1]
    else:
        window = source[pl.ds(first + 1, count), 1:6, 0]
    return window


def put_cells(target, first, count, parity, value):
    if parity == 0:
        target[pl.ds(first + 1, count), 0:5, 1] = value
    else:
        target[pl.ds(first + 1, count), 1:6, 0] = value


def stage_kernel(mine, boards_in, policy_t, boards, heads, done):
    games = boards.shape[3]
    half = pl.ds(pl.multiple_of(lax.axis_index("role") * games, games), games)
    fetch = pltpu.make_async_copy(boards_in.at[:, :, half], inner_cells(boards), done)
    fetch.start()
    clear_border(boards)
    spread = lax.broadcasted_iota(jnp.int32, (4, 1280), 1)
    row = lax.broadcasted_iota(jnp.int32, (4, 1280), 0)
    spread = (spread % 128 == 10 * row + spread // 128).astype(jnp.float32)
    by_column = lax.dot_general(
        policy_t[...], spread, (((0,), (0,)), ((), ())), preferred_element_type=jnp.float32
    )
    for j in range(10):
        heads[128 * j : 128 * j + 128, :] = by_column[:, 128 * j : 128 * j + 128].astype(jnp.bfloat16)
    fetch.wait()


def stage(mine, boards, policy_t):
    games = boards.shape[2] // 2
    vmem = pl.BlockSpec(memory_space=pltpu.VMEM)
    anywhere = pl.BlockSpec(memory_space=pltpu.HBM)
    return pl.pallas_call(
        stage_kernel,
        out_shape=[
            jax.ShapeDtypeStruct((12, 6, 2, games, 128), jnp.bfloat16),
            jax.ShapeDtypeStruct((1280, 128), jnp.bfloat16),
        ],
        in_specs=[anywhere, anywhere, vmem],
        out_specs=[vmem, vmem],
        scratch_shapes=[pltpu.SemaphoreType.DMA],
        compiler_params=pltpu.CompilerParams(vmem_limit_bytes=16 * 1024 * 1024),
        cost_estimate=pl.CostEstimate(
            flops=10**9, bytes_accessed=4 * 10**6, transcendentals=0
        ),
        name="stage",
    )(mine, boards, policy_t)


def actor_kernel(count, unroll, mine, other, boards, heads, out, pairs, middle, last):
    games = boards.shape[3]
    role = lax.axis_index("role")
    for layer in range(2):
        def kernel_of(p, q, layer=layer):
            parts = []
            for segment, first, last_row, _ in segment_parts(layer, 3 * p + q):
                y, owner = segment // 2, segment % 2
                rows = slice(first, last_row)
                parts.append(jnp.where(role == owner, mine[y, rows], other[y, rows]))
            return jnp.concatenate(parts, axis=0).astype(jnp.bfloat16)

        def store(block, value, layer=layer):
            pairs[layer, block * 128 : (block + 1) * 128, :] = value

        pair_kernels(kernel_of, store)
    clear_border(middle)

    def run_layer(layer, source, emit):
        def step(at, carry):
            first = at * count
            pre = conv_pairs(source, pairs[layer], first, count)
            for parity in range(2):
                part = pre[:, parity * 128 : (parity + 1) * 128].reshape(count, 5, games, 128)
                before = residual(source, first, count, parity).astype(jnp.float32)
                emit(first, parity, (before + jnp.maximum(part, 0.0)).astype(jnp.bfloat16))
            return carry

        lax.fori_loop(0, 10 // count, step, 0, unroll=unroll)

    run_layer(0, boards, lambda first, parity, value: put_cells(middle, first, count, parity, value))

    def to_last(first, parity, value):
        last[pl.ds(first, count), :, parity] = value

    run_layer(1, middle, to_last)
    cells = [last[:, j // 2, j % 2].reshape(-1, 128) for j in range(10)]
    logits = jnp.dot(jnp.concatenate(cells, axis=1), heads[...], preferred_element_type=jnp.float32)
    logits = logits.reshape(10, games, 128)
    lanes = lax.broadcasted_iota(jnp.int32, (games, 128), 1)
    moves = []
    total = jnp.zeros((games, 1), jnp.float32)
    for d in range(4):
        gathered = jnp.zeros((games, 128), jnp.float32)
        for i in range(10):
            turned = pltpu.roll(logits[i], (10 * i - 10 * d) % 128, 1)
            gathered = jnp.where((lanes >= 10 * i) & (lanes < 10 * i + 10), turned, gathered)
        moves.append(gathered)
        total = total + jnp.sum(
            jnp.where(lanes < 100, jnp.exp(gathered), 0.0), axis=1, keepdims=True
        )
    log_total = jnp.log(total)
    for d in range(4):
        out[:, 100 * d : 100 * d + 100] = (moves[d] - log_total)[:, :100]


def act(mine, other, boards, heads, count=2, unroll=5):
    games = boards.shape[3]
    vmem = pl.BlockSpec(memory_space=pltpu.VMEM)
    return pl.pallas_call(
        functools.partial(actor_kernel, count, unroll),
        out_shape=jax.ShapeDtypeStruct((games, 400), jnp.float32),
        in_specs=[vmem] * 4,
        out_specs=vmem,
        scratch_shapes=[
            pltpu.VMEM((2, 1536, 256), jnp.bfloat16),
            pltpu.VMEM((12, 6, 2, games, 128), jnp.bfloat16),
            pltpu.VMEM((10, 5, 2, games, 128), jnp.bfloat16),
        ],
        compiler_params=pltpu.CompilerParams(vmem_limit_bytes=32 * 1024 * 1024),
        cost_estimate=pl.CostEstimate(
            flops=8 * 10**9, bytes_accessed=4 * 10**6, transcendentals=30000
        ),
        name="act",
    )(mine, other, boards, heads)


def column_of(row):
    size = row.shape[1]
    across = lax.broadcasted_iota(jnp.int32, (size, size), 1)
    down = lax.broadcasted_iota(jnp.int32, (size, size), 0)
    spread = jnp.broadcast_to(row, (size, size))
    return jnp.sum(jnp.where(across == down, spread, jnp.zeros_like(spread)), axis=1, keepdims=True)


def later(x, reach):
    return jnp.concatenate([x[reach:], jnp.zeros((reach, x.shape[1]), x.dtype)], axis=0)


def learner_kernel(
    count, length_in, boards_in, actions_in, behaviour_in, regular_in, rewards_in, weights_in,
    policy_in, value_in, own, next1, next2, next3,
    grad, length, boards, weights, actions, behaviour, regular, rewards, policy_t, value_t, pairs, back_pairs,
    middle, last, masks, slope, turned, done,
):
    slots = boards.shape[3]
    role = lax.axis_index("role")
    y = lax.axis_index("dp") // (LINE * LINE)
    moves = [
        (weights_in.at[0:ROWS], weights.at[0:ROWS]),
        (boards_in, inner_cells(boards)),
        (weights_in.at[ROWS : 2 * ROWS], weights.at[ROWS : 2 * ROWS]),
        (actions_in, actions),
        (behaviour_in, behaviour),
        (regular_in, regular),
        (rewards_in, rewards),
        (policy_in, policy_t),
        (value_in, value_t),
        (length_in, length),
    ]
    copies = [pltpu.make_async_copy(a, b, done.at[k]) for k, (a, b) in enumerate(moves)]
    for copy in copies:
        copy.start()
    clear_border(boards)

    def make_pairs(layer):
        def kernel_of(p, q):
            at = layer * ROWS + (3 * p + q) * 128
            return weights[at : at + 128, :].astype(jnp.bfloat16)

        def store(block, value):
            pairs[layer, block * 128 : (block + 1) * 128, :] = value

        pair_kernels(kernel_of, store)

    clear_border(middle)
    clear_border(slope)
    copies[0].wait()
    make_pairs(0)
    copies[1].wait()

    def run_layer(layer, source, emit):
        for first in range(0, 10, count):
            pre = conv_pairs(source, pairs[layer], first, count)
            for parity in range(2):
                part = pre[:, parity * 128 : (parity + 1) * 128].reshape(count, 5, slots, 128)
                before = residual(source, first, count, parity).astype(jnp.float32)
                emit(first, parity, (before + jnp.maximum(part, 0.0)).astype(jnp.bfloat16))
                masks[layer, first : first + count, :, parity] = (part > 0).astype(jnp.bfloat16)

    run_layer(0, boards, lambda first, parity, value: put_cells(middle, first, count, parity, value))

    copies[2].wait()
    make_pairs(1)

    def to_last(first, parity, value):
        last[pl.ds(first, count), :, parity] = value

    run_layer(1, middle, to_last)

    for copy in copies[3:]:
        copy.wait()

    eight = jnp.concatenate(
        [
            policy_t[...].astype(jnp.float32),
            value_t[...].astype(jnp.float32),
            jnp.zeros((3, 128), jnp.float32),
        ],
        axis=0,
    )
    heads_t = jnp.concatenate(
        [eight, eight, eight, jnp.zeros((104, 128), jnp.float32)], axis=0
    ).astype(jnp.bfloat16)

    scores = lax.dot_general(
        last[...].reshape(-1, 128), heads_t, (((1,), (1,)), ((), ())),
        preferred_element_type=jnp.float32,
    ).reshape(100, slots, 128)
    lane = lax.broadcasted_iota(jnp.int32, (slots, 128), 1)
    weights_sum = jnp.sum(jnp.where(lane < 4, jnp.exp(scores), 0.0), axis=0)
    log_total = jnp.log(jnp.sum(weights_sum, axis=1, keepdims=True))
    action = column_of(actions[...])
    direction = action // 100
    cell = action - 100 * direction
    cells = lax.broadcasted_iota(jnp.int32, (100, slots, 128), 0)
    taken = (cells == cell[None]) & (lane % 8 == direction)[None]
    picked = jnp.sum(
        jnp.sum(jnp.where(taken & (lane < 4)[None], scores, 0.0), axis=0), axis=1, keepdims=True
    )
    value_sum = jnp.sum(scores, axis=0)
    value = jnp.tanh(
        jnp.sum(jnp.where(lane == 4, value_sum, 0.0), axis=1, keepdims=True) / 100.0
    )
    log_policy = picked - log_total

    positions = lax.broadcasted_iota(jnp.int32, (slots, 1), 0)
    live = (positions < length[0]).astype(jnp.float32)
    next_live = (positions + 1 < length[0]).astype(jnp.float32)
    ratio = jnp.minimum(1.0, jnp.exp(log_policy - column_of(behaviour[...])))
    shaped = column_of(rewards[...]) - ETA * (log_policy - column_of(regular[...]))
    next_values = later(value, 1) * next_live
    correction = live * ratio * (shaped + next_values - value)
    decay = live * ratio
    reach = 1
    while reach < slots:
        correction = correction + decay * later(correction, reach)
        decay = decay * later(decay, reach)
        reach *= 2
    targets = value + correction
    next_targets = later(targets, 1) * next_live
    policy_grad = -live * ratio * (shaped + next_targets - value)
    value_grad = -live * (targets - value)

    value_cell = value_grad * (1.0 - value * value) / 100.0
    by_policy = policy_grad[None] * (taken.astype(jnp.float32) - jnp.exp(scores - log_total[None]))
    by_score = jnp.where((lane % 8 == 4)[None], value_cell[None], by_policy)
    high = by_score.astype(jnp.bfloat16)
    rest = by_score - high.astype(jnp.float32)
    mid = rest.astype(jnp.bfloat16)
    low = rest - mid.astype(jnp.float32)
    parts = jnp.where(
        (lane < 8)[None],
        high.astype(jnp.float32),
        jnp.where((lane < 16)[None], mid.astype(jnp.float32), low),
    ).astype(jnp.bfloat16)
    out_grad = jnp.dot(
        parts.reshape(-1, 128), heads_t, preferred_element_type=jnp.float32
    )
    act_grad = (out_grad * masks[1].reshape(-1, 128).astype(jnp.float32)).astype(jnp.bfloat16)

    def kernel_of(p, q):
        at = ROWS + (8 - (3 * p + q)) * 128
        return weights[at : at + 128, :].T.astype(jnp.bfloat16)

    def store(block, value):
        back_pairs[block * 128 : (block + 1) * 128, :] = value

    pair_kernels(kernel_of, store)
    act_cells = act_grad.reshape(10, 5, 2, slots, 128)
    put_cells(slope, 0, 10, 0, act_cells[:, :, 0])
    put_cells(slope, 0, 10, 1, act_cells[:, :, 1])
    out_cells = out_grad.reshape(10, 5, 2, slots, 128)
    for first in range(0, 10, count):
        back = conv_pairs(slope, back_pairs[...], first, count)
        for parity in range(2):
            part = back[:, parity * 128 : (parity + 1) * 128].reshape(count, 5, slots, 128)
            total = out_cells[first : first + count, :, parity] + part
            gate = masks[0, first : first + count, :, parity].astype(jnp.float32)
            last[pl.ds(first, count), :, parity] = (total * gate).astype(jnp.bfloat16)
    turned[1] = act_grad.T
    turned[0] = last[...].reshape(-1, 128).T

    def layer_gradient(layer, source, core):
        kept = []
        for offset in range(9):
            parts = [x for x in segment_parts(layer, offset) if x[0] % 2 == core]
            if parts:
                kept.append((offset, parts))
        windows = []
        for offset, _ in kept:
            p, q = offset // 3, offset % 3
            cols = [source[p : p + 10, (j + q) // 2, (j + q) % 2] for j in range(10)]
            windows.append(jnp.stack(cols, axis=1).reshape(-1, 128))
        for pair in range(0, len(kept), 2):
            blocks = jnp.dot(
                turned[layer],
                jnp.concatenate(windows[pair : pair + 2], axis=1),
                preferred_element_type=jnp.float32,
            )
            for k in range(2):
                block = blocks[:, 128 * k : 128 * k + 128].T
                for segment, first, end, at in kept[pair + k][1]:
                    grad[segment // 2, first:end] = block[at : at + end - first]

    chunks = (own, next1, next2, next3)
    for layer, source in ((1, middle), (0, boards)):
        for core in range(2):
            pl.when(role == core)(functools.partial(layer_gradient, layer, source, core))
        for to_y in (2 * layer, 2 * layer + 1):
            for k, out in enumerate(chunks):

                @pl.when(lax.rem(y + k, LINE) == to_y)
                def _(to_y=to_y, k=k, out=out):
                    pltpu.make_async_copy(grad.at[to_y], out, done.at[k]).start()

    for k, out in enumerate(chunks):
        pltpu.make_async_copy(grad.at[0], out, done.at[k]).wait()


def learn(
    length, boards, actions, behaviour, regular, rewards, weights, policy_t, value_t, count=5
):
    slots = boards.shape[2]
    anywhere = pl.BlockSpec(memory_space=pltpu.HBM)
    cells = (10, 5, 2, slots, 128)
    around = (12, 6, 2, slots, 128)
    return pl.pallas_call(
        functools.partial(learner_kernel, count),
        out_shape=[jax.ShapeDtypeStruct((SEGMENT, 128), jnp.float32)] * LINE,
        in_specs=[anywhere] * 9,
        out_specs=[anywhere] * LINE,
        scratch_shapes=[
            pltpu.VMEM((LINE, SEGMENT, 128), jnp.float32),
            pltpu.SMEM((1,), jnp.int32),
            pltpu.VMEM(around, jnp.bfloat16),
            pltpu.VMEM((2 * ROWS, 128), jnp.float32),
            pltpu.VMEM((1, slots), jnp.int32),
            pltpu.VMEM((1, slots), jnp.float32),
            pltpu.VMEM((1, slots), jnp.float32),
            pltpu.VMEM((1, slots), jnp.float32),
            pltpu.VMEM(policy_t.shape, policy_t.dtype),
            pltpu.VMEM(value_t.shape, value_t.dtype),
            pltpu.VMEM((2, 1536, 256), jnp.bfloat16),
            pltpu.VMEM((1536, 256), jnp.bfloat16),
            pltpu.VMEM(around, jnp.bfloat16),
            pltpu.VMEM(cells, jnp.bfloat16),
            pltpu.VMEM((2,) + cells, jnp.bfloat16),
            pltpu.VMEM(around, jnp.bfloat16),
            pltpu.VMEM((2, 128, 100 * slots), jnp.bfloat16),
            pltpu.SemaphoreType.DMA((10,)),
        ],
        compiler_params=pltpu.CompilerParams(vmem_limit_bytes=60 * 1024 * 1024),
        cost_estimate=pl.CostEstimate(
            flops=4 * 10**9, bytes_accessed=3 * 10**6, transcendentals=10000
        ),
        name="learn",
    )(length, boards, actions, behaviour, regular, rewards, weights, policy_t, value_t)


def pull_kernel(own_in, first_in, second_in, own, both, first, second, done):
    moves = [(own_in, own), (first_in, first), (second_in, second)]
    copies = [pltpu.make_async_copy(a, b, done.at[k]) for k, (a, b) in enumerate(moves)]
    for copy in copies:
        copy.start()
    for copy in copies:
        copy.wait()
    both[0:PIECE] = first[...]
    both[PIECE : 2 * PIECE] = second[...]


def pull(own, first, second):
    vmem = pl.BlockSpec(memory_space=pltpu.VMEM)
    rows = pltpu.VMEM((PIECE, 128), jnp.float32)
    return pl.pallas_call(
        pull_kernel,
        out_shape=[
            jax.ShapeDtypeStruct((SEGMENT, 128), jnp.float32),
            jax.ShapeDtypeStruct((2 * PIECE, 128), jnp.float32),
        ],
        in_specs=[pl.BlockSpec(memory_space=pltpu.HBM)] * 3,
        out_specs=[vmem, vmem],
        scratch_shapes=[rows, rows, pltpu.SemaphoreType.DMA((3,))],
        compiler_params=pltpu.CompilerParams(vmem_limit_bytes=16 * 1024 * 1024),
        name="pull",
    )(own, first, second)


def update_kernel(summed, squares, moments, torso_in, fresh, old, first, second, done):
    y = lax.axis_index("dp") // (LINE * LINE)
    start = pl.multiple_of((2 * y + lax.axis_index("role")) * SEGMENT, SEGMENT)
    fetch = pltpu.make_async_copy(torso_in.at[pl.ds(start, SEGMENT)], old, done)
    fetch.start()
    square_sum = jnp.sum(squares[...], axis=1, keepdims=True)
    factor = jnp.minimum(1.0, jnp.sqrt(256.0 * ROWS) / jnp.sqrt(square_sum + NORM_EPS))
    for x in range(2):
        for z in range(LINE):
            rows = slice((LINE * x + z) * PIECE, (LINE * x + z + 1) * PIECE)
            first[rows] = moments[z, x, 0:PIECE]
            second[rows] = moments[z, x, PIECE : 2 * PIECE]
    fetch.wait()
    clipped = summed[...] * factor
    moment_one = BETA_ONE * first[...] + (1.0 - BETA_ONE) * clipped
    moment_two = BETA_TWO * second[...] + (1.0 - BETA_TWO) * clipped * clipped
    fresh[...] = old[...] - LEARN_RATE * moment_one / (jnp.sqrt(moment_two) + ADAM_EPS)


def update(summed, squares, moments, torso):
    vmem = pl.BlockSpec(memory_space=pltpu.VMEM)
    rows = pltpu.VMEM((SEGMENT, 128), jnp.float32)
    return pl.pallas_call(
        update_kernel,
        out_shape=jax.ShapeDtypeStruct((SEGMENT, 128), jnp.float32),
        in_specs=[
            vmem, vmem, vmem, pl.BlockSpec(memory_space=pltpu.HBM)
        ],
        out_specs=vmem,
        scratch_shapes=[rows, rows, rows, pltpu.SemaphoreType.DMA],
        compiler_params=pltpu.CompilerParams(vmem_limit_bytes=16 * 1024 * 1024),
        name="update",
    )(summed, squares, moments, torso)


def shifted(x, axis, step):
    stride = {"y": LINE * LINE, "x": LINE, "z": 1}[axis]
    pairs = []
    for d in range(LINE**3):
        at = d // stride % LINE
        pairs.append((d, d + ((at + step) % LINE - at) * stride))
    return lax.ppermute(x, "dp", pairs)


def line_total(x, axis):
    return (x + shifted(x, axis, 2)) + (shifted(x, axis, 1) + shifted(x, axis, 3))


def line_place(pieces, at):
    whole = jnp.zeros((LINE,) + pieces[0].shape, pieces[0].dtype)
    for step, piece in enumerate(pieces):
        whole = lax.dynamic_update_index_in_dim(whole, piece, (at - step) % LINE, 0)
    return whole


def line_gather(x, axis, at):
    return line_place([x] + [shifted(x, axis, step) for step in range(1, LINE)], at)


def moments_along_x(own, role, x):
    def device(role, x, rest):
        return role * LINE**3 + rest // LINE * LINE * LINE + x * LINE + rest % LINE

    same, next_to = [], []
    for rest in range(LINE * LINE):
        for to_role in range(2):
            for to_x in range(LINE):
                to = device(to_role, to_x, rest)
                if to_x // 2 != to_role:
                    same.append((device(to_role, to_x ^ 2, rest), to))
                next_to.append((device(to_x // 2, 2 * to_role + 1 - to_x % 2, rest), to))
    same = jnp.where(x // 2 == role, own, lax.ppermute(own, ("role", "dp"), same))
    next_to = lax.ppermute(own, ("role", "dp"), next_to)
    even = x % 2 == 0
    return jnp.concatenate([jnp.where(even, same, next_to), jnp.where(even, next_to, same)])


def swapped_z(x, bit):
    return lax.ppermute(x, "dp", [(d, d ^ bit) for d in range(LINE**3)])


def moments_along_z(x, z):
    near = swapped_z(x, 1)
    pair = jnp.where(z % 2 == 0, jnp.stack([x, near]), jnp.stack([near, x]))
    far = swapped_z(pair, 2)
    return jnp.where(z < 2, jnp.concatenate([pair, far]), jnp.concatenate([far, pair]))


def role_swap(x):
    return lax.ppermute(x, "role", [(0, 1), (1, 0)])


def body(
    board_now,
    traj_boards,
    actions,
    lengths,
    behaviour,
    regular,
    rewards,
    torso,
    policy_head,
    value_head,
    first_moment,
    second_moment,
):
    role = lax.axis_index("role")
    dp = lax.axis_index("dp")
    y, x, z = dp // (LINE * LINE), dp // LINE % LINE, dp % LINE
    own, next1, next2, next3 = learn(
        lengths,
        by_cell(traj_boards[0]),
        actions,
        behaviour,
        regular,
        rewards,
        torso,
        policy_head.T,
        value_head[None],
    )
    own, moments = pull(own, first_moment, second_moment)
    next2 = shifted(next2, "y", 2)
    next2, moments = lax.optimization_barrier((next2, moments))
    moments = moments_along_x(moments, role, x)
    moments = moments_along_z(moments, z)
    summed = (own + next2) + (shifted(next1, "y", 1) + shifted(next3, "y", 3))
    summed = line_total(line_total(summed, "x"), "z")
    squares = jnp.sum(summed * summed, axis=0, keepdims=True)
    squares = line_total(squares + role_swap(squares), "y")
    fresh = update(summed, squares, moments.reshape(LINE, 2, 2 * PIECE, 128), torso)
    mine = line_gather(fresh, "y", y)
    other = role_swap(mine)
    boards, heads = stage(mine, by_cell(board_now), policy_head.T.astype(jnp.float32))
    here = act(mine, other, boards, heads)
    there = role_swap(here)
    at = (LINE * x + z) % (2 * LINE) * PIECE
    new_share = jnp.where(
        role == x // 2,
        lax.dynamic_slice(mine, (y, at, 0), (1, PIECE, 128))[0],
        lax.dynamic_slice(other, (y, at, 0), (1, PIECE, 128))[0],
    )
    move_logp = jnp.concatenate([jnp.where(role == 0, here, there), jnp.where(role == 0, there, here)])
    return (new_share, move_logp)


def solution(mesh):
    return jax.shard_map(
        body,
        mesh=mesh,
        in_specs=(
            P("dp", None, None, None),
            P("dp", None, None, None, None),
            P("dp", None),
            P("dp"),
            P("dp", None),
            P("dp", None),
            P("dp", None),
            P(),
            P(),
            P(),
            P("dp", None),
            P("dp", None),
        ),
        out_specs=(P("dp", None), P("dp", None)),
        check_vma=False,
    )
```

```python
import functools

import jax
import jax.numpy as jnp
from jax import lax
from jax.experimental import pallas as pl
from jax.experimental.pallas import tpu as pltpu
from jax.sharding import PartitionSpec as P

ETA = 0.2
LEARN_RATE = 0.03
BETA_ONE = 0.9
BETA_TWO = 0.999
ADAM_EPS = 1e-08
NORM_EPS = 1e-12
ROWS = 1152
LINE = 4
SEGMENT = 2 * ROWS // (2 * LINE)
PIECE = SEGMENT // 8


def by_cell(boards):
    return jnp.transpose(boards, (1, 2, 0, 3))


def inner_cells(ref):
    return ref.reshape((12, 12) + ref.shape[3:]).at[1:11, 1:11]


def segment_parts(layer, offset):
    start = layer * ROWS + offset * 128
    at, parts = start, []
    while at < start + 128:
        segment = at // SEGMENT
        end = min(start + 128, (segment + 1) * SEGMENT)
        parts.append((segment, at - segment * SEGMENT, end - segment * SEGMENT, at - start))
        at = end
    return parts


def clear_border(ref):
    zero_row = jnp.zeros(ref.shape[1:], ref.dtype)
    ref[0] = zero_row
    ref[11] = zero_row
    zero_col = jnp.zeros((12,) + ref.shape[3:], ref.dtype)
    ref[:, 0, 0] = zero_col
    ref[:, 5, 1] = zero_col


def pair_kernels(kernel_of, store):
    nothing = jnp.zeros((128, 128), jnp.bfloat16)
    for p in range(3):
        row = [kernel_of(p, q) for q in range(3)]
        for q in range(4):
            left = row[q] if q < 3 else nothing
            right = row[q - 1] if q > 0 else nothing
            store(4 * p + q, jnp.concatenate([left, right], axis=1))


def conv_pairs(source, pair_weights, first, count):
    windows = []
    for p in range(3):
        for q in range(4):
            window = source[pl.ds(first + p, count), q // 2 : q // 2 + 5, q % 2]
            windows.append(window.reshape(-1, 128))
    return jnp.dot(
        jnp.concatenate(windows, axis=1), pair_weights, preferred_element_type=jnp.float32
    )


def residual(source, first, count, parity):
    if parity == 0:
        window = source[pl.ds(first + 1, count), 0:5, 1]
    else:
        window = source[pl.ds(first + 1, count), 1:6, 0]
    return window


def put_cells(target, first, count, parity, value):
    if parity == 0:
        target[pl.ds(first + 1, count), 0:5, 1] = value
    else:
        target[pl.ds(first + 1, count), 1:6, 0] = value


def stage_kernel(mine, boards_in, policy_t, boards, heads, done):
    games = boards.shape[3]
    half = pl.ds(pl.multiple_of(lax.axis_index("role") * games, games), games)
    fetch = pltpu.make_async_copy(boards_in.at[:, :, half], inner_cells(boards), done)
    fetch.start()
    clear_border(boards)
    spread = lax.broadcasted_iota(jnp.int32, (4, 1280), 1)
    row = lax.broadcasted_iota(jnp.int32, (4, 1280), 0)
    spread = (spread % 128 == 10 * row + spread // 128).astype(jnp.float32)
    by_column = lax.dot_general(
        policy_t[...], spread, (((0,), (0,)), ((), ())), preferred_element_type=jnp.float32
    )
    for j in range(10):
        heads[128 * j : 128 * j + 128, :] = by_column[:, 128 * j : 128 * j + 128].astype(jnp.bfloat16)
    fetch.wait()


def stage(mine, boards, policy_t):
    games = boards.shape[2] // 2
    vmem = pl.BlockSpec(memory_space=pltpu.VMEM)
    anywhere = pl.BlockSpec(memory_space=pltpu.HBM)
    return pl.pallas_call(
        stage_kernel,
        out_shape=[
            jax.ShapeDtypeStruct((12, 6, 2, games, 128), jnp.bfloat16),
            jax.ShapeDtypeStruct((1280, 128), jnp.bfloat16),
        ],
        in_specs=[anywhere, anywhere, vmem],
        out_specs=[vmem, vmem],
        scratch_shapes=[pltpu.SemaphoreType.DMA],
        compiler_params=pltpu.CompilerParams(vmem_limit_bytes=16 * 1024 * 1024),
        cost_estimate=pl.CostEstimate(
            flops=10**9, bytes_accessed=4 * 10**6, transcendentals=0
        ),
        name="stage",
    )(mine, boards, policy_t)


def actor_kernel(count, unroll, mine, other, boards, heads, out, pairs, middle, last):
    games = boards.shape[3]
    role = lax.axis_index("role")
    for layer in range(2):
        def kernel_of(p, q, layer=layer):
            parts = []
            for segment, first, last_row, _ in segment_parts(layer, 3 * p + q):
                y, owner = segment // 2, segment % 2
                rows = slice(first, last_row)
                parts.append(jnp.where(role == owner, mine[y, rows], other[y, rows]))
            return jnp.concatenate(parts, axis=0).astype(jnp.bfloat16)

        def store(block, value, layer=layer):
            pairs[layer, block * 128 : (block + 1) * 128, :] = value

        pair_kernels(kernel_of, store)
    clear_border(middle)

    def run_layer(layer, source, emit):
        def step(at, carry):
            first = at * count
            pre = conv_pairs(source, pairs[layer], first, count)
            for parity in range(2):
                part = pre[:, parity * 128 : (parity + 1) * 128].reshape(count, 5, games, 128)
                before = residual(source, first, count, parity).astype(jnp.float32)
                emit(first, parity, (before + jnp.maximum(part, 0.0)).astype(jnp.bfloat16))
            return carry

        lax.fori_loop(0, 10 // count, step, 0, unroll=unroll)

    run_layer(0, boards, lambda first, parity, value: put_cells(middle, first, count, parity, value))

    def to_last(first, parity, value):
        last[pl.ds(first, count), :, parity] = value

    run_layer(1, middle, to_last)
    cells = [last[:, j // 2, j % 2].reshape(-1, 128) for j in range(10)]
    logits = jnp.dot(jnp.concatenate(cells, axis=1), heads[...], preferred_element_type=jnp.float32)
    logits = logits.reshape(10, games, 128)
    lanes = lax.broadcasted_iota(jnp.int32, (games, 128), 1)
    moves = []
    total = jnp.zeros((games, 1), jnp.float32)
    for d in range(4):
        gathered = jnp.zeros((games, 128), jnp.float32)
        for i in range(10):
            turned = pltpu.roll(logits[i], (10 * i - 10 * d) % 128, 1)
            gathered = jnp.where((lanes >= 10 * i) & (lanes < 10 * i + 10), turned, gathered)
        moves.append(gathered)
        total = total + jnp.sum(
            jnp.where(lanes < 100, jnp.exp(gathered), 0.0), axis=1, keepdims=True
        )
    log_total = jnp.log(total)
    for d in range(4):
        out[:, 100 * d : 100 * d + 100] = (moves[d] - log_total)[:, :100]


def act(mine, other, boards, heads, count=2, unroll=5):
    games = boards.shape[3]
    vmem = pl.BlockSpec(memory_space=pltpu.VMEM)
    return pl.pallas_call(
        functools.partial(actor_kernel, count, unroll),
        out_shape=jax.ShapeDtypeStruct((games, 400), jnp.float32),
        in_specs=[vmem] * 4,
        out_specs=vmem,
        scratch_shapes=[
            pltpu.VMEM((2, 1536, 256), jnp.bfloat16),
            pltpu.VMEM((12, 6, 2, games, 128), jnp.bfloat16),
            pltpu.VMEM((10, 5, 2, games, 128), jnp.bfloat16),
        ],
        compiler_params=pltpu.CompilerParams(vmem_limit_bytes=32 * 1024 * 1024),
        cost_estimate=pl.CostEstimate(
            flops=8 * 10**9, bytes_accessed=4 * 10**6, transcendentals=30000
        ),
        name="act",
    )(mine, other, boards, heads)


def column_of(row):
    size = row.shape[1]
    across = lax.broadcasted_iota(jnp.int32, (size, size), 1)
    down = lax.broadcasted_iota(jnp.int32, (size, size), 0)
    spread = jnp.broadcast_to(row, (size, size))
    return jnp.sum(jnp.where(across == down, spread, jnp.zeros_like(spread)), axis=1, keepdims=True)


def later(x, reach):
    return jnp.concatenate([x[reach:], jnp.zeros((reach, x.shape[1]), x.dtype)], axis=0)


def learner_kernel(
    count, length_in, boards_in, actions_in, behaviour_in, regular_in, rewards_in, weights_in,
    policy_in, value_in, own, next1, next2, next3,
    grad, length, boards, weights, actions, behaviour, regular, rewards, policy_t, value_t, pairs, back_pairs,
    middle, last, masks, slope, turned, done,
):
    slots = boards.shape[3]
    role = lax.axis_index("role")
    y = lax.axis_index("dp") // (LINE * LINE)
    moves = [
        (weights_in.at[0:ROWS], weights.at[0:ROWS]),
        (boards_in, inner_cells(boards)),
        (weights_in.at[ROWS : 2 * ROWS], weights.at[ROWS : 2 * ROWS]),
        (actions_in, actions),
        (behaviour_in, behaviour),
        (regular_in, regular),
        (rewards_in, rewards),
        (policy_in, policy_t),
        (value_in, value_t),
        (length_in, length),
    ]
    copies = [pltpu.make_async_copy(a, b, done.at[k]) for k, (a, b) in enumerate(moves)]
    for copy in copies:
        copy.start()
    clear_border(boards)

    def make_pairs(layer):
        def kernel_of(p, q):
            at = layer * ROWS + (3 * p + q) * 128
            return weights[at : at + 128, :].astype(jnp.bfloat16)

        def store(block, value):
            pairs[layer, block * 128 : (block + 1) * 128, :] = value

        pair_kernels(kernel_of, store)

    clear_border(middle)
    clear_border(slope)
    copies[0].wait()
    make_pairs(0)
    copies[1].wait()

    def run_layer(layer, source, emit):
        for first in range(0, 10, count):
            pre = conv_pairs(source, pairs[layer], first, count)
            for parity in range(2):
                part = pre[:, parity * 128 : (parity + 1) * 128].reshape(count, 5, slots, 128)
                before = residual(source, first, count, parity).astype(jnp.float32)
                emit(first, parity, (before + jnp.maximum(part, 0.0)).astype(jnp.bfloat16))
                masks[layer, first : first + count, :, parity] = (part > 0).astype(jnp.bfloat16)

    run_layer(0, boards, lambda first, parity, value: put_cells(middle, first, count, parity, value))

    copies[2].wait()
    make_pairs(1)

    def to_last(first, parity, value):
        last[pl.ds(first, count), :, parity] = value

    run_layer(1, middle, to_last)

    for copy in copies[3:]:
        copy.wait()

    eight = jnp.concatenate(
        [
            policy_t[...].astype(jnp.float32),
            value_t[...].astype(jnp.float32),
            jnp.zeros((3, 128), jnp.float32),
        ],
        axis=0,
    )
    heads_t = jnp.concatenate(
        [eight, eight, eight, jnp.zeros((104, 128), jnp.float32)], axis=0
    ).astype(jnp.bfloat16)

    scores = lax.dot_general(
        last[...].reshape(-1, 128), heads_t, (((1,), (1,)), ((), ())),
        preferred_element_type=jnp.float32,
    ).reshape(100, slots, 128)
    lane = lax.broadcasted_iota(jnp.int32, (slots, 128), 1)
    weights_sum = jnp.sum(jnp.where(lane < 4, jnp.exp(scores), 0.0), axis=0)
    log_total = jnp.log(jnp.sum(weights_sum, axis=1, keepdims=True))
    action = column_of(actions[...])
    direction = action // 100
    cell = action - 100 * direction
    cells = lax.broadcasted_iota(jnp.int32, (100, slots, 128), 0)
    taken = (cells == cell[None]) & (lane % 8 == direction)[None]
    picked = jnp.sum(
        jnp.sum(jnp.where(taken & (lane < 4)[None], scores, 0.0), axis=0), axis=1, keepdims=True
    )
    value_sum = jnp.sum(scores, axis=0)
    value = jnp.tanh(
        jnp.sum(jnp.where(lane == 4, value_sum, 0.0), axis=1, keepdims=True) / 100.0
    )
    log_policy = picked - log_total

    positions = lax.broadcasted_iota(jnp.int32, (slots, 1), 0)
    live = (positions < length[0]).astype(jnp.float32)
    next_live = (positions + 1 < length[0]).astype(jnp.float32)
    ratio = jnp.minimum(1.0, jnp.exp(log_policy - column_of(behaviour[...])))
    shaped = column_of(rewards[...]) - ETA * (log_policy - column_of(regular[...]))
    next_values = later(value, 1) * next_live
    correction = live * ratio * (shaped + next_values - value)
    decay = live * ratio
    reach = 1
    while reach < slots:
        correction = correction + decay * later(correction, reach)
        decay = decay * later(decay, reach)
        reach *= 2
    targets = value + correction
    next_targets = later(targets, 1) * next_live
    policy_grad = -live * ratio * (shaped + next_targets - value)
    value_grad = -live * (targets - value)

    value_cell = value_grad * (1.0 - value * value) / 100.0
    by_policy = policy_grad[None] * (taken.astype(jnp.float32) - jnp.exp(scores - log_total[None]))
    by_score = jnp.where((lane % 8 == 4)[None], value_cell[None], by_policy)
    high = by_score.astype(jnp.bfloat16)
    rest = by_score - high.astype(jnp.float32)
    mid = rest.astype(jnp.bfloat16)
    low = rest - mid.astype(jnp.float32)
    parts = jnp.where(
        (lane < 8)[None],
        high.astype(jnp.float32),
        jnp.where((lane < 16)[None], mid.astype(jnp.float32), low),
    ).astype(jnp.bfloat16)
    out_grad = jnp.dot(
        parts.reshape(-1, 128), heads_t, preferred_element_type=jnp.float32
    )
    act_grad = (out_grad * masks[1].reshape(-1, 128).astype(jnp.float32)).astype(jnp.bfloat16)

    def kernel_of(p, q):
        at = ROWS + (8 - (3 * p + q)) * 128
        return weights[at : at + 128, :].T.astype(jnp.bfloat16)

    def store(block, value):
        back_pairs[block * 128 : (block + 1) * 128, :] = value

    pair_kernels(kernel_of, store)
    act_cells = act_grad.reshape(10, 5, 2, slots, 128)
    put_cells(slope, 0, 10, 0, act_cells[:, :, 0])
    put_cells(slope, 0, 10, 1, act_cells[:, :, 1])
    out_cells = out_grad.reshape(10, 5, 2, slots, 128)
    for first in range(0, 10, count):
        back = conv_pairs(slope, back_pairs[...], first, count)
        for parity in range(2):
            part = back[:, parity * 128 : (parity + 1) * 128].reshape(count, 5, slots, 128)
            total = out_cells[first : first + count, :, parity] + part
            gate = masks[0, first : first + count, :, parity].astype(jnp.float32)
            last[pl.ds(first, count), :, parity] = (total * gate).astype(jnp.bfloat16)
    turned[1] = act_grad.T
    turned[0] = last[...].reshape(-1, 128).T

    def layer_gradient(layer, source, core):
        kept = []
        for offset in range(9):
            parts = [x for x in segment_parts(layer, offset) if x[0] % 2 == core]
            if parts:
                kept.append((offset, parts))
        windows = []
        for offset, _ in kept:
            p, q = offset // 3, offset % 3
            cols = [source[p : p + 10, (j + q) // 2, (j + q) % 2] for j in range(10)]
            windows.append(jnp.stack(cols, axis=1).reshape(-1, 128))
        for pair in range(0, len(kept), 2):
            blocks = jnp.dot(
                turned[layer],
                jnp.concatenate(windows[pair : pair + 2], axis=1),
                preferred_element_type=jnp.float32,
            )
            for k in range(2):
                block = blocks[:, 128 * k : 128 * k + 128].T
                for segment, first, end, at in kept[pair + k][1]:
                    grad[segment // 2, first:end] = block[at : at + end - first]

    chunks = (own, next1, next2, next3)
    for layer, source in ((1, middle), (0, boards)):
        for core in range(2):
            pl.when(role == core)(functools.partial(layer_gradient, layer, source, core))
        for to_y in (2 * layer, 2 * layer + 1):
            for k, out in enumerate(chunks):

                @pl.when(lax.rem(y + k, LINE) == to_y)
                def _(to_y=to_y, k=k, out=out):
                    pltpu.make_async_copy(grad.at[to_y], out, done.at[k]).start()

    for k, out in enumerate(chunks):
        pltpu.make_async_copy(grad.at[0], out, done.at[k]).wait()


def learn(
    length, boards, actions, behaviour, regular, rewards, weights, policy_t, value_t, count=5
):
    slots = boards.shape[2]
    anywhere = pl.BlockSpec(memory_space=pltpu.HBM)
    cells = (10, 5, 2, slots, 128)
    around = (12, 6, 2, slots, 128)
    return pl.pallas_call(
        functools.partial(learner_kernel, count),
        out_shape=[jax.ShapeDtypeStruct((SEGMENT, 128), jnp.float32)] * LINE,
        in_specs=[anywhere] * 9,
        out_specs=[anywhere] * LINE,
        scratch_shapes=[
            pltpu.VMEM((LINE, SEGMENT, 128), jnp.float32),
            pltpu.SMEM((1,), jnp.int32),
            pltpu.VMEM(around, jnp.bfloat16),
            pltpu.VMEM((2 * ROWS, 128), jnp.float32),
            pltpu.VMEM((1, slots), jnp.int32),
            pltpu.VMEM((1, slots), jnp.float32),
            pltpu.VMEM((1, slots), jnp.float32),
            pltpu.VMEM((1, slots), jnp.float32),
            pltpu.VMEM(policy_t.shape, policy_t.dtype),
            pltpu.VMEM(value_t.shape, value_t.dtype),
            pltpu.VMEM((2, 1536, 256), jnp.bfloat16),
            pltpu.VMEM((1536, 256), jnp.bfloat16),
            pltpu.VMEM(around, jnp.bfloat16),
            pltpu.VMEM(cells, jnp.bfloat16),
            pltpu.VMEM((2,) + cells, jnp.bfloat16),
            pltpu.VMEM(around, jnp.bfloat16),
            pltpu.VMEM((2, 128, 100 * slots), jnp.bfloat16),
            pltpu.SemaphoreType.DMA((10,)),
        ],
        compiler_params=pltpu.CompilerParams(vmem_limit_bytes=60 * 1024 * 1024),
        cost_estimate=pl.CostEstimate(
            flops=4 * 10**9, bytes_accessed=3 * 10**6, transcendentals=10000
        ),
        name="learn",
    )(length, boards, actions, behaviour, regular, rewards, weights, policy_t, value_t)


def pull_kernel(own_in, first_in, second_in, own, both, first, second, done):
    moves = [(own_in, own), (first_in, first), (second_in, second)]
    copies = [pltpu.make_async_copy(a, b, done.at[k]) for k, (a, b) in enumerate(moves)]
    for copy in copies:
        copy.start()
    for copy in copies:
        copy.wait()
    both[0:PIECE] = first[...]
    both[PIECE : 2 * PIECE] = second[...]


def pull(own, first, second):
    vmem = pl.BlockSpec(memory_space=pltpu.VMEM)
    rows = pltpu.VMEM((PIECE, 128), jnp.float32)
    return pl.pallas_call(
        pull_kernel,
        out_shape=[
            jax.ShapeDtypeStruct((SEGMENT, 128), jnp.float32),
            jax.ShapeDtypeStruct((2 * PIECE, 128), jnp.float32),
        ],
        in_specs=[pl.BlockSpec(memory_space=pltpu.HBM)] * 3,
        out_specs=[vmem, vmem],
        scratch_shapes=[rows, rows, pltpu.SemaphoreType.DMA((3,))],
        compiler_params=pltpu.CompilerParams(vmem_limit_bytes=16 * 1024 * 1024),
        name="pull",
    )(own, first, second)


def update_kernel(summed, squares, moments, torso_in, fresh, old, first, second, done):
    y = lax.axis_index("dp") // (LINE * LINE)
    start = pl.multiple_of((2 * y + lax.axis_index("role")) * SEGMENT, SEGMENT)
    fetch = pltpu.make_async_copy(torso_in.at[pl.ds(start, SEGMENT)], old, done)
    fetch.start()
    square_sum = jnp.sum(squares[...], axis=1, keepdims=True)
    factor = jnp.minimum(1.0, jnp.sqrt(256.0 * ROWS) / jnp.sqrt(square_sum + NORM_EPS))
    for x in range(2):
        for z in range(LINE):
            rows = slice((LINE * x + z) * PIECE, (LINE * x + z + 1) * PIECE)
            first[rows] = moments[z, x, 0:PIECE]
            second[rows] = moments[z, x, PIECE : 2 * PIECE]
    fetch.wait()
    clipped = summed[...] * factor
    moment_one = BETA_ONE * first[...] + (1.0 - BETA_ONE) * clipped
    moment_two = BETA_TWO * second[...] + (1.0 - BETA_TWO) * clipped * clipped
    fresh[...] = old[...] - LEARN_RATE * moment_one / (jnp.sqrt(moment_two) + ADAM_EPS)


def update(summed, squares, moments, torso):
    vmem = pl.BlockSpec(memory_space=pltpu.VMEM)
    rows = pltpu.VMEM((SEGMENT, 128), jnp.float32)
    return pl.pallas_call(
        update_kernel,
        out_shape=jax.ShapeDtypeStruct((SEGMENT, 128), jnp.float32),
        in_specs=[
            vmem, vmem, vmem, pl.BlockSpec(memory_space=pltpu.HBM)
        ],
        out_specs=vmem,
        scratch_shapes=[rows, rows, rows, pltpu.SemaphoreType.DMA],
        compiler_params=pltpu.CompilerParams(vmem_limit_bytes=16 * 1024 * 1024),
        name="update",
    )(summed, squares, moments, torso)


def shifted(x, axis, step):
    stride = {"y": LINE * LINE, "x": LINE, "z": 1}[axis]
    pairs = []
    for d in range(LINE**3):
        at = d // stride % LINE
        pairs.append((d, d + ((at + step) % LINE - at) * stride))
    return lax.ppermute(x, "dp", pairs)


def line_total(x, axis):
    return (x + shifted(x, axis, 2)) + (shifted(x, axis, 1) + shifted(x, axis, 3))


def line_place(pieces, at):
    whole = jnp.zeros((LINE,) + pieces[0].shape, pieces[0].dtype)
    for step, piece in enumerate(pieces):
        whole = lax.dynamic_update_index_in_dim(whole, piece, (at - step) % LINE, 0)
    return whole


def line_gather(x, axis, at):
    return line_place([x] + [shifted(x, axis, step) for step in range(1, LINE)], at)


def moments_along_x(own, role, x):
    def device(role, x, rest):
        return role * LINE**3 + rest // LINE * LINE * LINE + x * LINE + rest % LINE

    same, next_to = [], []
    for rest in range(LINE * LINE):
        for to_role in range(2):
            for to_x in range(LINE):
                to = device(to_role, to_x, rest)
                if to_x // 2 != to_role:
                    same.append((device(to_role, to_x ^ 2, rest), to))
                next_to.append((device(to_x // 2, 2 * to_role + 1 - to_x % 2, rest), to))
    same = jnp.where(x // 2 == role, own, lax.ppermute(own, ("role", "dp"), same))
    next_to = lax.ppermute(own, ("role", "dp"), next_to)
    even = x % 2 == 0
    return jnp.concatenate([jnp.where(even, same, next_to), jnp.where(even, next_to, same)])


def swapped_z(x, bit):
    return lax.ppermute(x, "dp", [(d, d ^ bit) for d in range(LINE**3)])


def moments_along_z(x, z):
    near = swapped_z(x, 1)
    pair = jnp.where(z % 2 == 0, jnp.stack([x, near]), jnp.stack([near, x]))
    far = swapped_z(pair, 2)
    return jnp.where(z < 2, jnp.concatenate([pair, far]), jnp.concatenate([far, pair]))


def role_swap(x):
    return lax.ppermute(x, "role", [(0, 1), (1, 0)])


def body(
    board_now,
    traj_boards,
    actions,
    lengths,
    behaviour,
    regular,
    rewards,
    torso,
    policy_head,
    value_head,
    first_moment,
    second_moment,
):
    role = lax.axis_index("role")
    dp = lax.axis_index("dp")
    y, x, z = dp // (LINE * LINE), dp // LINE % LINE, dp % LINE
    own, next1, next2, next3 = learn(
        lengths,
        by_cell(traj_boards[0]),
        actions,
        behaviour,
        regular,
        rewards,
        torso,
        policy_head.T,
        value_head[None],
    )
    own, moments = pull(own, first_moment, second_moment)
    next2 = shifted(next2, "y", 2)
    moments = moments_along_x(moments, role, x)
    moments = moments_along_z(moments, z)
    summed = (own + next2) + (shifted(next1, "y", 1) + shifted(next3, "y", 3))
    summed = line_total(line_total(summed, "x"), "z")
    squares = jnp.sum(summed * summed, axis=0, keepdims=True)
    squares = line_total(squares + role_swap(squares), "y")
    fresh = update(summed, squares, moments.reshape(LINE, 2, 2 * PIECE, 128), torso)
    mine = line_gather(fresh, "y", y)
    other = role_swap(mine)
    boards, heads = stage(mine, by_cell(board_now), policy_head.T.astype(jnp.float32))
    here = act(mine, other, boards, heads)
    there = role_swap(here)
    at = (LINE * x + z) % (2 * LINE) * PIECE
    new_share = jnp.where(
        role == x // 2,
        lax.dynamic_slice(mine, (y, at, 0), (1, PIECE, 128))[0],
        lax.dynamic_slice(other, (y, at, 0), (1, PIECE, 128))[0],
    )
    move_logp = jnp.concatenate([jnp.where(role == 0, here, there), jnp.where(role == 0, there, here)])
    return (new_share, move_logp)


def solution(mesh):
    return jax.shard_map(
        body,
        mesh=mesh,
        in_specs=(
            P("dp", None, None, None),
            P("dp", None, None, None, None),
            P("dp", None),
            P("dp"),
            P("dp", None),
            P("dp", None),
            P("dp", None),
            P(),
            P(),
            P(),
            P("dp", None),
            P("dp", None),
        ),
        out_specs=(P("dp", None), P("dp", None)),
        check_vma=False,
    )
```

```python
import functools

import jax
import jax.numpy as jnp
from jax import lax
from jax.experimental import pallas as pl
from jax.experimental.pallas import tpu as pltpu
from jax.sharding import PartitionSpec as P

ETA = 0.2
LEARN_RATE = 0.03
BETA_ONE = 0.9
BETA_TWO = 0.999
ADAM_EPS = 1e-08
NORM_EPS = 1e-12
ROWS = 1152
LINE = 4
SEGMENT = 2 * ROWS // (2 * LINE)
PIECE = SEGMENT // 8


def by_cell(boards):
    return jnp.transpose(boards, (1, 2, 0, 3))


def inner_cells(ref):
    return ref.reshape((12, 12) + ref.shape[3:]).at[1:11, 1:11]


def segment_parts(layer, offset):
    start = layer * ROWS + offset * 128
    at, parts = start, []
    while at < start + 128:
        segment = at // SEGMENT
        end = min(start + 128, (segment + 1) * SEGMENT)
        parts.append((segment, at - segment * SEGMENT, end - segment * SEGMENT, at - start))
        at = end
    return parts


def clear_border(ref):
    zero_row = jnp.zeros(ref.shape[1:], ref.dtype)
    ref[0] = zero_row
    ref[11] = zero_row
    zero_col = jnp.zeros((12,) + ref.shape[3:], ref.dtype)
    ref[:, 0, 0] = zero_col
    ref[:, 5, 1] = zero_col


def pair_kernels(kernel_of, store):
    nothing = jnp.zeros((128, 128), jnp.bfloat16)
    for p in range(3):
        row = [kernel_of(p, q) for q in range(3)]
        for q in range(4):
            left = row[q] if q < 3 else nothing
            right = row[q - 1] if q > 0 else nothing
            store(4 * p + q, jnp.concatenate([left, right], axis=1))


def conv_pairs(source, pair_weights, first, count):
    windows = []
    for p in range(3):
        for q in range(4):
            window = source[pl.ds(first + p, count), q // 2 : q // 2 + 5, q % 2]
            windows.append(window.reshape(-1, 128))
    return jnp.dot(
        jnp.concatenate(windows, axis=1), pair_weights, preferred_element_type=jnp.float32
    )


def residual(source, first, count, parity):
    if parity == 0:
        window = source[pl.ds(first + 1, count), 0:5, 1]
    else:
        window = source[pl.ds(first + 1, count), 1:6, 0]
    return window


def put_cells(target, first, count, parity, value):
    if parity == 0:
        target[pl.ds(first + 1, count), 0:5, 1] = value
    else:
        target[pl.ds(first + 1, count), 1:6, 0] = value


def stage_kernel(mine, boards_in, policy_t, boards, heads, done):
    games = boards.shape[3]
    half = pl.ds(pl.multiple_of(lax.axis_index("role") * games, games), games)
    fetch = pltpu.make_async_copy(boards_in.at[:, :, half], inner_cells(boards), done)
    fetch.start()
    clear_border(boards)
    spread = lax.broadcasted_iota(jnp.int32, (4, 1280), 1)
    row = lax.broadcasted_iota(jnp.int32, (4, 1280), 0)
    spread = (spread % 128 == 10 * row + spread // 128).astype(jnp.float32)
    by_column = lax.dot_general(
        policy_t[...], spread, (((0,), (0,)), ((), ())), preferred_element_type=jnp.float32
    )
    for j in range(10):
        heads[128 * j : 128 * j + 128, :] = by_column[:, 128 * j : 128 * j + 128].astype(jnp.bfloat16)
    fetch.wait()


def stage(mine, boards, policy_t):
    games = boards.shape[2] // 2
    vmem = pl.BlockSpec(memory_space=pltpu.VMEM)
    anywhere = pl.BlockSpec(memory_space=pltpu.HBM)
    return pl.pallas_call(
        stage_kernel,
        out_shape=[
            jax.ShapeDtypeStruct((12, 6, 2, games, 128), jnp.bfloat16),
            jax.ShapeDtypeStruct((1280, 128), jnp.bfloat16),
        ],
        in_specs=[anywhere, anywhere, vmem],
        out_specs=[vmem, vmem],
        scratch_shapes=[pltpu.SemaphoreType.DMA],
        compiler_params=pltpu.CompilerParams(vmem_limit_bytes=16 * 1024 * 1024),
        cost_estimate=pl.CostEstimate(
            flops=10**9, bytes_accessed=4 * 10**6, transcendentals=0
        ),
        name="stage",
    )(mine, boards, policy_t)


def actor_kernel(count, unroll, mine, other, boards, heads, out, pairs, middle, last):
    games = boards.shape[3]
    role = lax.axis_index("role")
    for layer in range(2):
        def kernel_of(p, q, layer=layer):
            parts = []
            for segment, first, last_row, _ in segment_parts(layer, 3 * p + q):
                y, owner = segment // 2, segment % 2
                rows = slice(first, last_row)
                parts.append(jnp.where(role == owner, mine[y, rows], other[y, rows]))
            return jnp.concatenate(parts, axis=0).astype(jnp.bfloat16)

        def store(block, value, layer=layer):
            pairs[layer, block * 128 : (block + 1) * 128, :] = value

        pair_kernels(kernel_of, store)
    clear_border(middle)

    def run_layer(layer, source, emit):
        def step(at, carry):
            first = at * count
            pre = conv_pairs(source, pairs[layer], first, count)
            for parity in range(2):
                part = pre[:, parity * 128 : (parity + 1) * 128].reshape(count, 5, games, 128)
                before = residual(source, first, count, parity).astype(jnp.float32)
                emit(first, parity, (before + jnp.maximum(part, 0.0)).astype(jnp.bfloat16))
            return carry

        lax.fori_loop(0, 10 // count, step, 0, unroll=unroll)

    run_layer(0, boards, lambda first, parity, value: put_cells(middle, first, count, parity, value))

    def to_last(first, parity, value):
        last[pl.ds(first, count), :, parity] = value

    run_layer(1, middle, to_last)
    cells = [last[:, j // 2, j % 2].reshape(-1, 128) for j in range(10)]
    logits = jnp.dot(jnp.concatenate(cells, axis=1), heads[...], preferred_element_type=jnp.float32)
    logits = logits.reshape(10, games, 128)
    lanes = lax.broadcasted_iota(jnp.int32, (games, 128), 1)
    moves = []
    total = jnp.zeros((games, 1), jnp.float32)
    for d in range(4):
        gathered = jnp.zeros((games, 128), jnp.float32)
        for i in range(10):
            turned = pltpu.roll(logits[i], (10 * i - 10 * d) % 128, 1)
            gathered = jnp.where((lanes >= 10 * i) & (lanes < 10 * i + 10), turned, gathered)
        moves.append(gathered)
        total = total + jnp.sum(
            jnp.where(lanes < 100, jnp.exp(gathered), 0.0), axis=1, keepdims=True
        )
    log_total = jnp.log(total)
    for d in range(4):
        out[:, 100 * d : 100 * d + 100] = (moves[d] - log_total)[:, :100]


def act(mine, other, boards, heads, count=2, unroll=5):
    games = boards.shape[3]
    vmem = pl.BlockSpec(memory_space=pltpu.VMEM)
    return pl.pallas_call(
        functools.partial(actor_kernel, count, unroll),
        out_shape=jax.ShapeDtypeStruct((games, 400), jnp.float32),
        in_specs=[vmem] * 4,
        out_specs=vmem,
        scratch_shapes=[
            pltpu.VMEM((2, 1536, 256), jnp.bfloat16),
            pltpu.VMEM((12, 6, 2, games, 128), jnp.bfloat16),
            pltpu.VMEM((10, 5, 2, games, 128), jnp.bfloat16),
        ],
        compiler_params=pltpu.CompilerParams(vmem_limit_bytes=32 * 1024 * 1024),
        cost_estimate=pl.CostEstimate(
            flops=8 * 10**9, bytes_accessed=4 * 10**6, transcendentals=30000
        ),
        name="act",
    )(mine, other, boards, heads)


def column_of(row):
    size = row.shape[1]
    across = lax.broadcasted_iota(jnp.int32, (size, size), 1)
    down = lax.broadcasted_iota(jnp.int32, (size, size), 0)
    spread = jnp.broadcast_to(row, (size, size))
    return jnp.sum(jnp.where(across == down, spread, jnp.zeros_like(spread)), axis=1, keepdims=True)


def later(x, reach):
    return jnp.concatenate([x[reach:], jnp.zeros((reach, x.shape[1]), x.dtype)], axis=0)


def learner_kernel(
    count, length_in, boards_in, actions_in, behaviour_in, regular_in, rewards_in, weights_in,
    policy_in, value_in, own, next1, next2, next3,
    grad, length, boards, weights, actions, behaviour, regular, rewards, policy_t, value_t, pairs, back_pairs,
    middle, last, masks, slope, turned, done,
):
    slots = boards.shape[3]
    role = lax.axis_index("role")
    y = lax.axis_index("dp") // (LINE * LINE)
    moves = [
        (weights_in.at[0:ROWS], weights.at[0:ROWS]),
        (boards_in, inner_cells(boards)),
        (weights_in.at[ROWS : 2 * ROWS], weights.at[ROWS : 2 * ROWS]),
        (actions_in, actions),
        (behaviour_in, behaviour),
        (regular_in, regular),
        (rewards_in, rewards),
        (policy_in, policy_t),
        (value_in, value_t),
        (length_in, length),
    ]
    copies = [pltpu.make_async_copy(a, b, done.at[k]) for k, (a, b) in enumerate(moves)]
    for copy in copies:
        copy.start()
    clear_border(boards)

    def make_pairs(layer):
        def kernel_of(p, q):
            at = layer * ROWS + (3 * p + q) * 128
            return weights[at : at + 128, :].astype(jnp.bfloat16)

        def store(block, value):
            pairs[layer, block * 128 : (block + 1) * 128, :] = value

        pair_kernels(kernel_of, store)

    clear_border(middle)
    clear_border(slope)
    copies[0].wait()
    make_pairs(0)
    copies[1].wait()

    def run_layer(layer, source, emit):
        for first in range(0, 10, count):
            pre = conv_pairs(source, pairs[layer], first, count)
            for parity in range(2):
                part = pre[:, parity * 128 : (parity + 1) * 128].reshape(count, 5, slots, 128)
                before = residual(source, first, count, parity).astype(jnp.float32)
                emit(first, parity, (before + jnp.maximum(part, 0.0)).astype(jnp.bfloat16))
                masks[layer, first : first + count, :, parity] = (part > 0).astype(jnp.bfloat16)

    run_layer(0, boards, lambda first, parity, value: put_cells(middle, first, count, parity, value))

    copies[2].wait()
    make_pairs(1)

    def to_last(first, parity, value):
        last[pl.ds(first, count), :, parity] = value

    run_layer(1, middle, to_last)

    for copy in copies[3:]:
        copy.wait()

    eight = jnp.concatenate(
        [
            policy_t[...].astype(jnp.float32),
            value_t[...].astype(jnp.float32),
            jnp.zeros((3, 128), jnp.float32),
        ],
        axis=0,
    )
    heads_t = jnp.concatenate(
        [eight, eight, eight, jnp.zeros((104, 128), jnp.float32)], axis=0
    ).astype(jnp.bfloat16)

    scores = lax.dot_general(
        last[...].reshape(-1, 128), heads_t, (((1,), (1,)), ((), ())),
        preferred_element_type=jnp.float32,
    ).reshape(100, slots, 128)
    lane = lax.broadcasted_iota(jnp.int32, (slots, 128), 1)
    weights_sum = jnp.sum(jnp.where(lane < 4, jnp.exp(scores), 0.0), axis=0)
    log_total = jnp.log(jnp.sum(weights_sum, axis=1, keepdims=True))
    action = column_of(actions[...])
    direction = action // 100
    cell = action - 100 * direction
    cells = lax.broadcasted_iota(jnp.int32, (100, slots, 128), 0)
    taken = (cells == cell[None]) & (lane % 8 == direction)[None]
    picked = jnp.sum(
        jnp.sum(jnp.where(taken & (lane < 4)[None], scores, 0.0), axis=0), axis=1, keepdims=True
    )
    value_sum = jnp.sum(scores, axis=0)
    value = jnp.tanh(
        jnp.sum(jnp.where(lane == 4, value_sum, 0.0), axis=1, keepdims=True) / 100.0
    )
    log_policy = picked - log_total

    positions = lax.broadcasted_iota(jnp.int32, (slots, 1), 0)
    live = (positions < length[0]).astype(jnp.float32)
    next_live = (positions + 1 < length[0]).astype(jnp.float32)
    ratio = jnp.minimum(1.0, jnp.exp(log_policy - column_of(behaviour[...])))
    shaped = column_of(rewards[...]) - ETA * (log_policy - column_of(regular[...]))
    next_values = later(value, 1) * next_live
    correction = live * ratio * (shaped + next_values - value)
    decay = live * ratio
    reach = 1
    while reach < slots:
        correction = correction + decay * later(correction, reach)
        decay = decay * later(decay, reach)
        reach *= 2
    targets = value + correction
    next_targets = later(targets, 1) * next_live
    policy_grad = -live * ratio * (shaped + next_targets - value)
    value_grad = -live * (targets - value)

    value_cell = value_grad * (1.0 - value * value) / 100.0
    by_policy = policy_grad[None] * (taken.astype(jnp.float32) - jnp.exp(scores - log_total[None]))
    by_score = jnp.where((lane % 8 == 4)[None], value_cell[None], by_policy)
    high = by_score.astype(jnp.bfloat16)
    rest = by_score - high.astype(jnp.float32)
    mid = rest.astype(jnp.bfloat16)
    low = rest - mid.astype(jnp.float32)
    parts = jnp.where(
        (lane < 8)[None],
        high.astype(jnp.float32),
        jnp.where((lane < 16)[None], mid.astype(jnp.float32), low),
    ).astype(jnp.bfloat16)
    out_grad = jnp.dot(
        parts.reshape(-1, 128), heads_t, preferred_element_type=jnp.float32
    )
    act_grad = (out_grad * masks[1].reshape(-1, 128).astype(jnp.float32)).astype(jnp.bfloat16)

    def kernel_of(p, q):
        at = ROWS + (8 - (3 * p + q)) * 128
        return weights[at : at + 128, :].T.astype(jnp.bfloat16)

    def store(block, value):
        back_pairs[block * 128 : (block + 1) * 128, :] = value

    pair_kernels(kernel_of, store)
    act_cells = act_grad.reshape(10, 5, 2, slots, 128)
    put_cells(slope, 0, 10, 0, act_cells[:, :, 0])
    put_cells(slope, 0, 10, 1, act_cells[:, :, 1])
    out_cells = out_grad.reshape(10, 5, 2, slots, 128)
    for first in range(0, 10, count):
        back = conv_pairs(slope, back_pairs[...], first, count)
        for parity in range(2):
            part = back[:, parity * 128 : (parity + 1) * 128].reshape(count, 5, slots, 128)
            total = out_cells[first : first + count, :, parity] + part
            gate = masks[0, first : first + count, :, parity].astype(jnp.float32)
            last[pl.ds(first, count), :, parity] = (total * gate).astype(jnp.bfloat16)
    turned[1] = act_grad.T
    turned[0] = last[...].reshape(-1, 128).T

    def layer_gradient(layer, source, core):
        kept = []
        for offset in range(9):
            parts = [x for x in segment_parts(layer, offset) if x[0] % 2 == core]
            if parts:
                kept.append((offset, parts))
        windows = []
        for offset, _ in kept:
            p, q = offset // 3, offset % 3
            cols = [source[p : p + 10, (j + q) // 2, (j + q) % 2] for j in range(10)]
            windows.append(jnp.stack(cols, axis=1).reshape(-1, 128))
        for pair in range(0, len(kept), 2):
            blocks = jnp.dot(
                turned[layer],
                jnp.concatenate(windows[pair : pair + 2], axis=1),
                preferred_element_type=jnp.float32,
            )
            for k in range(2):
                block = blocks[:, 128 * k : 128 * k + 128].T
                for segment, first, end, at in kept[pair + k][1]:
                    grad[segment // 2, first:end] = block[at : at + end - first]

    chunks = (own, next1, next2, next3)
    for layer, source in ((1, middle), (0, boards)):
        for core in range(2):
            pl.when(role == core)(functools.partial(layer_gradient, layer, source, core))
        for to_y in (2 * layer, 2 * layer + 1):
            for k, out in enumerate(chunks):

                @pl.when(lax.rem(y + k, LINE) == to_y)
                def _(to_y=to_y, k=k, out=out):
                    pltpu.make_async_copy(grad.at[to_y], out, done.at[k]).start()

    for k, out in enumerate(chunks):
        pltpu.make_async_copy(grad.at[0], out, done.at[k]).wait()


def learn(
    length, boards, actions, behaviour, regular, rewards, weights, policy_t, value_t, count=5
):
    slots = boards.shape[2]
    anywhere = pl.BlockSpec(memory_space=pltpu.HBM)
    cells = (10, 5, 2, slots, 128)
    around = (12, 6, 2, slots, 128)
    return pl.pallas_call(
        functools.partial(learner_kernel, count),
        out_shape=[jax.ShapeDtypeStruct((SEGMENT, 128), jnp.float32)] * LINE,
        in_specs=[anywhere] * 9,
        out_specs=[anywhere] * LINE,
        scratch_shapes=[
            pltpu.VMEM((LINE, SEGMENT, 128), jnp.float32),
            pltpu.SMEM((1,), jnp.int32),
            pltpu.VMEM(around, jnp.bfloat16),
            pltpu.VMEM((2 * ROWS, 128), jnp.float32),
            pltpu.VMEM((1, slots), jnp.int32),
            pltpu.VMEM((1, slots), jnp.float32),
            pltpu.VMEM((1, slots), jnp.float32),
            pltpu.VMEM((1, slots), jnp.float32),
            pltpu.VMEM(policy_t.shape, policy_t.dtype),
            pltpu.VMEM(value_t.shape, value_t.dtype),
            pltpu.VMEM((2, 1536, 256), jnp.bfloat16),
            pltpu.VMEM((1536, 256), jnp.bfloat16),
            pltpu.VMEM(around, jnp.bfloat16),
            pltpu.VMEM(cells, jnp.bfloat16),
            pltpu.VMEM((2,) + cells, jnp.bfloat16),
            pltpu.VMEM(around, jnp.bfloat16),
            pltpu.VMEM((2, 128, 100 * slots), jnp.bfloat16),
            pltpu.SemaphoreType.DMA((10,)),
        ],
        compiler_params=pltpu.CompilerParams(vmem_limit_bytes=60 * 1024 * 1024),
        cost_estimate=pl.CostEstimate(
            flops=4 * 10**9, bytes_accessed=3 * 10**6, transcendentals=10000
        ),
        name="learn",
    )(length, boards, actions, behaviour, regular, rewards, weights, policy_t, value_t)


def pull_kernel(own_in, first_in, second_in, own, both, first, second, done):
    moves = [(own_in, own), (first_in, first), (second_in, second)]
    copies = [pltpu.make_async_copy(a, b, done.at[k]) for k, (a, b) in enumerate(moves)]
    for copy in copies:
        copy.start()
    for copy in copies:
        copy.wait()
    both[0:PIECE] = first[...]
    both[PIECE : 2 * PIECE] = second[...]


def pull(own, first, second):
    vmem = pl.BlockSpec(memory_space=pltpu.VMEM)
    rows = pltpu.VMEM((PIECE, 128), jnp.float32)
    return pl.pallas_call(
        pull_kernel,
        out_shape=[
            jax.ShapeDtypeStruct((SEGMENT, 128), jnp.float32),
            jax.ShapeDtypeStruct((2 * PIECE, 128), jnp.float32),
        ],
        in_specs=[pl.BlockSpec(memory_space=pltpu.HBM)] * 3,
        out_specs=[vmem, vmem],
        scratch_shapes=[rows, rows, pltpu.SemaphoreType.DMA((3,))],
        compiler_params=pltpu.CompilerParams(vmem_limit_bytes=16 * 1024 * 1024),
        name="pull",
    )(own, first, second)


def update_kernel(summed, squares, moments, torso_in, fresh, old, first, second, done):
    y = lax.axis_index("dp") // (LINE * LINE)
    start = pl.multiple_of((2 * y + lax.axis_index("role")) * SEGMENT, SEGMENT)
    fetch = pltpu.make_async_copy(torso_in.at[pl.ds(start, SEGMENT)], old, done)
    fetch.start()
    square_sum = jnp.sum(squares[...], axis=1, keepdims=True)
    factor = jnp.minimum(1.0, jnp.sqrt(256.0 * ROWS) / jnp.sqrt(square_sum + NORM_EPS))
    for x in range(2):
        for z in range(LINE):
            rows = slice((LINE * x + z) * PIECE, (LINE * x + z + 1) * PIECE)
            first[rows] = moments[z, x, 0:PIECE]
            second[rows] = moments[z, x, PIECE : 2 * PIECE]
    fetch.wait()
    clipped = summed[...] * factor
    moment_one = BETA_ONE * first[...] + (1.0 - BETA_ONE) * clipped
    moment_two = BETA_TWO * second[...] + (1.0 - BETA_TWO) * clipped * clipped
    fresh[...] = old[...] - LEARN_RATE * moment_one / (jnp.sqrt(moment_two) + ADAM_EPS)


def update(summed, squares, moments, torso):
    vmem = pl.BlockSpec(memory_space=pltpu.VMEM)
    rows = pltpu.VMEM((SEGMENT, 128), jnp.float32)
    return pl.pallas_call(
        update_kernel,
        out_shape=jax.ShapeDtypeStruct((SEGMENT, 128), jnp.float32),
        in_specs=[
            vmem, vmem, vmem, pl.BlockSpec(memory_space=pltpu.HBM)
        ],
        out_specs=vmem,
        scratch_shapes=[rows, rows, rows, pltpu.SemaphoreType.DMA],
        compiler_params=pltpu.CompilerParams(vmem_limit_bytes=16 * 1024 * 1024),
        name="update",
    )(summed, squares, moments, torso)


def shifted(x, axis, step):
    stride = {"y": LINE * LINE, "x": LINE, "z": 1}[axis]
    pairs = []
    for d in range(LINE**3):
        at = d // stride % LINE
        pairs.append((d, d + ((at + step) % LINE - at) * stride))
    return lax.ppermute(x, "dp", pairs)


def line_total(x, axis):
    return (x + shifted(x, axis, 2)) + (shifted(x, axis, 1) + shifted(x, axis, 3))


def line_place(pieces, at):
    whole = jnp.zeros((LINE,) + pieces[0].shape, pieces[0].dtype)
    for step, piece in enumerate(pieces):
        whole = lax.dynamic_update_index_in_dim(whole, piece, (at - step) % LINE, 0)
    return whole


def line_gather(x, axis, at):
    return line_place([x] + [shifted(x, axis, step) for step in range(1, LINE)], at)


def moments_along_x(own, role, x):
    def device(role, x, rest):
        return role * LINE**3 + rest // LINE * LINE * LINE + x * LINE + rest % LINE

    same, next_to = [], []
    for rest in range(LINE * LINE):
        for to_role in range(2):
            for to_x in range(LINE):
                to = device(to_role, to_x, rest)
                if to_x // 2 != to_role:
                    same.append((device(to_role, to_x ^ 2, rest), to))
                next_to.append((device(to_x // 2, 2 * to_role + 1 - to_x % 2, rest), to))
    same = jnp.where(x // 2 == role, own, lax.ppermute(own, ("role", "dp"), same))
    next_to = lax.ppermute(own, ("role", "dp"), next_to)
    even = x % 2 == 0
    return jnp.concatenate([jnp.where(even, same, next_to), jnp.where(even, next_to, same)])


def swapped_z(x, bit):
    return lax.ppermute(x, "dp", [(d, d ^ bit) for d in range(LINE**3)])


def moments_along_z(x, z):
    far = swapped_z(x, 2)
    pair = jnp.where(z < 2, jnp.stack([x, far]), jnp.stack([far, x]))
    near = swapped_z(pair, 1)
    even = z % 2 == 0
    return jnp.stack([jnp.where(even, pair, near), jnp.where(even, near, pair)], axis=1)


def pair_total_y(x):
    for partner in ((1, 0, 3, 2), (3, 2, 1, 0)):
        plane = LINE * LINE
        pairs = [(d, partner[d // plane] * plane + d % plane) for d in range(LINE**3)]
        x = x + lax.ppermute(x, "dp", pairs)
    return x


def role_swap(x):
    return lax.ppermute(x, "role", [(0, 1), (1, 0)])


def body(
    board_now,
    traj_boards,
    actions,
    lengths,
    behaviour,
    regular,
    rewards,
    torso,
    policy_head,
    value_head,
    first_moment,
    second_moment,
):
    role = lax.axis_index("role")
    dp = lax.axis_index("dp")
    y, x, z = dp // (LINE * LINE), dp // LINE % LINE, dp % LINE
    own, next1, next2, next3 = learn(
        lengths,
        by_cell(traj_boards[0]),
        actions,
        behaviour,
        regular,
        rewards,
        torso,
        policy_head.T,
        value_head[None],
    )
    own, moments = pull(own, first_moment, second_moment)
    next2 = shifted(next2, "y", 2)
    moments = moments_along_x(moments, role, x)
    moments = moments_along_z(moments, z)
    summed = (own + next2) + (shifted(next1, "y", 1) + shifted(next3, "y", 3))
    summed = line_total(line_total(summed, "x"), "z")
    squares = jnp.sum(summed * summed, axis=0, keepdims=True)
    squares = pair_total_y(squares + role_swap(squares))
    fresh = update(summed, squares, moments.reshape(LINE, 2, 2 * PIECE, 128), torso)
    mine = line_gather(fresh, "y", y)
    other = role_swap(mine)
    boards, heads = stage(mine, by_cell(board_now), policy_head.T.astype(jnp.float32))
    here = act(mine, other, boards, heads)
    there = role_swap(here)
    at = (LINE * x + z) % (2 * LINE) * PIECE
    new_share = jnp.where(
        role == x // 2,
        lax.dynamic_slice(mine, (y, at, 0), (1, PIECE, 128))[0],
        lax.dynamic_slice(other, (y, at, 0), (1, PIECE, 128))[0],
    )
    move_logp = jnp.concatenate([jnp.where(role == 0, here, there), jnp.where(role == 0, there, here)])
    return (new_share, move_logp)


def solution(mesh):
    return jax.shard_map(
        body,
        mesh=mesh,
        in_specs=(
            P("dp", None, None, None),
            P("dp", None, None, None, None),
            P("dp", None),
            P("dp"),
            P("dp", None),
            P("dp", None),
            P("dp", None),
            P(),
            P(),
            P(),
            P("dp", None),
            P("dp", None),
        ),
        out_specs=(P("dp", None), P("dp", None)),
        check_vma=False,
    )
```

```python
import functools

import jax
import jax.numpy as jnp
from jax import lax
from jax.experimental import pallas as pl
from jax.experimental.pallas import tpu as pltpu
from jax.sharding import PartitionSpec as P

ETA = 0.2
LEARN_RATE = 0.03
BETA_ONE = 0.9
BETA_TWO = 0.999
ADAM_EPS = 1e-08
NORM_EPS = 1e-12
ROWS = 1152
LINE = 4
SEGMENT = 2 * ROWS // (2 * LINE)
PIECE = SEGMENT // 8


def by_cell(boards):
    return jnp.transpose(boards, (1, 2, 0, 3))


def inner_cells(ref):
    return ref.reshape((12, 12) + ref.shape[3:]).at[1:11, 1:11]


def segment_parts(layer, offset):
    start = layer * ROWS + offset * 128
    at, parts = start, []
    while at < start + 128:
        segment = at // SEGMENT
        end = min(start + 128, (segment + 1) * SEGMENT)
        parts.append((segment, at - segment * SEGMENT, end - segment * SEGMENT, at - start))
        at = end
    return parts


def clear_border(ref):
    zero_row = jnp.zeros(ref.shape[1:], ref.dtype)
    ref[0] = zero_row
    ref[11] = zero_row
    zero_col = jnp.zeros((12,) + ref.shape[3:], ref.dtype)
    ref[:, 0, 0] = zero_col
    ref[:, 5, 1] = zero_col


def pair_kernels(kernel_of, store):
    nothing = jnp.zeros((128, 128), jnp.bfloat16)
    for p in range(3):
        row = [kernel_of(p, q) for q in range(3)]
        for q in range(4):
            left = row[q] if q < 3 else nothing
            right = row[q - 1] if q > 0 else nothing
            store(4 * p + q, jnp.concatenate([left, right], axis=1))


def conv_pairs(source, pair_weights, first, count):
    windows = []
    for p in range(3):
        for q in range(4):
            window = source[pl.ds(first + p, count), q // 2 : q // 2 + 5, q % 2]
            windows.append(window.reshape(-1, 128))
    return jnp.dot(
        jnp.concatenate(windows, axis=1), pair_weights, preferred_element_type=jnp.float32
    )


def residual(source, first, count, parity):
    if parity == 0:
        window = source[pl.ds(first + 1, count), 0:5, 1]
    else:
        window = source[pl.ds(first + 1, count), 1:6, 0]
    return window


def put_cells(target, first, count, parity, value):
    if parity == 0:
        target[pl.ds(first + 1, count), 0:5, 1] = value
    else:
        target[pl.ds(first + 1, count), 1:6, 0] = value


def stage_kernel(mine, boards_in, policy_t, boards, heads, done):
    games = boards.shape[3]
    half = pl.ds(pl.multiple_of(lax.axis_index("role") * games, games), games)
    fetch = pltpu.make_async_copy(boards_in.at[:, :, half], inner_cells(boards), done)
    fetch.start()
    clear_border(boards)
    spread = lax.broadcasted_iota(jnp.int32, (4, 1280), 1)
    row = lax.broadcasted_iota(jnp.int32, (4, 1280), 0)
    spread = (spread % 128 == 10 * row + spread // 128).astype(jnp.float32)
    by_column = lax.dot_general(
        policy_t[...], spread, (((0,), (0,)), ((), ())), preferred_element_type=jnp.float32
    )
    for j in range(10):
        heads[128 * j : 128 * j + 128, :] = by_column[:, 128 * j : 128 * j + 128].astype(jnp.bfloat16)
    fetch.wait()


def stage(mine, boards, policy_t):
    games = boards.shape[2] // 2
    vmem = pl.BlockSpec(memory_space=pltpu.VMEM)
    anywhere = pl.BlockSpec(memory_space=pltpu.HBM)
    return pl.pallas_call(
        stage_kernel,
        out_shape=[
            jax.ShapeDtypeStruct((12, 6, 2, games, 128), jnp.bfloat16),
            jax.ShapeDtypeStruct((1280, 128), jnp.bfloat16),
        ],
        in_specs=[anywhere, anywhere, vmem],
        out_specs=[vmem, vmem],
        scratch_shapes=[pltpu.SemaphoreType.DMA],
        compiler_params=pltpu.CompilerParams(vmem_limit_bytes=16 * 1024 * 1024),
        cost_estimate=pl.CostEstimate(
            flops=10**9, bytes_accessed=4 * 10**6, transcendentals=0
        ),
        name="stage",
    )(mine, boards, policy_t)


def actor_kernel(count, unroll, mine, other, boards, heads, out, pairs, middle, last):
    games = boards.shape[3]
    role = lax.axis_index("role")
    for layer in range(2):
        def kernel_of(p, q, layer=layer):
            parts = []
            for segment, first, last_row, _ in segment_parts(layer, 3 * p + q):
                y, owner = segment // 2, segment % 2
                rows = slice(first, last_row)
                parts.append(jnp.where(role == owner, mine[y, rows], other[y, rows]))
            return jnp.concatenate(parts, axis=0).astype(jnp.bfloat16)

        def store(block, value, layer=layer):
            pairs[layer, block * 128 : (block + 1) * 128, :] = value

        pair_kernels(kernel_of, store)
    clear_border(middle)

    def run_layer(layer, source, emit):
        def step(at, carry):
            first = at * count
            pre = conv_pairs(source, pairs[layer], first, count)
            for parity in range(2):
                part = pre[:, parity * 128 : (parity + 1) * 128].reshape(count, 5, games, 128)
                before = residual(source, first, count, parity).astype(jnp.float32)
                emit(first, parity, (before + jnp.maximum(part, 0.0)).astype(jnp.bfloat16))
            return carry

        lax.fori_loop(0, 10 // count, step, 0, unroll=unroll)

    run_layer(0, boards, lambda first, parity, value: put_cells(middle, first, count, parity, value))

    def to_last(first, parity, value):
        last[pl.ds(first, count), :, parity] = value

    run_layer(1, middle, to_last)
    cells = [last[:, j // 2, j % 2].reshape(-1, 128) for j in range(10)]
    logits = jnp.dot(jnp.concatenate(cells, axis=1), heads[...], preferred_element_type=jnp.float32)
    logits = logits.reshape(10, games, 128)
    lanes = lax.broadcasted_iota(jnp.int32, (games, 128), 1)
    moves = []
    total = jnp.zeros((games, 1), jnp.float32)
    for d in range(4):
        gathered = jnp.zeros((games, 128), jnp.float32)
        for i in range(10):
            turned = pltpu.roll(logits[i], (10 * i - 10 * d) % 128, 1)
            gathered = jnp.where((lanes >= 10 * i) & (lanes < 10 * i + 10), turned, gathered)
        moves.append(gathered)
        total = total + jnp.sum(
            jnp.where(lanes < 100, jnp.exp(gathered), 0.0), axis=1, keepdims=True
        )
    log_total = jnp.log(total)
    for d in range(4):
        out[:, 100 * d : 100 * d + 100] = (moves[d] - log_total)[:, :100]


def act(mine, other, boards, heads, count=2, unroll=5):
    games = boards.shape[3]
    vmem = pl.BlockSpec(memory_space=pltpu.VMEM)
    return pl.pallas_call(
        functools.partial(actor_kernel, count, unroll),
        out_shape=jax.ShapeDtypeStruct((games, 400), jnp.float32),
        in_specs=[vmem] * 4,
        out_specs=vmem,
        scratch_shapes=[
            pltpu.VMEM((2, 1536, 256), jnp.bfloat16),
            pltpu.VMEM((12, 6, 2, games, 128), jnp.bfloat16),
            pltpu.VMEM((10, 5, 2, games, 128), jnp.bfloat16),
        ],
        compiler_params=pltpu.CompilerParams(vmem_limit_bytes=32 * 1024 * 1024),
        cost_estimate=pl.CostEstimate(
            flops=8 * 10**9, bytes_accessed=4 * 10**6, transcendentals=30000
        ),
        name="act",
    )(mine, other, boards, heads)


def column_of(row):
    size = row.shape[1]
    across = lax.broadcasted_iota(jnp.int32, (size, size), 1)
    down = lax.broadcasted_iota(jnp.int32, (size, size), 0)
    spread = jnp.broadcast_to(row, (size, size))
    return jnp.sum(jnp.where(across == down, spread, jnp.zeros_like(spread)), axis=1, keepdims=True)


def later(x, reach):
    return jnp.concatenate([x[reach:], jnp.zeros((reach, x.shape[1]), x.dtype)], axis=0)


def learner_kernel(
    count, length_in, boards_in, actions_in, behaviour_in, regular_in, rewards_in, weights_in,
    policy_in, value_in, own, next1, next2, next3,
    grad, length, boards, weights, actions, behaviour, regular, rewards, policy_t, value_t, pairs, back_pairs,
    middle, last, masks, slope, turned, done,
):
    slots = boards.shape[3]
    role = lax.axis_index("role")
    y = lax.axis_index("dp") // (LINE * LINE)
    moves = [
        (weights_in.at[0:ROWS], weights.at[0:ROWS]),
        (boards_in, inner_cells(boards)),
        (weights_in.at[ROWS : 2 * ROWS], weights.at[ROWS : 2 * ROWS]),
        (actions_in, actions),
        (behaviour_in, behaviour),
        (regular_in, regular),
        (rewards_in, rewards),
        (policy_in, policy_t),
        (value_in, value_t),
        (length_in, length),
    ]
    copies = [pltpu.make_async_copy(a, b, done.at[k]) for k, (a, b) in enumerate(moves)]
    for copy in copies:
        copy.start()
    clear_border(boards)

    def make_pairs(layer):
        def kernel_of(p, q):
            at = layer * ROWS + (3 * p + q) * 128
            return weights[at : at + 128, :].astype(jnp.bfloat16)

        def store(block, value):
            pairs[layer, block * 128 : (block + 1) * 128, :] = value

        pair_kernels(kernel_of, store)

    clear_border(middle)
    clear_border(slope)
    copies[0].wait()
    make_pairs(0)
    copies[1].wait()

    def run_layer(layer, source, emit):
        for first in range(0, 10, count):
            pre = conv_pairs(source, pairs[layer], first, count)
            for parity in range(2):
                part = pre[:, parity * 128 : (parity + 1) * 128].reshape(count, 5, slots, 128)
                before = residual(source, first, count, parity).astype(jnp.float32)
                emit(first, parity, (before + jnp.maximum(part, 0.0)).astype(jnp.bfloat16))
                masks[layer, first : first + count, :, parity] = (part > 0).astype(jnp.bfloat16)

    run_layer(0, boards, lambda first, parity, value: put_cells(middle, first, count, parity, value))

    copies[2].wait()
    make_pairs(1)

    def to_last(first, parity, value):
        last[pl.ds(first, count), :, parity] = value

    run_layer(1, middle, to_last)

    for copy in copies[3:]:
        copy.wait()

    eight = jnp.concatenate(
        [
            policy_t[...].astype(jnp.float32),
            value_t[...].astype(jnp.float32),
            jnp.zeros((3, 128), jnp.float32),
        ],
        axis=0,
    )
    heads_t = jnp.concatenate(
        [eight, eight, eight, jnp.zeros((104, 128), jnp.float32)], axis=0
    ).astype(jnp.bfloat16)

    scores = lax.dot_general(
        last[...].reshape(-1, 128), heads_t, (((1,), (1,)), ((), ())),
        preferred_element_type=jnp.float32,
    ).reshape(100, slots, 128)
    lane = lax.broadcasted_iota(jnp.int32, (slots, 128), 1)
    weights_sum = jnp.sum(jnp.where(lane < 4, jnp.exp(scores), 0.0), axis=0)
    log_total = jnp.log(jnp.sum(weights_sum, axis=1, keepdims=True))
    action = column_of(actions[...])
    direction = action // 100
    cell = action - 100 * direction
    cells = lax.broadcasted_iota(jnp.int32, (100, slots, 128), 0)
    taken = (cells == cell[None]) & (lane % 8 == direction)[None]
    picked = jnp.sum(
        jnp.sum(jnp.where(taken & (lane < 4)[None], scores, 0.0), axis=0), axis=1, keepdims=True
    )
    value_sum = jnp.sum(scores, axis=0)
    value = jnp.tanh(
        jnp.sum(jnp.where(lane == 4, value_sum, 0.0), axis=1, keepdims=True) / 100.0
    )
    log_policy = picked - log_total

    positions = lax.broadcasted_iota(jnp.int32, (slots, 1), 0)
    live = (positions < length[0]).astype(jnp.float32)
    next_live = (positions + 1 < length[0]).astype(jnp.float32)
    ratio = jnp.minimum(1.0, jnp.exp(log_policy - column_of(behaviour[...])))
    shaped = column_of(rewards[...]) - ETA * (log_policy - column_of(regular[...]))
    next_values = later(value, 1) * next_live
    correction = live * ratio * (shaped + next_values - value)
    decay = live * ratio
    reach = 1
    while reach < slots:
        correction = correction + decay * later(correction, reach)
        decay = decay * later(decay, reach)
        reach *= 2
    targets = value + correction
    next_targets = later(targets, 1) * next_live
    policy_grad = -live * ratio * (shaped + next_targets - value)
    value_grad = -live * (targets - value)

    value_cell = value_grad * (1.0 - value * value) / 100.0
    by_policy = policy_grad[None] * (taken.astype(jnp.float32) - jnp.exp(scores - log_total[None]))
    by_score = jnp.where((lane % 8 == 4)[None], value_cell[None], by_policy)
    high = by_score.astype(jnp.bfloat16)
    rest = by_score - high.astype(jnp.float32)
    mid = rest.astype(jnp.bfloat16)
    low = rest - mid.astype(jnp.float32)
    parts = jnp.where(
        (lane < 8)[None],
        high.astype(jnp.float32),
        jnp.where((lane < 16)[None], mid.astype(jnp.float32), low),
    ).astype(jnp.bfloat16)
    out_grad = jnp.dot(
        parts.reshape(-1, 128), heads_t, preferred_element_type=jnp.float32
    )
    act_grad = (out_grad * masks[1].reshape(-1, 128).astype(jnp.float32)).astype(jnp.bfloat16)

    def kernel_of(p, q):
        at = ROWS + (8 - (3 * p + q)) * 128
        return weights[at : at + 128, :].T.astype(jnp.bfloat16)

    def store(block, value):
        back_pairs[block * 128 : (block + 1) * 128, :] = value

    pair_kernels(kernel_of, store)
    act_cells = act_grad.reshape(10, 5, 2, slots, 128)
    put_cells(slope, 0, 10, 0, act_cells[:, :, 0])
    put_cells(slope, 0, 10, 1, act_cells[:, :, 1])
    out_cells = out_grad.reshape(10, 5, 2, slots, 128)
    for first in range(0, 10, count):
        back = conv_pairs(slope, back_pairs[...], first, count)
        for parity in range(2):
            part = back[:, parity * 128 : (parity + 1) * 128].reshape(count, 5, slots, 128)
            total = out_cells[first : first + count, :, parity] + part
            gate = masks[0, first : first + count, :, parity].astype(jnp.float32)
            last[pl.ds(first, count), :, parity] = (total * gate).astype(jnp.bfloat16)
    turned[1] = act_grad.T
    turned[0] = last[...].reshape(-1, 128).T

    def layer_gradient(layer, source, core):
        kept = []
        for offset in range(9):
            parts = [x for x in segment_parts(layer, offset) if x[0] % 2 == core]
            if parts:
                kept.append((offset, parts))
        windows = []
        for offset, _ in kept:
            p, q = offset // 3, offset % 3
            cols = [source[p : p + 10, (j + q) // 2, (j + q) % 2] for j in range(10)]
            windows.append(jnp.stack(cols, axis=1).reshape(-1, 128))
        for pair in range(0, len(kept), 2):
            blocks = jnp.dot(
                turned[layer],
                jnp.concatenate(windows[pair : pair + 2], axis=1),
                preferred_element_type=jnp.float32,
            )
            for k in range(2):
                block = blocks[:, 128 * k : 128 * k + 128].T
                for segment, first, end, at in kept[pair + k][1]:
                    grad[segment // 2, first:end] = block[at : at + end - first]

    chunks = (own, next1, next2, next3)
    for layer, source in ((1, middle), (0, boards)):
        for core in range(2):
            pl.when(role == core)(functools.partial(layer_gradient, layer, source, core))
        for to_y in (2 * layer, 2 * layer + 1):
            for k, out in enumerate(chunks):

                @pl.when(lax.rem(y + k, LINE) == to_y)
                def _(to_y=to_y, k=k, out=out):
                    pltpu.make_async_copy(grad.at[to_y], out, done.at[k]).start()

    for k, out in enumerate(chunks):
        pltpu.make_async_copy(grad.at[0], out, done.at[k]).wait()


def learn(
    length, boards, actions, behaviour, regular, rewards, weights, policy_t, value_t, count=5
):
    slots = boards.shape[2]
    anywhere = pl.BlockSpec(memory_space=pltpu.HBM)
    cells = (10, 5, 2, slots, 128)
    around = (12, 6, 2, slots, 128)
    return pl.pallas_call(
        functools.partial(learner_kernel, count),
        out_shape=[jax.ShapeDtypeStruct((SEGMENT, 128), jnp.float32)] * LINE,
        in_specs=[anywhere] * 9,
        out_specs=[anywhere] * LINE,
        scratch_shapes=[
            pltpu.VMEM((LINE, SEGMENT, 128), jnp.float32),
            pltpu.SMEM((1,), jnp.int32),
            pltpu.VMEM(around, jnp.bfloat16),
            pltpu.VMEM((2 * ROWS, 128), jnp.float32),
            pltpu.VMEM((1, slots), jnp.int32),
            pltpu.VMEM((1, slots), jnp.float32),
            pltpu.VMEM((1, slots), jnp.float32),
            pltpu.VMEM((1, slots), jnp.float32),
            pltpu.VMEM(policy_t.shape, policy_t.dtype),
            pltpu.VMEM(value_t.shape, value_t.dtype),
            pltpu.VMEM((2, 1536, 256), jnp.bfloat16),
            pltpu.VMEM((1536, 256), jnp.bfloat16),
            pltpu.VMEM(around, jnp.bfloat16),
            pltpu.VMEM(cells, jnp.bfloat16),
            pltpu.VMEM((2,) + cells, jnp.bfloat16),
            pltpu.VMEM(around, jnp.bfloat16),
            pltpu.VMEM((2, 128, 100 * slots), jnp.bfloat16),
            pltpu.SemaphoreType.DMA((10,)),
        ],
        compiler_params=pltpu.CompilerParams(vmem_limit_bytes=60 * 1024 * 1024),
        cost_estimate=pl.CostEstimate(
            flops=4 * 10**9, bytes_accessed=3 * 10**6, transcendentals=10000
        ),
        name="learn",
    )(length, boards, actions, behaviour, regular, rewards, weights, policy_t, value_t)


def pull_kernel(own_in, first_in, second_in, own, both, first, second, done):
    moves = [(own_in, own), (first_in, first), (second_in, second)]
    copies = [pltpu.make_async_copy(a, b, done.at[k]) for k, (a, b) in enumerate(moves)]
    for copy in copies:
        copy.start()
    for copy in copies:
        copy.wait()
    both[0:PIECE] = first[...]
    both[PIECE : 2 * PIECE] = second[...]


def pull(own, first, second):
    vmem = pl.BlockSpec(memory_space=pltpu.VMEM)
    rows = pltpu.VMEM((PIECE, 128), jnp.float32)
    return pl.pallas_call(
        pull_kernel,
        out_shape=[
            jax.ShapeDtypeStruct((SEGMENT, 128), jnp.float32),
            jax.ShapeDtypeStruct((2 * PIECE, 128), jnp.float32),
        ],
        in_specs=[pl.BlockSpec(memory_space=pltpu.HBM)] * 3,
        out_specs=[vmem, vmem],
        scratch_shapes=[rows, rows, pltpu.SemaphoreType.DMA((3,))],
        compiler_params=pltpu.CompilerParams(vmem_limit_bytes=16 * 1024 * 1024),
        name="pull",
    )(own, first, second)


def arrange_kernel(moments, first, second):
    for x in range(2):
        for z in range(LINE):
            rows = slice((LINE * x + z) * PIECE, (LINE * x + z + 1) * PIECE)
            first[rows] = BETA_ONE * moments[z, x, 0:PIECE]
            second[rows] = BETA_TWO * moments[z, x, PIECE : 2 * PIECE]


def arrange(moments):
    vmem = pl.BlockSpec(memory_space=pltpu.VMEM)
    return pl.pallas_call(
        arrange_kernel,
        out_shape=[jax.ShapeDtypeStruct((SEGMENT, 128), jnp.float32)] * 2,
        in_specs=[vmem],
        out_specs=[vmem, vmem],
        compiler_params=pltpu.CompilerParams(vmem_limit_bytes=16 * 1024 * 1024),
        cost_estimate=pl.CostEstimate(
            flops=4 * 10**9, bytes_accessed=10**6, transcendentals=0
        ),
        name="arrange",
    )(moments)


def update_kernel(summed, squares, first, second, torso_in, fresh, old, done):
    y = lax.axis_index("dp") // (LINE * LINE)
    start = pl.multiple_of((2 * y + lax.axis_index("role")) * SEGMENT, SEGMENT)
    fetch = pltpu.make_async_copy(torso_in.at[pl.ds(start, SEGMENT)], old, done)
    fetch.start()
    square_sum = jnp.sum(squares[...], axis=1, keepdims=True)
    factor = jnp.minimum(1.0, jnp.sqrt(256.0 * ROWS) / jnp.sqrt(square_sum + NORM_EPS))
    clipped = summed[...] * factor
    moment_one = first[...] + (1.0 - BETA_ONE) * clipped
    moment_two = second[...] + (1.0 - BETA_TWO) * clipped * clipped
    step = LEARN_RATE * moment_one / (jnp.sqrt(moment_two) + ADAM_EPS)
    fetch.wait()
    fresh[...] = old[...] - step


def update(summed, squares, first, second, torso):
    vmem = pl.BlockSpec(memory_space=pltpu.VMEM)
    return pl.pallas_call(
        update_kernel,
        out_shape=jax.ShapeDtypeStruct((SEGMENT, 128), jnp.float32),
        in_specs=[vmem] * 4 + [pl.BlockSpec(memory_space=pltpu.HBM)],
        out_specs=vmem,
        scratch_shapes=[pltpu.VMEM((SEGMENT, 128), jnp.float32), pltpu.SemaphoreType.DMA],
        compiler_params=pltpu.CompilerParams(vmem_limit_bytes=16 * 1024 * 1024),
        name="update",
    )(summed, squares, first, second, torso)


def shifted(x, axis, step):
    stride = {"y": LINE * LINE, "x": LINE, "z": 1}[axis]
    pairs = []
    for d in range(LINE**3):
        at = d // stride % LINE
        pairs.append((d, d + ((at + step) % LINE - at) * stride))
    return lax.ppermute(x, "dp", pairs)


def line_total(x, axis):
    return (x + shifted(x, axis, 2)) + (shifted(x, axis, 1) + shifted(x, axis, 3))


def line_place(pieces, at):
    whole = jnp.zeros((LINE,) + pieces[0].shape, pieces[0].dtype)
    for step, piece in enumerate(pieces):
        whole = lax.dynamic_update_index_in_dim(whole, piece, (at - step) % LINE, 0)
    return whole


def line_gather(x, axis, at):
    return line_place([x] + [shifted(x, axis, step) for step in range(1, LINE)], at)


def moments_along_x(own, role, x):
    def device(role, x, rest):
        return role * LINE**3 + rest // LINE * LINE * LINE + x * LINE + rest % LINE

    same, next_to = [], []
    for rest in range(LINE * LINE):
        for to_role in range(2):
            for to_x in range(LINE):
                to = device(to_role, to_x, rest)
                if to_x // 2 != to_role:
                    same.append((device(to_role, to_x ^ 2, rest), to))
                next_to.append((device(to_x // 2, 2 * to_role + 1 - to_x % 2, rest), to))
    same = jnp.where(x // 2 == role, own, lax.ppermute(own, ("role", "dp"), same))
    next_to = lax.ppermute(own, ("role", "dp"), next_to)
    even = x % 2 == 0
    return jnp.concatenate([jnp.where(even, same, next_to), jnp.where(even, next_to, same)])


def swapped_z(x, bit):
    return lax.ppermute(x, "dp", [(d, d ^ bit) for d in range(LINE**3)])


def moments_along_z(x, z):
    far = swapped_z(x, 2)
    pair = jnp.where(z < 2, jnp.stack([x, far]), jnp.stack([far, x]))
    near = swapped_z(pair, 1)
    even = z % 2 == 0
    return jnp.stack([jnp.where(even, pair, near), jnp.where(even, near, pair)], axis=1)


def pair_total_y(x):
    for partner in ((1, 0, 3, 2), (3, 2, 1, 0)):
        plane = LINE * LINE
        pairs = [(d, partner[d // plane] * plane + d % plane) for d in range(LINE**3)]
        x = x + lax.ppermute(x, "dp", pairs)
    return x


def role_swap(x):
    return lax.ppermute(x, "role", [(0, 1), (1, 0)])


def body(
    board_now,
    traj_boards,
    actions,
    lengths,
    behaviour,
    regular,
    rewards,
    torso,
    policy_head,
    value_head,
    first_moment,
    second_moment,
):
    role = lax.axis_index("role")
    dp = lax.axis_index("dp")
    y, x, z = dp // (LINE * LINE), dp // LINE % LINE, dp % LINE
    own, next1, next2, next3 = learn(
        lengths,
        by_cell(traj_boards[0]),
        actions,
        behaviour,
        regular,
        rewards,
        torso,
        policy_head.T,
        value_head[None],
    )
    own, moments = pull(own, first_moment, second_moment)
    next2 = shifted(next2, "y", 2)
    moments = moments_along_x(moments, role, x)
    first, second = arrange(moments_along_z(moments, z).reshape(LINE, 2, 2 * PIECE, 128))
    summed = (own + next2) + (shifted(next1, "y", 1) + shifted(next3, "y", 3))
    summed = line_total(line_total(summed, "x"), "z")
    squares = jnp.sum(summed * summed, axis=0, keepdims=True)
    squares = pair_total_y(squares + role_swap(squares))
    fresh = update(summed, squares, first, second, torso)
    mine = line_gather(fresh, "y", y)
    other = role_swap(mine)
    boards, heads = stage(mine, by_cell(board_now), policy_head.T.astype(jnp.float32))
    here = act(mine, other, boards, heads)
    there = role_swap(here)
    at = (LINE * x + z) % (2 * LINE) * PIECE
    new_share = jnp.where(
        role == x // 2,
        lax.dynamic_slice(mine, (y, at, 0), (1, PIECE, 128))[0],
        lax.dynamic_slice(other, (y, at, 0), (1, PIECE, 128))[0],
    )
    move_logp = jnp.concatenate([jnp.where(role == 0, here, there), jnp.where(role == 0, there, here)])
    return (new_share, move_logp)


def solution(mesh):
    return jax.shard_map(
        body,
        mesh=mesh,
        in_specs=(
            P("dp", None, None, None),
            P("dp", None, None, None, None),
            P("dp", None),
            P("dp"),
            P("dp", None),
            P("dp", None),
            P("dp", None),
            P(),
            P(),
            P(),
            P("dp", None),
            P("dp", None),
        ),
        out_specs=(P("dp", None), P("dp", None)),
        check_vma=False,
    )
```

```python
import functools

import jax
import jax.numpy as jnp
from jax import lax
from jax.experimental import pallas as pl
from jax.experimental.pallas import tpu as pltpu
from jax.sharding import PartitionSpec as P

ETA = 0.2
LEARN_RATE = 0.03
BETA_ONE = 0.9
BETA_TWO = 0.999
ADAM_EPS = 1e-08
NORM_EPS = 1e-12
ROWS = 1152
LINE = 4
SEGMENT = 2 * ROWS // (2 * LINE)
PIECE = SEGMENT // 8


def by_cell(boards):
    return jnp.transpose(boards, (1, 2, 0, 3))


def inner_cells(ref):
    return ref.reshape((12, 12) + ref.shape[3:]).at[1:11, 1:11]


def segment_parts(layer, offset):
    start = layer * ROWS + offset * 128
    at, parts = start, []
    while at < start + 128:
        segment = at // SEGMENT
        end = min(start + 128, (segment + 1) * SEGMENT)
        parts.append((segment, at - segment * SEGMENT, end - segment * SEGMENT, at - start))
        at = end
    return parts


def clear_border(ref):
    zero_row = jnp.zeros(ref.shape[1:], ref.dtype)
    ref[0] = zero_row
    ref[11] = zero_row
    zero_col = jnp.zeros((12,) + ref.shape[3:], ref.dtype)
    ref[:, 0, 0] = zero_col
    ref[:, 5, 1] = zero_col


def pair_kernels(kernel_of, store):
    nothing = jnp.zeros((128, 128), jnp.bfloat16)
    for p in range(3):
        row = [kernel_of(p, q) for q in range(3)]
        for q in range(4):
            left = row[q] if q < 3 else nothing
            right = row[q - 1] if q > 0 else nothing
            store(4 * p + q, jnp.concatenate([left, right], axis=1))


def conv_pairs(source, pair_weights, first, count):
    windows = []
    for p in range(3):
        for q in range(4):
            window = source[pl.ds(first + p, count), q // 2 : q // 2 + 5, q % 2]
            windows.append(window.reshape(-1, 128))
    return jnp.dot(
        jnp.concatenate(windows, axis=1), pair_weights, preferred_element_type=jnp.float32
    )


def residual(source, first, count, parity):
    if parity == 0:
        window = source[pl.ds(first + 1, count), 0:5, 1]
    else:
        window = source[pl.ds(first + 1, count), 1:6, 0]
    return window


def put_cells(target, first, count, parity, value):
    if parity == 0:
        target[pl.ds(first + 1, count), 0:5, 1] = value
    else:
        target[pl.ds(first + 1, count), 1:6, 0] = value


def stage_kernel(mine, boards_in, policy_t, boards, heads, done):
    games = boards.shape[3]
    half = pl.ds(pl.multiple_of(lax.axis_index("role") * games, games), games)
    fetch = pltpu.make_async_copy(boards_in.at[:, :, half], inner_cells(boards), done)
    fetch.start()
    clear_border(boards)
    spread = lax.broadcasted_iota(jnp.int32, (4, 1280), 1)
    row = lax.broadcasted_iota(jnp.int32, (4, 1280), 0)
    spread = (spread % 128 == 10 * row + spread // 128).astype(jnp.float32)
    by_column = lax.dot_general(
        policy_t[...], spread, (((0,), (0,)), ((), ())), preferred_element_type=jnp.float32
    )
    for j in range(10):
        heads[128 * j : 128 * j + 128, :] = by_column[:, 128 * j : 128 * j + 128].astype(jnp.bfloat16)
    fetch.wait()


def stage(mine, boards, policy_t):
    games = boards.shape[2] // 2
    vmem = pl.BlockSpec(memory_space=pltpu.VMEM)
    anywhere = pl.BlockSpec(memory_space=pltpu.HBM)
    return pl.pallas_call(
        stage_kernel,
        out_shape=[
            jax.ShapeDtypeStruct((12, 6, 2, games, 128), jnp.bfloat16),
            jax.ShapeDtypeStruct((1280, 128), jnp.bfloat16),
        ],
        in_specs=[anywhere, anywhere, vmem],
        out_specs=[vmem, vmem],
        scratch_shapes=[pltpu.SemaphoreType.DMA],
        compiler_params=pltpu.CompilerParams(vmem_limit_bytes=16 * 1024 * 1024),
        cost_estimate=pl.CostEstimate(
            flops=10**9, bytes_accessed=4 * 10**6, transcendentals=0
        ),
        name="stage",
    )(mine, boards, policy_t)


def actor_kernel(count, unroll, mine, other, boards, heads, out, pairs, middle, last):
    games = boards.shape[3]
    role = lax.axis_index("role")
    for layer in range(2):
        def kernel_of(p, q, layer=layer):
            parts = []
            for segment, first, last_row, _ in segment_parts(layer, 3 * p + q):
                y, owner = segment // 2, segment % 2
                rows = slice(first, last_row)
                parts.append(jnp.where(role == owner, mine[y, rows], other[y, rows]))
            return jnp.concatenate(parts, axis=0).astype(jnp.bfloat16)

        def store(block, value, layer=layer):
            pairs[layer, block * 128 : (block + 1) * 128, :] = value

        pair_kernels(kernel_of, store)
    clear_border(middle)

    def run_layer(layer, source, emit):
        def step(at, carry):
            first = at * count
            pre = conv_pairs(source, pairs[layer], first, count)
            for parity in range(2):
                part = pre[:, parity * 128 : (parity + 1) * 128].reshape(count, 5, games, 128)
                before = residual(source, first, count, parity).astype(jnp.float32)
                emit(first, parity, (before + jnp.maximum(part, 0.0)).astype(jnp.bfloat16))
            return carry

        lax.fori_loop(0, 10 // count, step, 0, unroll=unroll)

    run_layer(0, boards, lambda first, parity, value: put_cells(middle, first, count, parity, value))

    def to_last(first, parity, value):
        last[pl.ds(first, count), :, parity] = value

    run_layer(1, middle, to_last)
    cells = [last[:, j // 2, j % 2].reshape(-1, 128) for j in range(10)]
    logits = jnp.dot(jnp.concatenate(cells, axis=1), heads[...], preferred_element_type=jnp.float32)
    logits = logits.reshape(10, games, 128)
    lanes = lax.broadcasted_iota(jnp.int32, (games, 128), 1)
    moves = []
    total = jnp.zeros((games, 1), jnp.float32)
    for d in range(4):
        gathered = jnp.zeros((games, 128), jnp.float32)
        for i in range(10):
            turned = pltpu.roll(logits[i], (10 * i - 10 * d) % 128, 1)
            gathered = jnp.where((lanes >= 10 * i) & (lanes < 10 * i + 10), turned, gathered)
        moves.append(gathered)
        total = total + jnp.sum(
            jnp.where(lanes < 100, jnp.exp(gathered), 0.0), axis=1, keepdims=True
        )
    log_total = jnp.log(total)
    for d in range(4):
        out[:, 100 * d : 100 * d + 100] = (moves[d] - log_total)[:, :100]


def act(mine, other, boards, heads, count=1, unroll=10):
    games = boards.shape[3]
    vmem = pl.BlockSpec(memory_space=pltpu.VMEM)
    return pl.pallas_call(
        functools.partial(actor_kernel, count, unroll),
        out_shape=jax.ShapeDtypeStruct((games, 400), jnp.float32),
        in_specs=[vmem] * 4,
        out_specs=vmem,
        scratch_shapes=[
            pltpu.VMEM((2, 1536, 256), jnp.bfloat16),
            pltpu.VMEM((12, 6, 2, games, 128), jnp.bfloat16),
            pltpu.VMEM((10, 5, 2, games, 128), jnp.bfloat16),
        ],
        compiler_params=pltpu.CompilerParams(vmem_limit_bytes=32 * 1024 * 1024),
        cost_estimate=pl.CostEstimate(
            flops=8 * 10**9, bytes_accessed=4 * 10**6, transcendentals=30000
        ),
        name="act",
    )(mine, other, boards, heads)


def column_of(row):
    size = row.shape[1]
    across = lax.broadcasted_iota(jnp.int32, (size, size), 1)
    down = lax.broadcasted_iota(jnp.int32, (size, size), 0)
    spread = jnp.broadcast_to(row, (size, size))
    return jnp.sum(jnp.where(across == down, spread, jnp.zeros_like(spread)), axis=1, keepdims=True)


def later(x, reach):
    return jnp.concatenate([x[reach:], jnp.zeros((reach, x.shape[1]), x.dtype)], axis=0)


def learner_kernel(
    count, length_in, boards_in, actions_in, behaviour_in, regular_in, rewards_in, weights_in,
    policy_in, value_in, own, next1, next2, next3,
    grad, length, boards, weights, actions, behaviour, regular, rewards, policy_t, value_t, pairs, back_pairs,
    middle, last, masks, slope, turned, done,
):
    slots = boards.shape[3]
    role = lax.axis_index("role")
    y = lax.axis_index("dp") // (LINE * LINE)
    moves = [
        (weights_in.at[0:ROWS], weights.at[0:ROWS]),
        (boards_in, inner_cells(boards)),
        (weights_in.at[ROWS : 2 * ROWS], weights.at[ROWS : 2 * ROWS]),
        (actions_in, actions),
        (behaviour_in, behaviour),
        (regular_in, regular),
        (rewards_in, rewards),
        (policy_in, policy_t),
        (value_in, value_t),
        (length_in, length),
    ]
    copies = [pltpu.make_async_copy(a, b, done.at[k]) for k, (a, b) in enumerate(moves)]
    for copy in copies:
        copy.start()
    clear_border(boards)

    def make_pairs(layer):
        def kernel_of(p, q):
            at = layer * ROWS + (3 * p + q) * 128
            return weights[at : at + 128, :].astype(jnp.bfloat16)

        def store(block, value):
            pairs[layer, block * 128 : (block + 1) * 128, :] = value

        pair_kernels(kernel_of, store)

    clear_border(middle)
    clear_border(slope)
    copies[0].wait()
    make_pairs(0)
    copies[1].wait()

    def run_layer(layer, source, emit):
        for first in range(0, 10, count):
            pre = conv_pairs(source, pairs[layer], first, count)
            for parity in range(2):
                part = pre[:, parity * 128 : (parity + 1) * 128].reshape(count, 5, slots, 128)
                before = residual(source, first, count, parity).astype(jnp.float32)
                emit(first, parity, (before + jnp.maximum(part, 0.0)).astype(jnp.bfloat16))
                masks[layer, first : first + count, :, parity] = (part > 0).astype(jnp.bfloat16)

    run_layer(0, boards, lambda first, parity, value: put_cells(middle, first, count, parity, value))

    copies[2].wait()
    make_pairs(1)

    def to_last(first, parity, value):
        last[pl.ds(first, count), :, parity] = value

    run_layer(1, middle, to_last)

    for copy in copies[3:]:
        copy.wait()

    eight = jnp.concatenate(
        [
            policy_t[...].astype(jnp.float32),
            value_t[...].astype(jnp.float32),
            jnp.zeros((3, 128), jnp.float32),
        ],
        axis=0,
    )
    heads_t = jnp.concatenate(
        [eight, eight, eight, jnp.zeros((104, 128), jnp.float32)], axis=0
    ).astype(jnp.bfloat16)

    scores = lax.dot_general(
        last[...].reshape(-1, 128), heads_t, (((1,), (1,)), ((), ())),
        preferred_element_type=jnp.float32,
    ).reshape(100, slots, 128)
    lane = lax.broadcasted_iota(jnp.int32, (slots, 128), 1)
    weights_sum = jnp.sum(jnp.where(lane < 4, jnp.exp(scores), 0.0), axis=0)
    log_total = jnp.log(jnp.sum(weights_sum, axis=1, keepdims=True))
    action = column_of(actions[...])
    direction = action // 100
    cell = action - 100 * direction
    cells = lax.broadcasted_iota(jnp.int32, (100, slots, 128), 0)
    taken = (cells == cell[None]) & (lane % 8 == direction)[None]
    picked = jnp.sum(
        jnp.sum(jnp.where(taken & (lane < 4)[None], scores, 0.0), axis=0), axis=1, keepdims=True
    )
    value_sum = jnp.sum(scores, axis=0)
    value = jnp.tanh(
        jnp.sum(jnp.where(lane == 4, value_sum, 0.0), axis=1, keepdims=True) / 100.0
    )
    log_policy = picked - log_total

    positions = lax.broadcasted_iota(jnp.int32, (slots, 1), 0)
    live = (positions < length[0]).astype(jnp.float32)
    next_live = (positions + 1 < length[0]).astype(jnp.float32)
    ratio = jnp.minimum(1.0, jnp.exp(log_policy - column_of(behaviour[...])))
    shaped = column_of(rewards[...]) - ETA * (log_policy - column_of(regular[...]))
    next_values = later(value, 1) * next_live
    correction = live * ratio * (shaped + next_values - value)
    decay = live * ratio
    reach = 1
    while reach < slots:
        correction = correction + decay * later(correction, reach)
        decay = decay * later(decay, reach)
        reach *= 2
    targets = value + correction
    next_targets = later(targets, 1) * next_live
    policy_grad = -live * ratio * (shaped + next_targets - value)
    value_grad = -live * (targets - value)

    value_cell = value_grad * (1.0 - value * value) / 100.0
    by_policy = policy_grad[None] * (taken.astype(jnp.float32) - jnp.exp(scores - log_total[None]))
    by_score = jnp.where((lane % 8 == 4)[None], value_cell[None], by_policy)
    high = by_score.astype(jnp.bfloat16)
    rest = by_score - high.astype(jnp.float32)
    mid = rest.astype(jnp.bfloat16)
    low = rest - mid.astype(jnp.float32)
    parts = jnp.where(
        (lane < 8)[None],
        high.astype(jnp.float32),
        jnp.where((lane < 16)[None], mid.astype(jnp.float32), low),
    ).astype(jnp.bfloat16)
    out_grad = jnp.dot(
        parts.reshape(-1, 128), heads_t, preferred_element_type=jnp.float32
    )
    act_grad = (out_grad * masks[1].reshape(-1, 128).astype(jnp.float32)).astype(jnp.bfloat16)

    def kernel_of(p, q):
        at = ROWS + (8 - (3 * p + q)) * 128
        return weights[at : at + 128, :].T.astype(jnp.bfloat16)

    def store(block, value):
        back_pairs[block * 128 : (block + 1) * 128, :] = value

    pair_kernels(kernel_of, store)
    act_cells = act_grad.reshape(10, 5, 2, slots, 128)
    put_cells(slope, 0, 10, 0, act_cells[:, :, 0])
    put_cells(slope, 0, 10, 1, act_cells[:, :, 1])
    out_cells = out_grad.reshape(10, 5, 2, slots, 128)
    for first in range(0, 10, count):
        back = conv_pairs(slope, back_pairs[...], first, count)
        for parity in range(2):
            part = back[:, parity * 128 : (parity + 1) * 128].reshape(count, 5, slots, 128)
            total = out_cells[first : first + count, :, parity] + part
            gate = masks[0, first : first + count, :, parity].astype(jnp.float32)
            last[pl.ds(first, count), :, parity] = (total * gate).astype(jnp.bfloat16)
    turned[1] = act_grad.T
    turned[0] = last[...].reshape(-1, 128).T

    def layer_gradient(layer, source, core):
        kept = []
        for offset in range(9):
            parts = [x for x in segment_parts(layer, offset) if x[0] % 2 == core]
            if parts:
                kept.append((offset, parts))
        windows = []
        for offset, _ in kept:
            p, q = offset // 3, offset % 3
            cols = [source[p : p + 10, (j + q) // 2, (j + q) % 2] for j in range(10)]
            windows.append(jnp.stack(cols, axis=1).reshape(-1, 128))
        for pair in range(0, len(kept), 2):
            blocks = jnp.dot(
                turned[layer],
                jnp.concatenate(windows[pair : pair + 2], axis=1),
                preferred_element_type=jnp.float32,
            )
            for k in range(2):
                block = blocks[:, 128 * k : 128 * k + 128].T
                for segment, first, end, at in kept[pair + k][1]:
                    grad[segment // 2, first:end] = block[at : at + end - first]

    chunks = (own, next1, next2, next3)
    for layer, source in ((1, middle), (0, boards)):
        for core in range(2):
            pl.when(role == core)(functools.partial(layer_gradient, layer, source, core))
        for to_y in (2 * layer, 2 * layer + 1):
            for k, out in enumerate(chunks):

                @pl.when(lax.rem(y + k, LINE) == to_y)
                def _(to_y=to_y, k=k, out=out):
                    pltpu.make_async_copy(grad.at[to_y], out, done.at[k]).start()

    for k, out in enumerate(chunks):
        pltpu.make_async_copy(grad.at[0], out, done.at[k]).wait()


def learn(
    length, boards, actions, behaviour, regular, rewards, weights, policy_t, value_t, count=5
):
    slots = boards.shape[2]
    anywhere = pl.BlockSpec(memory_space=pltpu.HBM)
    cells = (10, 5, 2, slots, 128)
    around = (12, 6, 2, slots, 128)
    return pl.pallas_call(
        functools.partial(learner_kernel, count),
        out_shape=[jax.ShapeDtypeStruct((SEGMENT, 128), jnp.float32)] * LINE,
        in_specs=[anywhere] * 9,
        out_specs=[anywhere] * LINE,
        scratch_shapes=[
            pltpu.VMEM((LINE, SEGMENT, 128), jnp.float32),
            pltpu.SMEM((1,), jnp.int32),
            pltpu.VMEM(around, jnp.bfloat16),
            pltpu.VMEM((2 * ROWS, 128), jnp.float32),
            pltpu.VMEM((1, slots), jnp.int32),
            pltpu.VMEM((1, slots), jnp.float32),
            pltpu.VMEM((1, slots), jnp.float32),
            pltpu.VMEM((1, slots), jnp.float32),
            pltpu.VMEM(policy_t.shape, policy_t.dtype),
            pltpu.VMEM(value_t.shape, value_t.dtype),
            pltpu.VMEM((2, 1536, 256), jnp.bfloat16),
            pltpu.VMEM((1536, 256), jnp.bfloat16),
            pltpu.VMEM(around, jnp.bfloat16),
            pltpu.VMEM(cells, jnp.bfloat16),
            pltpu.VMEM((2,) + cells, jnp.bfloat16),
            pltpu.VMEM(around, jnp.bfloat16),
            pltpu.VMEM((2, 128, 100 * slots), jnp.bfloat16),
            pltpu.SemaphoreType.DMA((10,)),
        ],
        compiler_params=pltpu.CompilerParams(vmem_limit_bytes=60 * 1024 * 1024),
        cost_estimate=pl.CostEstimate(
            flops=4 * 10**9, bytes_accessed=3 * 10**6, transcendentals=10000
        ),
        name="learn",
    )(length, boards, actions, behaviour, regular, rewards, weights, policy_t, value_t)


def pull_kernel(own_in, first_in, second_in, own, both, first, second, done):
    moves = [(own_in, own), (first_in, first), (second_in, second)]
    copies = [pltpu.make_async_copy(a, b, done.at[k]) for k, (a, b) in enumerate(moves)]
    for copy in copies:
        copy.start()
    for copy in copies:
        copy.wait()
    both[0:PIECE] = first[...]
    both[PIECE : 2 * PIECE] = second[...]


def pull(own, first, second):
    vmem = pl.BlockSpec(memory_space=pltpu.VMEM)
    rows = pltpu.VMEM((PIECE, 128), jnp.float32)
    return pl.pallas_call(
        pull_kernel,
        out_shape=[
            jax.ShapeDtypeStruct((SEGMENT, 128), jnp.float32),
            jax.ShapeDtypeStruct((2 * PIECE, 128), jnp.float32),
        ],
        in_specs=[pl.BlockSpec(memory_space=pltpu.HBM)] * 3,
        out_specs=[vmem, vmem],
        scratch_shapes=[rows, rows, pltpu.SemaphoreType.DMA((3,))],
        compiler_params=pltpu.CompilerParams(vmem_limit_bytes=16 * 1024 * 1024),
        name="pull",
    )(own, first, second)


def arrange_kernel(moments, first, second):
    for x in range(2):
        for z in range(LINE):
            rows = slice((LINE * x + z) * PIECE, (LINE * x + z + 1) * PIECE)
            first[rows] = BETA_ONE * moments[z, x, 0:PIECE]
            second[rows] = BETA_TWO * moments[z, x, PIECE : 2 * PIECE]


def arrange(moments):
    vmem = pl.BlockSpec(memory_space=pltpu.VMEM)
    return pl.pallas_call(
        arrange_kernel,
        out_shape=[jax.ShapeDtypeStruct((SEGMENT, 128), jnp.float32)] * 2,
        in_specs=[vmem],
        out_specs=[vmem, vmem],
        compiler_params=pltpu.CompilerParams(vmem_limit_bytes=16 * 1024 * 1024),
        cost_estimate=pl.CostEstimate(
            flops=4 * 10**9, bytes_accessed=10**6, transcendentals=0
        ),
        name="arrange",
    )(moments)


def update_kernel(summed, squares, first, second, torso_in, fresh, old, done):
    y = lax.axis_index("dp") // (LINE * LINE)
    start = pl.multiple_of((2 * y + lax.axis_index("role")) * SEGMENT, SEGMENT)
    fetch = pltpu.make_async_copy(torso_in.at[pl.ds(start, SEGMENT)], old, done)
    fetch.start()
    square_sum = jnp.sum(squares[...], axis=1, keepdims=True)
    factor = jnp.minimum(1.0, jnp.sqrt(256.0 * ROWS) / jnp.sqrt(square_sum + NORM_EPS))
    clipped = summed[...] * factor
    moment_one = first[...] + (1.0 - BETA_ONE) * clipped
    moment_two = second[...] + (1.0 - BETA_TWO) * clipped * clipped
    step = LEARN_RATE * moment_one / (jnp.sqrt(moment_two) + ADAM_EPS)
    fetch.wait()
    fresh[...] = old[...] - step


def update(summed, squares, first, second, torso):
    vmem = pl.BlockSpec(memory_space=pltpu.VMEM)
    return pl.pallas_call(
        update_kernel,
        out_shape=jax.ShapeDtypeStruct((SEGMENT, 128), jnp.float32),
        in_specs=[vmem] * 4 + [pl.BlockSpec(memory_space=pltpu.HBM)],
        out_specs=vmem,
        scratch_shapes=[pltpu.VMEM((SEGMENT, 128), jnp.float32), pltpu.SemaphoreType.DMA],
        compiler_params=pltpu.CompilerParams(vmem_limit_bytes=16 * 1024 * 1024),
        name="update",
    )(summed, squares, first, second, torso)


def shifted(x, axis, step):
    stride = {"y": LINE * LINE, "x": LINE, "z": 1}[axis]
    pairs = []
    for d in range(LINE**3):
        at = d // stride % LINE
        pairs.append((d, d + ((at + step) % LINE - at) * stride))
    return lax.ppermute(x, "dp", pairs)


def line_total(x, axis):
    return (x + shifted(x, axis, 2)) + (shifted(x, axis, 1) + shifted(x, axis, 3))


def line_gather(x, axis, at):
    whole = jnp.zeros((LINE,) + x.shape, x.dtype)
    for step in (0, 2, 1, 3):
        piece = shifted(x, axis, step) if step else x
        whole = lax.dynamic_update_index_in_dim(whole, piece, (at - step) % LINE, 0)
    return whole


def moments_along_x(own, role, x):
    def device(role, x, rest):
        return role * LINE**3 + rest // LINE * LINE * LINE + x * LINE + rest % LINE

    same, next_to = [], []
    for rest in range(LINE * LINE):
        for to_role in range(2):
            for to_x in range(LINE):
                to = device(to_role, to_x, rest)
                if to_x // 2 != to_role:
                    same.append((device(to_role, to_x ^ 2, rest), to))
                next_to.append((device(to_x // 2, 2 * to_role + 1 - to_x % 2, rest), to))
    same = jnp.where(x // 2 == role, own, lax.ppermute(own, ("role", "dp"), same))
    next_to = lax.ppermute(own, ("role", "dp"), next_to)
    even = x % 2 == 0
    return jnp.concatenate([jnp.where(even, same, next_to), jnp.where(even, next_to, same)])


def swapped_z(x, bit):
    return lax.ppermute(x, "dp", [(d, d ^ bit) for d in range(LINE**3)])


def moments_along_z(x, z):
    far = swapped_z(x, 2)
    pair = jnp.where(z < 2, jnp.stack([x, far]), jnp.stack([far, x]))
    near = swapped_z(pair, 1)
    even = z % 2 == 0
    return jnp.stack([jnp.where(even, pair, near), jnp.where(even, near, pair)], axis=1)


def pair_total_y(x):
    for partner in ((1, 0, 3, 2), (3, 2, 1, 0)):
        plane = LINE * LINE
        pairs = [(d, partner[d // plane] * plane + d % plane) for d in range(LINE**3)]
        x = x + lax.ppermute(x, "dp", pairs)
    return x


def role_swap(x):
    return lax.ppermute(x, "role", [(0, 1), (1, 0)])


def body(
    board_now,
    traj_boards,
    actions,
    lengths,
    behaviour,
    regular,
    rewards,
    torso,
    policy_head,
    value_head,
    first_moment,
    second_moment,
):
    role = lax.axis_index("role")
    dp = lax.axis_index("dp")
    y, x, z = dp // (LINE * LINE), dp // LINE % LINE, dp % LINE
    own, next1, next2, next3 = learn(
        lengths,
        by_cell(traj_boards[0]),
        actions,
        behaviour,
        regular,
        rewards,
        torso,
        policy_head.T,
        value_head[None],
    )
    own, moments = pull(own, first_moment, second_moment)
    next2 = shifted(next2, "y", 2)
    moments = moments_along_x(moments, role, x)
    first, second = arrange(moments_along_z(moments, z).reshape(LINE, 2, 2 * PIECE, 128))
    summed = (own + next2) + (shifted(next1, "y", 1) + shifted(next3, "y", 3))
    summed = line_total(line_total(summed, "x"), "z")
    squares = jnp.sum(summed * summed, axis=0, keepdims=True)
    squares = pair_total_y(squares + role_swap(squares))
    fresh = update(summed, squares, first, second, torso)
    mine = line_gather(fresh, "y", y)
    other = role_swap(mine)
    boards, heads = stage(mine, by_cell(board_now), policy_head.T.astype(jnp.float32))
    here = act(mine, other, boards, heads)
    there = role_swap(here)
    at = (LINE * x + z) % (2 * LINE) * PIECE
    new_share = jnp.where(
        role == x // 2,
        lax.dynamic_slice(mine, (y, at, 0), (1, PIECE, 128))[0],
        lax.dynamic_slice(other, (y, at, 0), (1, PIECE, 128))[0],
    )
    move_logp = jnp.concatenate([jnp.where(role == 0, here, there), jnp.where(role == 0, there, here)])
    return (new_share, move_logp)


def solution(mesh):
    return jax.shard_map(
        body,
        mesh=mesh,
        in_specs=(
            P("dp", None, None, None),
            P("dp", None, None, None, None),
            P("dp", None),
            P("dp"),
            P("dp", None),
            P("dp", None),
            P("dp", None),
            P(),
            P(),
            P(),
            P("dp", None),
            P("dp", None),
        ),
        out_specs=(P("dp", None), P("dp", None)),
        check_vma=False,
    )
```

```python
import functools

import jax
import jax.numpy as jnp
from jax import lax
from jax.experimental import pallas as pl
from jax.experimental.pallas import tpu as pltpu
from jax.sharding import PartitionSpec as P

ETA = 0.2
LEARN_RATE = 0.03
BETA_ONE = 0.9
BETA_TWO = 0.999
ADAM_EPS = 1e-08
NORM_EPS = 1e-12
ROWS = 1152
LINE = 4
SEGMENT = 2 * ROWS // (2 * LINE)
PIECE = SEGMENT // 8


def by_cell(boards):
    return jnp.transpose(boards, (1, 2, 0, 3))


def inner_cells(ref):
    return ref.reshape((12, 12) + ref.shape[3:]).at[1:11, 1:11]


def segment_parts(layer, offset):
    start = layer * ROWS + offset * 128
    at, parts = start, []
    while at < start + 128:
        segment = at // SEGMENT
        end = min(start + 128, (segment + 1) * SEGMENT)
        parts.append((segment, at - segment * SEGMENT, end - segment * SEGMENT, at - start))
        at = end
    return parts


def clear_border(ref):
    zero_row = jnp.zeros(ref.shape[1:], ref.dtype)
    ref[0] = zero_row
    ref[11] = zero_row
    zero_col = jnp.zeros((12,) + ref.shape[3:], ref.dtype)
    ref[:, 0, 0] = zero_col
    ref[:, 5, 1] = zero_col


def pair_kernels(kernel_of, store):
    nothing = jnp.zeros((128, 128), jnp.bfloat16)
    for p in range(3):
        row = [kernel_of(p, q) for q in range(3)]
        for q in range(4):
            left = row[q] if q < 3 else nothing
            right = row[q - 1] if q > 0 else nothing
            store(4 * p + q, jnp.concatenate([left, right], axis=1))


def conv_pairs(source, pair_weights, first, count):
    windows = []
    for p in range(3):
        for q in range(4):
            window = source[pl.ds(first + p, count), q // 2 : q // 2 + 5, q % 2]
            windows.append(window.reshape(-1, 128))
    return jnp.dot(
        jnp.concatenate(windows, axis=1), pair_weights, preferred_element_type=jnp.float32
    )


def residual(source, first, count, parity):
    if parity == 0:
        window = source[pl.ds(first + 1, count), 0:5, 1]
    else:
        window = source[pl.ds(first + 1, count), 1:6, 0]
    return window


def put_cells(target, first, count, parity, value):
    if parity == 0:
        target[pl.ds(first + 1, count), 0:5, 1] = value
    else:
        target[pl.ds(first + 1, count), 1:6, 0] = value


def stage_kernel(mine, boards_in, policy_t, boards, heads, done):
    games = boards.shape[3]
    half = pl.ds(pl.multiple_of(lax.axis_index("role") * games, games), games)
    fetch = pltpu.make_async_copy(boards_in.at[:, :, half], inner_cells(boards), done)
    fetch.start()
    clear_border(boards)
    spread = lax.broadcasted_iota(jnp.int32, (4, 1280), 1)
    row = lax.broadcasted_iota(jnp.int32, (4, 1280), 0)
    spread = (spread % 128 == 10 * row + spread // 128).astype(jnp.float32)
    by_column = lax.dot_general(
        policy_t[...], spread, (((0,), (0,)), ((), ())), preferred_element_type=jnp.float32
    )
    for j in range(10):
        heads[128 * j : 128 * j + 128, :] = by_column[:, 128 * j : 128 * j + 128].astype(jnp.bfloat16)
    fetch.wait()


def stage(mine, boards, policy_t):
    games = boards.shape[2] // 2
    vmem = pl.BlockSpec(memory_space=pltpu.VMEM)
    anywhere = pl.BlockSpec(memory_space=pltpu.HBM)
    return pl.pallas_call(
        stage_kernel,
        out_shape=[
            jax.ShapeDtypeStruct((12, 6, 2, games, 128), jnp.bfloat16),
            jax.ShapeDtypeStruct((1280, 128), jnp.bfloat16),
        ],
        in_specs=[anywhere, anywhere, vmem],
        out_specs=[vmem, vmem],
        scratch_shapes=[pltpu.SemaphoreType.DMA],
        compiler_params=pltpu.CompilerParams(vmem_limit_bytes=16 * 1024 * 1024),
        cost_estimate=pl.CostEstimate(
            flops=10**9, bytes_accessed=4 * 10**6, transcendentals=0
        ),
        name="stage",
    )(mine, boards, policy_t)


def actor_kernel(count, unroll, mine, other, boards, heads, out, pairs, middle, last):
    games = boards.shape[3]
    role = lax.axis_index("role")
    for layer in range(2):
        def kernel_of(p, q, layer=layer):
            parts = []
            for segment, first, last_row, _ in segment_parts(layer, 3 * p + q):
                y, owner = segment // 2, segment % 2
                rows = slice(first, last_row)
                parts.append(jnp.where(role == owner, mine[y, rows], other[y, rows]))
            return jnp.concatenate(parts, axis=0).astype(jnp.bfloat16)

        def store(block, value, layer=layer):
            pairs[layer, block * 128 : (block + 1) * 128, :] = value

        pair_kernels(kernel_of, store)
    clear_border(middle)

    def run_layer(layer, source, emit):
        def step(at, carry):
            first = at * count
            pre = conv_pairs(source, pairs[layer], first, count)
            for parity in range(2):
                part = pre[:, parity * 128 : (parity + 1) * 128].reshape(count, 5, games, 128)
                before = residual(source, first, count, parity).astype(jnp.float32)
                emit(first, parity, (before + jnp.maximum(part, 0.0)).astype(jnp.bfloat16))
            return carry

        lax.fori_loop(0, 10 // count, step, 0, unroll=unroll)

    run_layer(0, boards, lambda first, parity, value: put_cells(middle, first, count, parity, value))

    def to_last(first, parity, value):
        last[pl.ds(first, count), :, parity] = value

    run_layer(1, middle, to_last)
    cells = [last[:, j // 2, j % 2].reshape(-1, 128) for j in range(10)]
    logits = jnp.dot(jnp.concatenate(cells, axis=1), heads[...], preferred_element_type=jnp.float32)
    logits = logits.reshape(10, games, 128)
    lanes = lax.broadcasted_iota(jnp.int32, (games, 128), 1)
    moves = []
    total = jnp.zeros((games, 1), jnp.float32)
    for d in range(4):
        gathered = jnp.zeros((games, 128), jnp.float32)
        for i in range(10):
            turned = pltpu.roll(logits[i], (10 * i - 10 * d) % 128, 1)
            gathered = jnp.where((lanes >= 10 * i) & (lanes < 10 * i + 10), turned, gathered)
        moves.append(gathered)
        total = total + jnp.sum(
            jnp.where(lanes < 100, jnp.exp(gathered), 0.0), axis=1, keepdims=True
        )
    log_total = jnp.log(total)
    for d in range(4):
        out[:, 100 * d : 100 * d + 100] = (moves[d] - log_total)[:, :100]


def act(mine, other, boards, heads, count=1, unroll=10):
    games = boards.shape[3]
    vmem = pl.BlockSpec(memory_space=pltpu.VMEM)
    return pl.pallas_call(
        functools.partial(actor_kernel, count, unroll),
        out_shape=jax.ShapeDtypeStruct((games, 400), jnp.float32),
        in_specs=[vmem] * 4,
        out_specs=vmem,
        scratch_shapes=[
            pltpu.VMEM((2, 1536, 256), jnp.bfloat16),
            pltpu.VMEM((12, 6, 2, games, 128), jnp.bfloat16),
            pltpu.VMEM((10, 5, 2, games, 128), jnp.bfloat16),
        ],
        compiler_params=pltpu.CompilerParams(vmem_limit_bytes=32 * 1024 * 1024),
        cost_estimate=pl.CostEstimate(
            flops=8 * 10**9, bytes_accessed=4 * 10**6, transcendentals=30000
        ),
        name="act",
    )(mine, other, boards, heads)


def column_of(row):
    size = row.shape[1]
    across = lax.broadcasted_iota(jnp.int32, (size, size), 1)
    down = lax.broadcasted_iota(jnp.int32, (size, size), 0)
    spread = jnp.broadcast_to(row, (size, size))
    return jnp.sum(jnp.where(across == down, spread, jnp.zeros_like(spread)), axis=1, keepdims=True)


def later(x, reach):
    return jnp.concatenate([x[reach:], jnp.zeros((reach, x.shape[1]), x.dtype)], axis=0)


def learner_kernel(
    count, length_in, boards_in, actions_in, behaviour_in, regular_in, rewards_in, weights_in,
    policy_in, value_in, own, next1, next2, next3,
    grad, length, boards, weights, actions, behaviour, regular, rewards, policy_t, value_t, pairs, back_pairs,
    middle, last, masks, slope, turned, done,
):
    slots = boards.shape[3]
    role = lax.axis_index("role")
    y = lax.axis_index("dp") // (LINE * LINE)
    moves = [
        (weights_in.at[0:ROWS], weights.at[0:ROWS]),
        (boards_in, inner_cells(boards)),
        (weights_in.at[ROWS : 2 * ROWS], weights.at[ROWS : 2 * ROWS]),
        (actions_in, actions),
        (behaviour_in, behaviour),
        (regular_in, regular),
        (rewards_in, rewards),
        (policy_in, policy_t),
        (value_in, value_t),
        (length_in, length),
    ]
    copies = [pltpu.make_async_copy(a, b, done.at[k]) for k, (a, b) in enumerate(moves)]
    for copy in copies:
        copy.start()
    clear_border(boards)

    def make_pairs(layer):
        def kernel_of(p, q):
            at = layer * ROWS + (3 * p + q) * 128
            return weights[at : at + 128, :].astype(jnp.bfloat16)

        def store(block, value):
            pairs[layer, block * 128 : (block + 1) * 128, :] = value

        pair_kernels(kernel_of, store)

    clear_border(middle)
    clear_border(slope)
    copies[0].wait()
    make_pairs(0)
    copies[1].wait()

    def run_layer(layer, source, emit):
        for first in range(0, 10, count):
            pre = conv_pairs(source, pairs[layer], first, count)
            for parity in range(2):
                part = pre[:, parity * 128 : (parity + 1) * 128].reshape(count, 5, slots, 128)
                before = residual(source, first, count, parity).astype(jnp.float32)
                emit(first, parity, (before + jnp.maximum(part, 0.0)).astype(jnp.bfloat16))
                masks[layer, first : first + count, :, parity] = (part > 0).astype(jnp.bfloat16)

    run_layer(0, boards, lambda first, parity, value: put_cells(middle, first, count, parity, value))

    copies[2].wait()
    make_pairs(1)

    def to_last(first, parity, value):
        last[pl.ds(first, count), :, parity] = value

    run_layer(1, middle, to_last)

    for copy in copies[3:]:
        copy.wait()

    eight = jnp.concatenate(
        [
            policy_t[...].astype(jnp.float32),
            value_t[...].astype(jnp.float32),
            jnp.zeros((3, 128), jnp.float32),
        ],
        axis=0,
    )
    heads_t = jnp.concatenate(
        [eight, eight, eight, jnp.zeros((104, 128), jnp.float32)], axis=0
    ).astype(jnp.bfloat16)

    scores = lax.dot_general(
        last[...].reshape(-1, 128), heads_t, (((1,), (1,)), ((), ())),
        preferred_element_type=jnp.float32,
    ).reshape(100, slots, 128)
    lane = lax.broadcasted_iota(jnp.int32, (slots, 128), 1)
    weights_sum = jnp.sum(jnp.where(lane < 4, jnp.exp(scores), 0.0), axis=0)
    log_total = jnp.log(jnp.sum(weights_sum, axis=1, keepdims=True))
    action = column_of(actions[...])
    direction = action // 100
    cell = action - 100 * direction
    cells = lax.broadcasted_iota(jnp.int32, (100, slots, 128), 0)
    taken = (cells == cell[None]) & (lane % 8 == direction)[None]
    picked = jnp.sum(
        jnp.sum(jnp.where(taken & (lane < 4)[None], scores, 0.0), axis=0), axis=1, keepdims=True
    )
    value_sum = jnp.sum(scores, axis=0)
    value = jnp.tanh(
        jnp.sum(jnp.where(lane == 4, value_sum, 0.0), axis=1, keepdims=True) / 100.0
    )
    log_policy = picked - log_total

    positions = lax.broadcasted_iota(jnp.int32, (slots, 1), 0)
    live = (positions < length[0]).astype(jnp.float32)
    next_live = (positions + 1 < length[0]).astype(jnp.float32)
    ratio = jnp.minimum(1.0, jnp.exp(log_policy - column_of(behaviour[...])))
    shaped = column_of(rewards[...]) - ETA * (log_policy - column_of(regular[...]))
    next_values = later(value, 1) * next_live
    correction = live * ratio * (shaped + next_values - value)
    decay = live * ratio
    reach = 1
    while reach < slots:
        correction = correction + decay * later(correction, reach)
        decay = decay * later(decay, reach)
        reach *= 2
    targets = value + correction
    next_targets = later(targets, 1) * next_live
    policy_grad = -live * ratio * (shaped + next_targets - value)
    value_grad = -live * (targets - value)

    value_cell = value_grad * (1.0 - value * value) / 100.0
    by_policy = policy_grad[None] * (taken.astype(jnp.float32) - jnp.exp(scores - log_total[None]))
    by_score = jnp.where((lane % 8 == 4)[None], value_cell[None], by_policy)
    high = by_score.astype(jnp.bfloat16)
    rest = by_score - high.astype(jnp.float32)
    mid = rest.astype(jnp.bfloat16)
    low = rest - mid.astype(jnp.float32)
    parts = jnp.where(
        (lane < 8)[None],
        high.astype(jnp.float32),
        jnp.where((lane < 16)[None], mid.astype(jnp.float32), low),
    ).astype(jnp.bfloat16)
    out_grad = jnp.dot(
        parts.reshape(-1, 128), heads_t, preferred_element_type=jnp.float32
    )
    act_grad = (out_grad * masks[1].reshape(-1, 128).astype(jnp.float32)).astype(jnp.bfloat16)

    def kernel_of(p, q):
        at = ROWS + (8 - (3 * p + q)) * 128
        return weights[at : at + 128, :].T.astype(jnp.bfloat16)

    def store(block, value):
        back_pairs[block * 128 : (block + 1) * 128, :] = value

    pair_kernels(kernel_of, store)
    act_cells = act_grad.reshape(10, 5, 2, slots, 128)
    put_cells(slope, 0, 10, 0, act_cells[:, :, 0])
    put_cells(slope, 0, 10, 1, act_cells[:, :, 1])
    out_cells = out_grad.reshape(10, 5, 2, slots, 128)
    for first in range(0, 10, count):
        back = conv_pairs(slope, back_pairs[...], first, count)
        for parity in range(2):
            part = back[:, parity * 128 : (parity + 1) * 128].reshape(count, 5, slots, 128)
            total = out_cells[first : first + count, :, parity] + part
            gate = masks[0, first : first + count, :, parity].astype(jnp.float32)
            last[pl.ds(first, count), :, parity] = (total * gate).astype(jnp.bfloat16)
    turned[1] = act_grad.T
    turned[0] = last[...].reshape(-1, 128).T

    def layer_gradient(layer, source, core):
        kept = []
        for offset in range(9):
            parts = [x for x in segment_parts(layer, offset) if x[0] % 2 == core]
            if parts:
                kept.append((offset, parts))
        windows = []
        for offset, _ in kept:
            p, q = offset // 3, offset % 3
            cols = [source[p : p + 10, (j + q) // 2, (j + q) % 2] for j in range(10)]
            windows.append(jnp.stack(cols, axis=1).reshape(-1, 128))
        for pair in range(0, len(kept), 2):
            blocks = jnp.dot(
                turned[layer],
                jnp.concatenate(windows[pair : pair + 2], axis=1),
                preferred_element_type=jnp.float32,
            )
            for k in range(2):
                block = blocks[:, 128 * k : 128 * k + 128].T
                for segment, first, end, at in kept[pair + k][1]:
                    grad[segment // 2, first:end] = block[at : at + end - first]

    chunks = (own, next1, next2, next3)
    for layer, source in ((1, middle), (0, boards)):
        for core in range(2):
            pl.when(role == core)(functools.partial(layer_gradient, layer, source, core))
        for to_y in (2 * layer, 2 * layer + 1):
            for k, out in enumerate(chunks):

                @pl.when(lax.rem(y + k, LINE) == to_y)
                def _(to_y=to_y, k=k, out=out):
                    pltpu.make_async_copy(grad.at[to_y], out, done.at[k]).start()

    for k, out in enumerate(chunks):
        pltpu.make_async_copy(grad.at[0], out, done.at[k]).wait()


def learn(
    length, boards, actions, behaviour, regular, rewards, weights, policy_t, value_t, count=5
):
    slots = boards.shape[2]
    anywhere = pl.BlockSpec(memory_space=pltpu.HBM)
    cells = (10, 5, 2, slots, 128)
    around = (12, 6, 2, slots, 128)
    return pl.pallas_call(
        functools.partial(learner_kernel, count),
        out_shape=[jax.ShapeDtypeStruct((SEGMENT, 128), jnp.float32)] * LINE,
        in_specs=[anywhere] * 9,
        out_specs=[anywhere] * LINE,
        scratch_shapes=[
            pltpu.VMEM((LINE, SEGMENT, 128), jnp.float32),
            pltpu.SMEM((1,), jnp.int32),
            pltpu.VMEM(around, jnp.bfloat16),
            pltpu.VMEM((2 * ROWS, 128), jnp.float32),
            pltpu.VMEM((1, slots), jnp.int32),
            pltpu.VMEM((1, slots), jnp.float32),
            pltpu.VMEM((1, slots), jnp.float32),
            pltpu.VMEM((1, slots), jnp.float32),
            pltpu.VMEM(policy_t.shape, policy_t.dtype),
            pltpu.VMEM(value_t.shape, value_t.dtype),
            pltpu.VMEM((2, 1536, 256), jnp.bfloat16),
            pltpu.VMEM((1536, 256), jnp.bfloat16),
            pltpu.VMEM(around, jnp.bfloat16),
            pltpu.VMEM(cells, jnp.bfloat16),
            pltpu.VMEM((2,) + cells, jnp.bfloat16),
            pltpu.VMEM(around, jnp.bfloat16),
            pltpu.VMEM((2, 128, 100 * slots), jnp.bfloat16),
            pltpu.SemaphoreType.DMA((10,)),
        ],
        compiler_params=pltpu.CompilerParams(vmem_limit_bytes=60 * 1024 * 1024),
        cost_estimate=pl.CostEstimate(
            flops=4 * 10**9, bytes_accessed=3 * 10**6, transcendentals=10000
        ),
        name="learn",
    )(length, boards, actions, behaviour, regular, rewards, weights, policy_t, value_t)


def pull_kernel(own_in, first_in, second_in, own, both, first, second, done):
    moves = [(own_in, own), (first_in, first), (second_in, second)]
    copies = [pltpu.make_async_copy(a, b, done.at[k]) for k, (a, b) in enumerate(moves)]
    for copy in copies:
        copy.start()
    for copy in copies:
        copy.wait()
    both[0:PIECE] = first[...]
    both[PIECE : 2 * PIECE] = second[...]


def pull(own, first, second):
    vmem = pl.BlockSpec(memory_space=pltpu.VMEM)
    rows = pltpu.VMEM((PIECE, 128), jnp.float32)
    return pl.pallas_call(
        pull_kernel,
        out_shape=[
            jax.ShapeDtypeStruct((SEGMENT, 128), jnp.float32),
            jax.ShapeDtypeStruct((2 * PIECE, 128), jnp.float32),
        ],
        in_specs=[pl.BlockSpec(memory_space=pltpu.HBM)] * 3,
        out_specs=[vmem, vmem],
        scratch_shapes=[rows, rows, pltpu.SemaphoreType.DMA((3,))],
        compiler_params=pltpu.CompilerParams(vmem_limit_bytes=16 * 1024 * 1024),
        name="pull",
    )(own, first, second)


def arrange_kernel(moments, first, second):
    for x in range(2):
        for z in range(LINE):
            rows = slice((LINE * x + z) * PIECE, (LINE * x + z + 1) * PIECE)
            first[rows] = BETA_ONE * moments[z, x, 0:PIECE]
            second[rows] = BETA_TWO * moments[z, x, PIECE : 2 * PIECE]


def arrange(moments):
    vmem = pl.BlockSpec(memory_space=pltpu.VMEM)
    return pl.pallas_call(
        arrange_kernel,
        out_shape=[jax.ShapeDtypeStruct((SEGMENT, 128), jnp.float32)] * 2,
        in_specs=[vmem],
        out_specs=[vmem, vmem],
        compiler_params=pltpu.CompilerParams(vmem_limit_bytes=16 * 1024 * 1024),
        cost_estimate=pl.CostEstimate(
            flops=4 * 10**9, bytes_accessed=10**6, transcendentals=0
        ),
        name="arrange",
    )(moments)


def update_kernel(summed, squares, first, second, torso_in, fresh, old, done):
    y = lax.axis_index("dp") // (LINE * LINE)
    start = pl.multiple_of((2 * y + lax.axis_index("role")) * SEGMENT, SEGMENT)
    fetch = pltpu.make_async_copy(torso_in.at[pl.ds(start, SEGMENT)], old, done)
    fetch.start()
    square_sum = jnp.sum(squares[...], axis=1, keepdims=True)
    factor = jnp.minimum(1.0, jnp.sqrt(256.0 * ROWS) / jnp.sqrt(square_sum + NORM_EPS))
    clipped = summed[...] * factor
    moment_one = first[...] + (1.0 - BETA_ONE) * clipped
    moment_two = second[...] + (1.0 - BETA_TWO) * clipped * clipped
    step = LEARN_RATE * moment_one / (jnp.sqrt(moment_two) + ADAM_EPS)
    fetch.wait()
    fresh[...] = old[...] - step


def update(summed, squares, first, second, torso):
    vmem = pl.BlockSpec(memory_space=pltpu.VMEM)
    return pl.pallas_call(
        update_kernel,
        out_shape=jax.ShapeDtypeStruct((SEGMENT, 128), jnp.float32),
        in_specs=[vmem] * 4 + [pl.BlockSpec(memory_space=pltpu.HBM)],
        out_specs=vmem,
        scratch_shapes=[pltpu.VMEM((SEGMENT, 128), jnp.float32), pltpu.SemaphoreType.DMA],
        compiler_params=pltpu.CompilerParams(vmem_limit_bytes=16 * 1024 * 1024),
        name="update",
    )(summed, squares, first, second, torso)


def shifted(x, axis, step):
    stride = {"y": LINE * LINE, "x": LINE, "z": 1}[axis]
    pairs = []
    for d in range(LINE**3):
        at = d // stride % LINE
        pairs.append((d, d + ((at + step) % LINE - at) * stride))
    return lax.ppermute(x, "dp", pairs)


def line_total(x, axis):
    return (x + shifted(x, axis, 2)) + (shifted(x, axis, 1) + shifted(x, axis, 3))


def line_gather(x, axis, at):
    mine = jnp.zeros((LINE,) + x.shape, x.dtype)
    other = jnp.zeros((LINE,) + x.shape, x.dtype)
    for step in (0, 2, 1, 3):
        piece = shifted(x, axis, step) if step else x
        place = (at - step) % LINE
        mine = lax.dynamic_update_index_in_dim(mine, piece, place, 0)
        other = lax.dynamic_update_index_in_dim(other, role_swap(piece), place, 0)
    return mine, other


def moments_along_x(own, role, x):
    def device(role, x, rest):
        return role * LINE**3 + rest // LINE * LINE * LINE + x * LINE + rest % LINE

    same, next_to = [], []
    for rest in range(LINE * LINE):
        for to_role in range(2):
            for to_x in range(LINE):
                to = device(to_role, to_x, rest)
                if to_x // 2 != to_role:
                    same.append((device(to_role, to_x ^ 2, rest), to))
                next_to.append((device(to_x // 2, 2 * to_role + 1 - to_x % 2, rest), to))
    same = jnp.where(x // 2 == role, own, lax.ppermute(own, ("role", "dp"), same))
    next_to = lax.ppermute(own, ("role", "dp"), next_to)
    even = x % 2 == 0
    return jnp.concatenate([jnp.where(even, same, next_to), jnp.where(even, next_to, same)])


def swapped_z(x, bit):
    return lax.ppermute(x, "dp", [(d, d ^ bit) for d in range(LINE**3)])


def moments_along_z(x, z):
    far = swapped_z(x, 2)
    pair = jnp.where(z < 2, jnp.stack([x, far]), jnp.stack([far, x]))
    near = swapped_z(pair, 1)
    even = z % 2 == 0
    return jnp.stack([jnp.where(even, pair, near), jnp.where(even, near, pair)], axis=1)


def pair_total_y(x):
    for partner in ((1, 0, 3, 2), (3, 2, 1, 0)):
        plane = LINE * LINE
        pairs = [(d, partner[d // plane] * plane + d % plane) for d in range(LINE**3)]
        x = x + lax.ppermute(x, "dp", pairs)
    return x


def role_swap(x):
    return lax.ppermute(x, "role", [(0, 1), (1, 0)])


def body(
    board_now,
    traj_boards,
    actions,
    lengths,
    behaviour,
    regular,
    rewards,
    torso,
    policy_head,
    value_head,
    first_moment,
    second_moment,
):
    role = lax.axis_index("role")
    dp = lax.axis_index("dp")
    y, x, z = dp // (LINE * LINE), dp // LINE % LINE, dp % LINE
    own, next1, next2, next3 = learn(
        lengths,
        by_cell(traj_boards[0]),
        actions,
        behaviour,
        regular,
        rewards,
        torso,
        policy_head.T,
        value_head[None],
    )
    own, moments = pull(own, first_moment, second_moment)
    next2 = shifted(next2, "y", 2)
    moments = moments_along_x(moments, role, x)
    first, second = arrange(moments_along_z(moments, z).reshape(LINE, 2, 2 * PIECE, 128))
    summed = (own + next2) + (shifted(next1, "y", 1) + shifted(next3, "y", 3))
    summed = line_total(line_total(summed, "x"), "z")
    squares = jnp.sum(summed * summed, axis=0, keepdims=True)
    squares = pair_total_y(squares + role_swap(squares))
    fresh = update(summed, squares, first, second, torso)
    mine, other = line_gather(fresh, "y", y)
    boards, heads = stage(mine, by_cell(board_now), policy_head.T.astype(jnp.float32))
    here = act(mine, other, boards, heads)
    there = role_swap(here)
    at = (LINE * x + z) % (2 * LINE) * PIECE
    new_share = jnp.where(
        role == x // 2,
        lax.dynamic_slice(mine, (y, at, 0), (1, PIECE, 128))[0],
        lax.dynamic_slice(other, (y, at, 0), (1, PIECE, 128))[0],
    )
    move_logp = jnp.concatenate([jnp.where(role == 0, here, there), jnp.where(role == 0, there, here)])
    return (new_share, move_logp)


def solution(mesh):
    return jax.shard_map(
        body,
        mesh=mesh,
        in_specs=(
            P("dp", None, None, None),
            P("dp", None, None, None, None),
            P("dp", None),
            P("dp"),
            P("dp", None),
            P("dp", None),
            P("dp", None),
            P(),
            P(),
            P(),
            P("dp", None),
            P("dp", None),
        ),
        out_specs=(P("dp", None), P("dp", None)),
        check_vma=False,
    )
```
